128 devices in a mesh: lat: 4 (over x_hi, core), lon: 32 (over x_lo, y, z).
Axes of the slice: x: 4 (x_hi: 2, x_lo: 2; x = x_hi * 2 + x_lo), y: 4, z: 4, core: 2. Of those that a mesh axis runs over, the one named last changes fastest.
Arguments:
- grid: bfloat16 [2, 20, 768, 1536], P(None, None, 'lat', 'lon'), may hold values from -6 to 6
- patch_weight: bfloat16 [5120, 768], replicated, may hold values from -0.078125 to 0.078125
- norm_gain_one: float32 [768], replicated, may hold values from 0.1 to 1.9
- spectral_one: float32 [2, 8, 96, 96], replicated, may hold values from -0.4375 to 0.4375
- spectral_bias: float32 [2, 768], replicated, may hold values from -1.5 to 1.5
- spectral_two: float32 [2, 8, 96, 96], replicated, may hold values from -0.4375 to 0.4375
- norm_gain_two: float32 [768], replicated, may hold values from 0.1 to 1.9
- fc_up: bfloat16 [768, 3072], replicated, may hold values from -0.21875 to 0.21875
- fc_down: bfloat16 [3072, 768], replicated, may hold values from -0.109375 to 0.109375
Outputs:
- block_out: bfloat16 [2, 96, 192, 768], P(None, 'lat', 'lon')
The draws below stay inside these ranges and needn't reach their ends.
All inputs are finite; a program needn't handle non-finite values.
Results may differ from the reference program's by a relative error of at most 0.014.
Values may be sent and summed in bfloat16 or wider, within the bound.
A program may use at most 128 MiB of HBM per device.

```python
import jax
import jax.numpy as jnp
from jax import lax

V = 20
C = 768
NB = 8
HID = 3072
PATCH = 8
SAMPLES = 2
BS = 96
PATCH_IN = 5120
H = 96
W = 192
KW = 64


def shard_levels(own_key, extent, split, least, largest):
    loudness, own = 1.0, jax.random.fold_in(own_key, 6)
    for position, shards_of in split:
        draws = jnp.exp(jax.random.uniform(jax.random.fold_in(own, position), (shards_of,), jnp.float32, least / len(split), largest / len(split)))
        loudness = loudness * jnp.repeat(draws, extent[position] // shards_of).reshape([-1 if axis == position else 1 for axis in range(len(extent))])
    return loudness


def noise(rng, dims, scale, reach, cuts=(), dtype=jnp.bfloat16):
    array = jax.random.normal(rng, dims, jnp.float32) * scale
    if len(cuts) > 0:
        array = shard_levels(rng, dims, cuts, -0.22, 0.18) * array
    return jnp.clip(array, min=-reach, max=reach).astype(dtype)


def setup_inputs(seed: int = 0) -> dict:
    seeds = jax.random.split(jax.random.key(seed), 10)
    return {
        "grid": noise(seeds[0], (SAMPLES, V, PATCH * H, PATCH * W), 1.0, 6.0, ((2, 4), (3, 32))),
        "patch_weight": noise(seeds[1], (PATCH_IN, C), PATCH_IN ** -0.5, 0.078125),
        "norm_gain_one": jnp.clip(1.0 + 0.18 * jax.random.normal(seeds[2], (C,), jnp.float32), 0.1, 1.9),
        "spectral_one": noise(seeds[3], (2, NB, BS, BS), (2 * BS) ** -0.5, 0.4375, (), jnp.float32),
        "spectral_bias": noise(seeds[4], (2, C), 0.3, 1.5, (), jnp.float32),
        "spectral_two": noise(seeds[5], (2, NB, BS, BS), (2 * BS) ** -0.5, 0.4375, (), jnp.float32),
        "norm_gain_two": jnp.clip(1.0 + 0.18 * jax.random.normal(seeds[6], (C,), jnp.float32), 0.1, 1.9),
        "fc_up": noise(seeds[7], (C, HID), C ** -0.5, 0.21875),
        "fc_down": noise(seeds[8], (HID, C), HID ** -0.5, 0.109375),
    }


def embed(padded, weight, rows, cols):
    samples, depth, tall, broad = padded.shape
    half = PATCH // 2
    cells = padded.reshape(samples, depth, tall // half, half, broad // half, half)
    cells = cells.transpose(0, 2, 4, 1, 3, 5).reshape(samples, tall // half, broad // half, depth * half * half)
    pieces = [cells[:, row_off:row_off + 2 * rows:2, col_off:col_off + 2 * cols:2, :] for row_off in range(4) for col_off in range(4)]
    patches = jnp.concatenate(pieces, axis=-1)
    flat = patches.reshape(samples * rows * cols, patches.shape[-1])
    result = jnp.dot(flat, weight, preferred_element_type=jnp.float32)
    return result.reshape(samples, rows, cols, weight.shape[1]).astype(jnp.bfloat16)

def layer_norm(values, gain):
    flat = values.astype(jnp.float32)
    centre = lax.optimization_barrier(jnp.mean(flat, axis=-1, keepdims=True))
    spread = lax.optimization_barrier(jnp.mean(jnp.square(flat - centre), axis=-1, keepdims=True))
    return ((flat - centre) * lax.rsqrt(spread + 1e-05) * gain).astype(jnp.bfloat16)

def spectral_mlp(spec, first_w, bias, second_w):
    blocks = first_w.shape[1]
    width = first_w.shape[2]
    real_in = spec[..., 0, :]
    imag_in = spec[..., 1, :]
    lead = real_in.shape[:-1]
    real_in = real_in.reshape(lead + (blocks, width))
    imag_in = imag_in.reshape(lead + (blocks, width))

    def mult(left, right):
        return jnp.einsum('...bi,bio->...bo', left, right, precision=lax.Precision.HIGHEST)
    bias_re = bias[0].reshape(blocks, width)
    bias_im = bias[1].reshape(blocks, width)
    mid_re = jax.nn.relu(mult(real_in, first_w[0]) - mult(imag_in, first_w[1]) + bias_re)
    mid_im = jax.nn.relu(mult(real_in, first_w[1]) + mult(imag_in, first_w[0]) + bias_im)
    out_re = mult(mid_re, second_w[0]) - mult(mid_im, second_w[1])
    out_im = mult(mid_re, second_w[1]) + mult(mid_im, second_w[0])
    out_re = out_re - jnp.clip(out_re, -0.01, 0.01)
    out_im = out_im - jnp.clip(out_im, -0.01, 0.01)
    return jnp.stack([out_re.reshape(lead + (blocks * width,)), out_im.reshape(lead + (blocks * width,))], axis=-2)

def token_mlp(middle, gain, fc_up, fc_down):
    normed = layer_norm(middle, gain)
    shape = normed.shape
    flat = normed.reshape(-1, shape[-1])
    hidden = jax.nn.gelu(jnp.dot(flat, fc_up, preferred_element_type=jnp.float32), approximate=False).astype(jnp.bfloat16)
    update = jnp.dot(hidden, fc_down, preferred_element_type=jnp.float32).reshape(shape)
    return (middle.astype(jnp.float32) + update).astype(jnp.bfloat16)

def one_sample(sample, patch_weight, norm_gain_one, spectral_one, spectral_bias, spectral_two, norm_gain_two, fc_up, fc_down):
    half = PATCH // 2
    padded = jnp.pad(sample, ((0, 0), (half, half), (0, 0)))
    padded = jnp.concatenate([padded[:, :, -half:], padded, padded[:, :, :half]], axis=2)
    tokens = embed(padded[None], patch_weight, H, W)[0]
    normed_one = layer_norm(tokens, norm_gain_one)
    spectrum = jnp.fft.rfft2(normed_one.astype(jnp.float32), axes=(0, 1), norm='ortho')[:, :KW, :]
    stacked = jnp.stack([jnp.real(spectrum), jnp.imag(spectrum)], axis=2).astype(jnp.float32)
    filtered = spectral_mlp(stacked, spectral_one, spectral_bias, spectral_two)
    modes = filtered[:, :, 0, :] + 1j * filtered[:, :, 1, :]
    modes = jnp.pad(modes, ((0, 0), (0, W // 2 + 1 - KW), (0, 0)))
    field = jnp.fft.irfft2(modes, s=(H, W), axes=(0, 1), norm='ortho').astype(jnp.float32)
    middle = (field + normed_one.astype(jnp.float32) + tokens.astype(jnp.float32)).astype(jnp.bfloat16)
    return token_mlp(middle, norm_gain_two, fc_up, fc_down)

def reference(grid, patch_weight, norm_gain_one, spectral_one, spectral_bias, spectral_two, norm_gain_two, fc_up, fc_down):

    def apply(sample):
        return one_sample(sample, patch_weight, norm_gain_one, spectral_one, spectral_bias, spectral_two, norm_gain_two, fc_up, fc_down)
    return lax.map(apply, grid)
```

```python
import math

import jax
import jax.numpy as jnp
import numpy as np
from jax import lax
from jax.experimental import pallas as pl
from jax.experimental.pallas import tpu as pltpu
from jax.sharding import PartitionSpec as P

MESH = pl.DeviceIdType.MESH
F32 = jnp.float32
BF16 = jnp.bfloat16

NLAT, NLON = 4, 32
NV, C, HID, NB, BS = 20, 768, 3072, 8, 96
H, W, KW = 96, 192, 64
ROWS, COLS = 24, 6
ROW12 = 12
MSG = ROW12 * BS


def pick_table():
    sel = np.zeros((64, 48), np.float32)
    for q8 in range(8):
        for jj in range(7):
            lon = 8 * jj + q8 - 4
            if 0 <= lon < 48:
                sel[q8 * 8 + jj, lon] = 1.0
    return sel


def feature_table(shift):
    table = np.zeros((4, 160, 768), np.float32)
    for q in range(4):
        for v in range(NV):
            for r8 in range(8):
                table[q, v * 8 + r8, (r8 // 4) * 384 + shift + v * 16 + (r8 % 4) * 4 + q] = 1.0
    return table


def lon_tables():
    k = np.arange(KW)
    w = np.arange(W)
    angle = 2.0 * math.pi * ((k[:, None] * w[None, :]) % W) / W
    scale = 1.0 / math.sqrt(W)
    both = np.stack([np.cos(angle), -np.sin(angle)]) * scale
    fwd = both.reshape(2, 8, 8, NLON, COLS).transpose(1, 0, 2, 3, 4).reshape(128, NLON, COLS)
    fwd = np.pad(fwd, ((0, 0), (0, 0), (0, 2))).reshape(128, 256)
    weight = np.where(k == 0, 1.0, 2.0)
    back = both * weight[None, :, None]
    back = back.reshape(2, 8, 8, NLON, COLS).transpose(3, 4, 1, 0, 2).reshape(NLON, COLS, 128)
    back = np.pad(back, ((0, 0), (0, 2), (0, 0))).reshape(256, 128)
    return fwd, back


def lat_tables():
    h = np.arange(H)
    angle = 2.0 * math.pi * ((h[:, None] * h[None, :]) % H) / H
    cos, sin = np.cos(angle) / math.sqrt(H), np.sin(angle) / math.sqrt(H)
    fwd = np.block([[cos, sin], [-sin, cos]])
    back = np.block([[cos, -sin], [sin, cos]])
    return fwd, back


def norm(values, gain):
    centre = jnp.mean(values, axis=-1, keepdims=True)
    off = values - centre
    spread = jnp.mean(jnp.square(off), axis=-1, keepdims=True)
    return off * lax.rsqrt(spread + 1e-05) * gain


def dot(left, right):
    return jnp.dot(left, right, preferred_element_type=F32)


def kernel(
    grid_h, pw_h, one_h, two_h, up_h, down_h, elo_h, ehi_h,
    g1_ref, bias_ref, g2_ref, sel_ref, fw_ref, bw_ref, fh_ref, bh_ref,
    out_ref,
    grid_v, pw_v, one_v, two_v, up_v, down_v, elo_v, ehi_v,
    t_v, lo_v, hi_v, s_v, lhs_v, acc_v, tn_v, mid_v, nrm_v,
    ew_s, ew_r, ns_s, ns_r,
    p1_s, p1_r, p2_s, p2_r, p3_s, p3_r, p4_s, p4_r,
    z_v, v_v, w1_v, w2_v,
    lsem, halo_ss, halo_rs, s1, r1, s2, r2, s3, r3, s4, r4,
):
    a = lax.axis_index("lat")
    b = lax.axis_index("lon")
    q = b // 16
    p = b % 16
    n = b % 8
    g = 2 * a + q

    def load(index, src, dst):
        copy = pltpu.make_async_copy(src, dst, lsem.at[index])
        copy.start()
        return copy

    c_grid = load(0, grid_h, grid_v)
    c_elo = load(1, elo_h, elo_v)
    c_ehi = load(2, ehi_h, ehi_v)
    c_pw = load(3, pw_h, pw_v)
    c_one = load(4, one_h.at[:, n], one_v)
    c_two = load(5, two_h.at[:, n], two_v)
    c_up = load(6, up_h, up_v)
    c_down = load(7, down_h, down_v)

    barrier = pltpu.get_barrier_semaphore()

    def greet_lon(d, _):
        pl.semaphore_signal(
            barrier, inc=1, device_id=(a, lax.rem(b + d, NLON)), device_id_type=MESH
        )
        return 0

    lax.fori_loop(1, NLON, greet_lon, 0)

    def greet_lat(d, _):
        mate = lax.rem(a + 1 + d // 2, NLAT)
        pl.semaphore_signal(
            barrier, inc=1, device_id=(mate, (d % 2) * 16 + p), device_id_type=MESH
        )
        return 0

    lax.fori_loop(0, 6, greet_lat, 0)

    c_grid.wait()

    def turn(it, _):
        smp = it // 12
        rp = it % 12
        block = grid_v[smp, :, pl.ds(pl.multiple_of(16 * rp, 16), 16), :]
        block = block.astype(F32).reshape(NV, 2, 8, 48)
        turned = []
        for half in range(2):
            x = block[:, half].reshape(NV * 8, 48).astype(BF16)
            turned.append(
                lax.dot_general(
                    sel_ref[...], x, (((1,), (1,)), ((), ())), preferred_element_type=F32
                )
            )
        for q8 in range(8):
            pair = jnp.concatenate([t[8 * q8 : 8 * q8 + 8] for t in turned], axis=0)
            t_v[q8, pl.ds(pl.multiple_of(16 * it, 16), 16), :] = pair.astype(BF16)
        return 0

    lax.fori_loop(0, 24, turn, 0)

    c_elo.wait()
    c_ehi.wait()
    for part, (table, total) in enumerate(((elo_v, lo_v), (ehi_v, hi_v))):
        value = dot(t_v[4 * part], table[0])
        for i in range(1, 4):
            value = value + dot(t_v[4 * part + i], table[i])
        for tile in range(6):
            total[tile] = value[:, 128 * tile : 128 * tile + 128]

    pl.semaphore_wait(barrier, NLON - 1 + 6)

    def remote(src, dst, ssem, rsem, dev):
        return pltpu.make_async_remote_copy(
            src_ref=src, dst_ref=dst, send_sem=ssem, recv_sem=rsem,
            device_id=dev, device_id_type=MESH,
        )

    for tile in range(6):
        cols = slice(128 * tile, 128 * tile + 128)
        ew_s[0, :, cols] = lo_v[tile, pl.ds(6, 48, stride=8), :].astype(BF16)
        ew_s[1, :, cols] = hi_v[tile, pl.ds(0, 48, stride=8), :].astype(BF16)
    east = remote(ew_s.at[0], ew_r.at[0], halo_ss.at[0], halo_rs.at[0], (a, lax.rem(b + 1, NLON)))
    west = remote(
        ew_s.at[1], ew_r.at[1], halo_ss.at[1], halo_rs.at[1], (a, lax.rem(b + NLON - 1, NLON))
    )
    east.start()
    west.start()
    east.wait_recv()
    west.wait_recv()
    for tile in range(6):
        cols = slice(128 * tile, 128 * tile + 128)
        lo_v[tile, pl.ds(0, 48, stride=8), :] = ew_r[0, :, cols].astype(F32)
        hi_v[tile, pl.ds(6, 48, stride=8), :] = ew_r[1, :, cols].astype(F32)
    for half in range(2):
        lo = [lo_v[3 * half + tile] for tile in range(3)]
        hi = [hi_v[3 * half + tile] for tile in range(3)]
        for tile, value in enumerate((lo[0], lo[1], lo[2] + hi[0], hi[1], hi[2])):
            both = value.reshape(2, ROWS, 8, 128)
            for smp in range(2):
                s_v[half, smp, 1 : 1 + ROWS, :, 128 * tile : 128 * tile + 128] = both[smp]
    ns_s[0] = s_v[1, :, ROWS].astype(BF16)
    ns_s[1] = s_v[0, :, 1].astype(BF16)
    south = remote(ns_s.at[0], ns_r.at[0], halo_ss.at[2], halo_rs.at[2], (lax.rem(a + 1, NLAT), b))
    north = remote(
        ns_s.at[1], ns_r.at[1], halo_ss.at[3], halo_rs.at[3], (lax.rem(a + NLAT - 1, NLAT), b)
    )
    south.start()
    north.start()

    c_pw.wait()
    for count, (off, half, first) in enumerate(((1, 0, 1), (2, 1, 1), (0, 1, 0), (3, 0, 2))):
        if count == 2:
            south.wait_recv()
            north.wait_recv()
            s_v[1, :, 0] = jnp.where(a > 0, ns_r[0].astype(F32), 0.0)
            s_v[0, :, ROWS + 1] = jnp.where(a < NLAT - 1, ns_r[1].astype(F32), 0.0)
        for smp in range(2):
            x = s_v[half, smp, first : first + ROWS]
            rows = slice(192 * smp, 192 * smp + 192)
            lhs_v[rows, :640] = x.reshape(192, 640).astype(BF16)
            shifted = jnp.concatenate([x[:, 1:], x[:, :1]], axis=1)
            lhs_v[rows, 640:] = shifted.reshape(192, 640).astype(BF16)
        for tile in range(3):
            cols = slice(256 * tile, 256 * tile + 256)
            value = dot(lhs_v[...], pw_v[1280 * off : 1280 * off + 1280, cols])
            if count == 0:
                acc_v[:, cols] = value
            else:
                acc_v[:, cols] += value

    def send_tokens(c, _):
        rows = pl.ds(pl.multiple_of(c * 96, 96), 96)
        tok = acc_v[rows, :].astype(BF16).astype(F32)
        normed = norm(tok, g1_ref[...]).astype(BF16).astype(F32)
        tn_v[rows, :] = tok + normed
        planes = normed.reshape(ROW12, 8, C)
        smp = c // 2
        part = c % 2
        for blk in range(NB):
            msg = jnp.concatenate(
                [planes[i][:, BS * blk : BS * blk + BS] for i in range(ROW12)], axis=1
            )
            dest = part * 16 + smp * 8 + blk
            p1_s[dest] = msg.astype(BF16)

            @pl.when(dest != b)
            def _():
                remote(p1_s.at[dest], p1_r.at[b], s1.at[dest], r1.at[b], (a, dest)).start()

            @pl.when(dest == b)
            def _():
                p1_r[b] = msg.astype(BF16)

        return 0

    lax.fori_loop(0, 4, send_tokens, 0)

    c_one.wait()
    c_two.wait()
    for src, dst in ((one_v, w1_v), (two_v, w2_v)):
        dst[...] = jnp.zeros_like(dst)
        dst[0:BS, 0:BS] = src[0].astype(BF16)
        dst[0:BS, 128 : 128 + BS] = src[1].astype(BF16)
        dst[128 : 128 + BS, 0:BS] = -src[1].astype(BF16)
        dst[128 : 128 + BS, 128 : 128 + BS] = src[0].astype(BF16)
    bias = jnp.zeros((1, 256), F32)
    for blk in range(NB):
        parts = []
        for ri in range(2):
            parts.append(bias_ref[ri : ri + 1, BS * blk : BS * blk + BS])
            parts.append(jnp.zeros((1, 32), F32))
        bias = bias + jnp.where(n == blk, jnp.concatenate(parts, axis=1), 0.0)

    def wait1(d, _):
        src = lax.rem(b + d, NLON)
        remote(p1_s.at[src], p1_r.at[src], s1.at[src], r1.at[src], (a, src)).wait_recv()
        return 0

    lax.fori_loop(1, NLON, wait1, 0)

    x = p1_r[...].astype(F32).reshape(256, MSG).astype(BF16)
    y = dot(fw_ref[...], x)
    p2_s[...] = y.reshape(8, 16, MSG).astype(BF16)

    def mate_of(d):
        other = lax.rem(g + d, 8)
        return other, (other // 2, (other % 2) * 16 + p)

    def send2(d, _):
        other, dev = mate_of(d)
        remote(p2_s.at[other], p2_r.at[g], s2.at[other], r2.at[g], dev).start()
        return 0

    lax.fori_loop(1, 8, send2, 0)

    def spread(src, value):
        for i in range(ROW12):
            piece = value[:, BS * i : BS * i + BS]
            piece = jnp.concatenate([piece, jnp.zeros((16, 128 - BS), F32)], axis=1)
            z_v[pl.ds(ROW12 * src + i, 8, stride=192), :] = piece[:8]
            z_v[pl.ds(H + ROW12 * src + i, 8, stride=192), :] = piece[8:]

    spread(g, p2_s[g].astype(F32))

    def take2(d, _):
        other, dev = mate_of(d)
        remote(p2_s.at[other], p2_r.at[other], s2.at[other], r2.at[other], dev).wait_recv()
        spread(other, p2_r[other].astype(F32))
        return 0

    lax.fori_loop(1, 8, take2, 0)

    for pair in range(4):
        k0, k1 = 384 * pair, 384 * pair + 192
        z = jnp.concatenate([z_v[k0 : k0 + 192, :], z_v[k1 : k1 + 192, :]], axis=1).astype(BF16)
        spec = dot(fh_ref[...], z)
        modes = jnp.concatenate(
            [
                jnp.concatenate([spec[:H, :128], spec[H:, :128]], axis=1),
                jnp.concatenate([spec[:H, 128:], spec[H:, 128:]], axis=1),
            ],
            axis=0,
        )
        mid = jnp.maximum(dot(modes.astype(BF16), w1_v[...]) + bias, 0.0)
        res = dot(mid.astype(BF16), w2_v[...])
        res = res - jnp.clip(res, -0.01, 0.01)
        back = jnp.concatenate(
            [
                jnp.concatenate([res[:H, :128], res[H:, :128]], axis=1),
                jnp.concatenate([res[:H, 128:], res[H:, 128:]], axis=1),
            ],
            axis=0,
        )
        rows = dot(bh_ref[...], back.astype(BF16))
        v_v[k0 : k0 + 192, :] = rows[:, :128]
        v_v[k1 : k1 + 192, :] = rows[:, 128:]

    def gather_rows(dest):
        pieces = []
        for i in range(ROW12):
            re = v_v[pl.ds(ROW12 * dest + i, 8, stride=192), :]
            im = v_v[pl.ds(H + ROW12 * dest + i, 8, stride=192), :]
            pieces.append(jnp.concatenate([re, im], axis=0)[:, :BS])
        return jnp.concatenate(pieces, axis=1).astype(BF16)

    def send3(d, _):
        other, dev = mate_of(d)
        p3_s[other] = gather_rows(other)
        remote(p3_s.at[other], p3_r.at[g], s3.at[other], r3.at[g], dev).start()
        return 0

    lax.fori_loop(1, 8, send3, 0)
    p3_r[g] = gather_rows(g)

    def wait3(d, _):
        other, dev = mate_of(d)
        remote(p3_s.at[other], p3_r.at[other], s3.at[other], r3.at[other], dev).wait_recv()
        return 0

    lax.fori_loop(1, 8, wait3, 0)

    field = dot(bw_ref[...], p3_r[...].reshape(128, MSG))
    p4_s[...] = field.reshape(NLON, 8, MSG).astype(BF16)

    def send4(d, _):
        dest = lax.rem(b + d, NLON)
        remote(p4_s.at[dest], p4_r.at[b], s4.at[dest], r4.at[b], (a, dest)).start()
        return 0

    lax.fori_loop(1, NLON, send4, 0)
    p4_r[b] = p4_s[b]

    def wait4(d, _):
        src = lax.rem(b + d, NLON)
        remote(p4_s.at[src], p4_r.at[src], s4.at[src], r4.at[src], (a, src)).wait_recv()
        return 0

    lax.fori_loop(1, NLON, wait4, 0)

    def join(c, _):
        rows = pl.ds(pl.multiple_of(c * 96, 96), 96)
        smp = c // 2
        part = c % 2
        msgs = [p4_r[part * 16 + smp * 8 + blk].astype(F32) for blk in range(NB)]
        planes = [
            jnp.concatenate([m[:, BS * i : BS * i + BS] for m in msgs], axis=1)
            for i in range(ROW12)
        ]
        middle = jnp.concatenate(planes, axis=0) + tn_v[rows, :]
        middle = middle.astype(BF16).astype(F32)
        mid_v[rows, :] = middle
        nrm_v[rows, :] = norm(middle, g2_ref[...]).astype(BF16)
        return 0

    lax.fori_loop(0, 4, join, 0)

    c_up.wait()
    c_down.wait()

    def mlp(step, _):
        cols = pl.ds(pl.multiple_of(step * 256, 256), 256)
        hidden = dot(nrm_v[...], up_v[:, cols])
        hidden = 0.5 * hidden * (1.0 + lax.erf(hidden * (1.0 / math.sqrt(2.0))))
        mid_v[...] += dot(hidden.astype(BF16), down_v[cols, :])
        return 0

    lax.fori_loop(0, HID // 256, mlp, 0)

    for smp in range(2):
        rows = slice(192 * smp, 192 * smp + 192)
        out_ref[smp] = mid_v[rows, :].reshape(ROWS, 8, C)[:, :COLS].astype(BF16)

    for copy in (east, west, south, north):
        copy.wait_send()

    def drain_lon(d, _):
        dest = lax.rem(b + d, NLON)
        remote(p1_s.at[dest], p1_r.at[b], s1.at[dest], r1.at[b], (a, dest)).wait_send()
        remote(p4_s.at[dest], p4_r.at[b], s4.at[dest], r4.at[b], (a, dest)).wait_send()
        return 0

    lax.fori_loop(1, NLON, drain_lon, 0)

    def drain_lat(d, _):
        other, dev = mate_of(d)
        remote(p2_s.at[other], p2_r.at[g], s2.at[other], r2.at[g], dev).wait_send()
        remote(p3_s.at[other], p3_r.at[g], s3.at[other], r3.at[g], dev).wait_send()
        return 0

    lax.fori_loop(1, 8, drain_lat, 0)


def local(
    grid, patch_weight, norm_gain_one, spectral_one, spectral_bias, spectral_two,
    norm_gain_two, fc_up, fc_down,
):
    fw, bw = lon_tables()
    fh, bh = lat_tables()
    const = lambda x: jnp.asarray(x, F32).astype(BF16)
    any_spec = pl.BlockSpec(memory_space=pl.ANY)
    vmem = pl.BlockSpec(memory_space=pltpu.VMEM)
    dma = pltpu.SemaphoreType.DMA
    return pl.pallas_call(
        kernel,
        out_shape=jax.ShapeDtypeStruct((2, ROWS, COLS, C), BF16),
        in_specs=[any_spec] * 8 + [vmem] * 8,
        out_specs=vmem,
        scratch_shapes=[
            pltpu.VMEM((2, NV, 192, 48), BF16),
            pltpu.VMEM((5120, C), BF16),
            pltpu.VMEM((2, BS, BS), F32),
            pltpu.VMEM((2, BS, BS), F32),
            pltpu.VMEM((C, HID), BF16),
            pltpu.VMEM((HID, C), BF16),
            pltpu.VMEM((4, 160, 768), BF16),
            pltpu.VMEM((4, 160, 768), BF16),
            pltpu.VMEM((8, 384, 160), BF16),
            pltpu.VMEM((6, 384, 128), F32),
            pltpu.VMEM((6, 384, 128), F32),
            pltpu.VMEM((2, 2, ROWS + 2, 8, 640), F32),
            pltpu.VMEM((384, 1280), BF16),
            pltpu.VMEM((384, C), F32),
            pltpu.VMEM((384, C), F32),
            pltpu.VMEM((384, C), F32),
            pltpu.VMEM((384, C), BF16),
            pltpu.VMEM((2, 48, 768), BF16),
            pltpu.VMEM((2, 48, 768), BF16),
            pltpu.VMEM((2, 2, 8, 640), BF16),
            pltpu.VMEM((2, 2, 8, 640), BF16),
            pltpu.VMEM((NLON, 8, MSG), BF16),
            pltpu.VMEM((NLON, 8, MSG), BF16),
            pltpu.VMEM((8, 16, MSG), BF16),
            pltpu.VMEM((8, 16, MSG), BF16),
            pltpu.VMEM((8, 16, MSG), BF16),
            pltpu.VMEM((8, 16, MSG), BF16),
            pltpu.VMEM((NLON, 8, MSG), BF16),
            pltpu.VMEM((NLON, 8, MSG), BF16),
            pltpu.VMEM((8 * 192, 128), F32),
            pltpu.VMEM((8 * 192, 128), F32),
            pltpu.VMEM((256, 256), BF16),
            pltpu.VMEM((256, 256), BF16),
            dma((8,)),
            dma((4,)),
            dma((4,)),
            dma((NLON,)),
            dma((NLON,)),
            dma((8,)),
            dma((8,)),
            dma((8,)),
            dma((8,)),
            dma((NLON,)),
            dma((NLON,)),
        ],
        compiler_params=pltpu.CompilerParams(
            collective_id=0, has_side_effects=True, vmem_limit_bytes=56 * 1024 * 1024
        ),
    )(
        grid, patch_weight, spectral_one, spectral_two, fc_up, fc_down,
        const(feature_table(0)), const(feature_table(64)),
        norm_gain_one.reshape(1, C), spectral_bias, norm_gain_two.reshape(1, C),
        const(pick_table()), const(fw), const(bw), const(fh), const(bh),
    )


def solution(mesh):
    in_specs = (P(None, None, "lat", "lon"), P(), P(), P(), P(), P(), P(), P(), P())
    out_specs = P(None, "lat", "lon", None)
    return jax.shard_map(local, mesh=mesh, in_specs=in_specs, out_specs=out_specs, check_vma=False)
```

```python
import math

import jax
import jax.numpy as jnp
import numpy as np
from jax import lax
from jax.experimental import pallas as pl
from jax.experimental.pallas import tpu as pltpu
from jax.sharding import PartitionSpec as P

MESH = pl.DeviceIdType.MESH
F32 = jnp.float32
BF16 = jnp.bfloat16

NLAT, NLON = 4, 32
NV, C, HID, NB, BS = 20, 768, 3072, 8, 96
H, W, KW = 96, 192, 64
ROWS, COLS = 24, 6
ROW12 = 12
MSG = ROW12 * BS


def pick_table():
    sel = np.zeros((192, 192), np.float32)
    for r8 in range(8):
        for row in range(ROWS):
            sel[r8 * ROWS + row, 8 * row + r8] = 1.0
    return sel


def feature_table():
    table = np.zeros((4, 160, 768), np.float32)
    for r in range(4):
        for v in range(NV):
            for c8 in range(8):
                table[r, v * 8 + c8, (64, 384)[c8 // 4] + v * 16 + 4 * r + c8 % 4] = 1.0
    return table


def lon_tables():
    k = np.arange(KW)
    w = np.arange(W)
    angle = 2.0 * math.pi * ((k[:, None] * w[None, :]) % W) / W
    scale = 1.0 / math.sqrt(W)
    both = np.stack([np.cos(angle), -np.sin(angle)]) * scale
    fwd = both.reshape(2, 8, 8, NLON, COLS).transpose(1, 0, 2, 3, 4).reshape(128, NLON, COLS)
    fwd = np.pad(fwd, ((0, 0), (0, 0), (0, 2))).reshape(128, 256)
    weight = np.where(k == 0, 1.0, 2.0)
    back = both * weight[None, :, None]
    back = back.reshape(2, 8, 8, NLON, COLS).transpose(3, 4, 1, 0, 2).reshape(NLON, COLS, 128)
    back = np.pad(back, ((0, 0), (0, 2), (0, 0))).reshape(256, 128)
    return fwd, back


def lat_tables():
    h = np.arange(H)
    angle = 2.0 * math.pi * ((h[:, None] * h[None, :]) % H) / H
    cos, sin = np.cos(angle) / math.sqrt(H), np.sin(angle) / math.sqrt(H)
    fwd = np.block([[cos, sin], [-sin, cos]])
    back = np.block([[cos, -sin], [sin, cos]])
    return fwd, back


def norm(values, gain):
    centre = jnp.mean(values, axis=-1, keepdims=True)
    off = values - centre
    spread = jnp.mean(jnp.square(off), axis=-1, keepdims=True)
    return off * lax.rsqrt(spread + 1e-05) * gain


def dot(left, right):
    return jnp.dot(left, right, preferred_element_type=F32)


def kernel(
    grid_h, pw_h, one_h, two_h, up_h, down_h, tab_h,
    g1_ref, bias_ref, g2_ref, sel_ref, fw_ref, bw_ref, fh_ref, bh_ref,
    out_ref,
    grid_v, pw_v, one_v, two_v, up_v, down_v, tab_v,
    t_v, m_v, l_v, lhs_v, acc_v, nf_v, tn_v, nrm_v,
    ew_s, ew_r, ns_s, ns_r,
    p1_s, p1_r, p2_s, p2_r, p3_s, p3_r, p4_s, p4_r,
    z_v, v_v, w1_v, w2_v,
    lsem, halo_ss, halo_rs, s1, r1, s2, r2, s3, r3, s4, r4,
):
    a = lax.axis_index("lat")
    b = lax.axis_index("lon")
    q = b // 16
    p = b % 16
    n = b % 8
    g = 2 * a + q

    def load(index, src, dst):
        copy = pltpu.make_async_copy(src, dst, lsem.at[index])
        copy.start()
        return copy

    c_grid = load(0, grid_h, grid_v)
    c_tab = load(1, tab_h, tab_v)
    c_pw = load(3, pw_h, pw_v)
    c_one = load(4, one_h.at[:, n], one_v)
    c_two = load(5, two_h.at[:, n], two_v)
    c_up = load(6, up_h, up_v)
    c_down = load(7, down_h, down_v)

    barrier = pltpu.get_barrier_semaphore()

    def greet_lon(d, _):
        pl.semaphore_signal(
            barrier, inc=1, device_id=(a, lax.rem(b + d, NLON)), device_id_type=MESH
        )
        return 0

    lax.fori_loop(1, NLON, greet_lon, 0)

    def greet_lat(d, _):
        mate = lax.rem(a + 1 + d // 2, NLAT)
        pl.semaphore_signal(
            barrier, inc=1, device_id=(mate, (d % 2) * 16 + p), device_id_type=MESH
        )
        return 0

    lax.fori_loop(0, 6, greet_lat, 0)

    nf_v[:, :, 144:] = jnp.zeros((6, 2, 48, 128), F32)
    ns_s[...] = jnp.zeros_like(ns_s)
    c_grid.wait()
    for smp in range(2):
        for lp in range(3):
            block = grid_v[smp, :, 16 * lp : 16 * lp + 16, :]
            block = block.astype(F32).reshape(NV, 2, 8, 192)
            for half in range(2):
                x = block[:, half].reshape(NV * 8, 192).astype(BF16)
                turned = lax.dot_general(
                    sel_ref[...], x, (((1,), (1,)), ((), ())), preferred_element_type=F32
                )
                first = (6 * smp + 2 * lp + half) * ROWS
                for r8 in range(8):
                    t_v[r8, first : first + ROWS, :] = turned[ROWS * r8 : ROWS * r8 + ROWS]

    c_tab.wait()
    for half in range(2):
        value = dot(t_v[4 * half].astype(BF16), tab_v[0])
        for r in range(1, 4):
            value = value + dot(t_v[4 * half + r].astype(BF16), tab_v[r])
        for tile in range(6):
            part = value[:, 128 * tile : 128 * tile + 128].reshape(2, COLS, ROWS, 128)
            for smp in range(2):
                m_v[half, tile, smp, 1 : 1 + COLS] = part[smp]
                if tile >= 3:
                    ew_s[0, half, tile - 3, smp] = part[smp, COLS - 1].astype(BF16)
                else:
                    ew_s[1, half, tile, smp] = part[smp, 0].astype(BF16)

    pl.semaphore_wait(barrier, NLON - 1 + 6)

    def remote(src, dst, ssem, rsem, dev):
        return pltpu.make_async_remote_copy(
            src_ref=src, dst_ref=dst, send_sem=ssem, recv_sem=rsem,
            device_id=dev, device_id_type=MESH,
        )

    east = remote(ew_s.at[0], ew_r.at[0], halo_ss.at[0], halo_rs.at[0], (a, lax.rem(b + 1, NLON)))
    west = remote(
        ew_s.at[1], ew_r.at[1], halo_ss.at[1], halo_rs.at[1], (a, lax.rem(b + NLON - 1, NLON))
    )
    east.start()
    west.start()
    east.wait_recv()
    west.wait_recv()
    for half in range(2):
        for tile in range(3):
            for smp in range(2):
                m_v[half, 3 + tile, smp, 0] = ew_r[0, half, tile, smp].astype(F32)
                m_v[half, tile, smp, COLS + 1] = ew_r[1, half, tile, smp].astype(F32)

    def patch_tile(half, tile, smp):
        lane, slot = ((3, 0), (4, 0), (5, 0), (1, 1), (2, 1), (3, 1), (4, 1), (5, 1), (1, 2), (2, 2))[tile]
        value = m_v[half, lane, smp, slot : slot + COLS]
        if tile in (2, 7):
            value = value + m_v[half, 0, smp, slot + 1 : slot + 1 + COLS]
        return value

    for half in (1, 0):
        for tile in range(10):
            for smp in range(2):
                value = patch_tile(half, tile, smp)
                for j in range(COLS):
                    first = 40 * (COLS * smp + j) + 8
                    l_v[half, tile, first : first + ROWS, :] = value[j]
                lhs_v[half, 144 * smp : 144 * smp + 144, 128 * tile : 128 * tile + 128] = (
                    value.reshape(144, 128).astype(BF16)
                )
            cols = slice(128 * tile, 128 * tile + 128)
            if half == 1:
                ns_s[0, :12, cols] = l_v[1, tile, pl.ds(31, 12, stride=40), :].astype(BF16)
            else:
                ns_s[1, :12, cols] = l_v[0, tile, pl.ds(8, 12, stride=40), :].astype(BF16)
    south = remote(ns_s.at[0], ns_r.at[0], halo_ss.at[2], halo_rs.at[2], (lax.rem(a + 1, NLAT), b))
    north = remote(
        ns_s.at[1], ns_r.at[1], halo_ss.at[3], halo_rs.at[3], (lax.rem(a + NLAT - 1, NLAT), b)
    )
    south.start()
    north.start()

    c_pw.wait()
    for count, (off, half) in enumerate(((1, 0), (2, 1), (0, 1), (3, 0))):
        if count == 2:
            south.wait_recv()
            north.wait_recv()
            for tile in range(10):
                cols = slice(128 * tile, 128 * tile + 128)
                l_v[1, tile, pl.ds(7, 12, stride=40), :] = jnp.where(
                    a > 0, ns_r[0, :12, cols].astype(F32), 0.0
                )
                l_v[0, tile, pl.ds(32, 12, stride=40), :] = jnp.where(
                    a < NLAT - 1, ns_r[1, :12, cols].astype(F32), 0.0
                )
        if count >= 2:
            lead = 7 if half == 1 else 9
            for tile in range(10):
                rows = [l_v[half, tile, 40 * m + lead : 40 * m + lead + ROWS, :] for m in range(12)]
                lhs_v[half, :, 128 * tile : 128 * tile + 128] = jnp.concatenate(
                    rows, axis=0
                ).astype(BF16)
        for tile in range(3):
            cols = slice(256 * tile, 256 * tile + 256)
            value = dot(lhs_v[half], pw_v[1280 * off : 1280 * off + 1280, cols])
            if count == 0:
                acc_v[:, cols] = value
            else:
                acc_v[:, cols] += value

    for smp in range(2):
        rows = slice(144 * smp, 144 * smp + 144)
        tok = acc_v[rows, :].astype(BF16).astype(F32)
        normed = norm(tok, g1_ref[...].reshape(1, C)).astype(BF16).astype(F32)
        tn_v[rows, :] = tok + normed
        for tile in range(6):
            nf_v[tile, smp, :144] = normed[:, 128 * tile : 128 * tile + 128]

        def send_tokens(part, _):
            planes = [
                jnp.concatenate(
                    [nf_v[t, smp, pl.ds(part * ROW12 + i, 8, stride=ROWS), :] for t in range(6)],
                    axis=1,
                )
                for i in range(ROW12)
            ]
            for blk in range(NB):
                msg = jnp.concatenate(
                    [plane[:, BS * blk : BS * blk + BS] for plane in planes], axis=1
                )
                dest = part * 16 + smp * 8 + blk
                p1_s[dest] = msg.astype(BF16)

                @pl.when(dest != b)
                def _():
                    remote(p1_s.at[dest], p1_r.at[b], s1.at[dest], r1.at[b], (a, dest)).start()

                @pl.when(dest == b)
                def _():
                    p1_r[b] = msg.astype(BF16)

            return 0

        lax.fori_loop(0, 2, send_tokens, 0)

    c_one.wait()
    c_two.wait()
    for src, dst in ((one_v, w1_v), (two_v, w2_v)):
        dst[...] = jnp.zeros_like(dst)
        dst[0:BS, 0:BS] = src[0].astype(BF16)
        dst[0:BS, 128 : 128 + BS] = src[1].astype(BF16)
        dst[128 : 128 + BS, 0:BS] = -src[1].astype(BF16)
        dst[128 : 128 + BS, 128 : 128 + BS] = src[0].astype(BF16)
    bias = jnp.zeros((1, 256), F32)
    for blk in range(NB):
        parts = []
        for ri in range(2):
            parts.append(bias_ref[ri : ri + 1, BS * blk : BS * blk + BS])
            parts.append(jnp.zeros((1, 32), F32))
        bias = bias + jnp.where(n == blk, jnp.concatenate(parts, axis=1), 0.0)

    def wait1(d, _):
        src = lax.rem(b + d, NLON)
        remote(p1_s.at[src], p1_r.at[src], s1.at[src], r1.at[src], (a, src)).wait_recv()
        return 0

    lax.fori_loop(1, NLON, wait1, 0)

    x = p1_r[...].astype(F32).reshape(256, MSG).astype(BF16)
    y = dot(fw_ref[...], x)
    p2_s[...] = y.reshape(8, 16, MSG).astype(BF16)

    def mate_of(d):
        other = lax.rem(g + d, 8)
        return other, (other // 2, (other % 2) * 16 + p)

    def send2(d, _):
        other, dev = mate_of(d)
        remote(p2_s.at[other], p2_r.at[g], s2.at[other], r2.at[g], dev).start()
        return 0

    lax.fori_loop(1, 8, send2, 0)

    def spread(src, value):
        for i in range(ROW12):
            piece = value[:, BS * i : BS * i + BS]
            piece = jnp.concatenate([piece, jnp.zeros((16, 128 - BS), F32)], axis=1)
            z_v[pl.ds(ROW12 * src + i, 8, stride=192), :] = piece[:8]
            z_v[pl.ds(H + ROW12 * src + i, 8, stride=192), :] = piece[8:]

    spread(g, p2_s[g].astype(F32))

    def take2(d, _):
        other, dev = mate_of(d)
        remote(p2_s.at[other], p2_r.at[other], s2.at[other], r2.at[other], dev).wait_recv()
        spread(other, p2_r[other].astype(F32))
        return 0

    lax.fori_loop(1, 8, take2, 0)

    for pair in range(4):
        k0, k1 = 384 * pair, 384 * pair + 192
        z = jnp.concatenate([z_v[k0 : k0 + 192, :], z_v[k1 : k1 + 192, :]], axis=1).astype(BF16)
        spec = dot(fh_ref[...], z)
        modes = jnp.concatenate(
            [
                jnp.concatenate([spec[:H, :128], spec[H:, :128]], axis=1),
                jnp.concatenate([spec[:H, 128:], spec[H:, 128:]], axis=1),
            ],
            axis=0,
        )
        mid = jnp.maximum(dot(modes.astype(BF16), w1_v[...]) + bias, 0.0)
        res = dot(mid.astype(BF16), w2_v[...])
        res = res - jnp.clip(res, -0.01, 0.01)
        back = jnp.concatenate(
            [
                jnp.concatenate([res[:H, :128], res[H:, :128]], axis=1),
                jnp.concatenate([res[:H, 128:], res[H:, 128:]], axis=1),
            ],
            axis=0,
        )
        rows = dot(bh_ref[...], back.astype(BF16))
        v_v[k0 : k0 + 192, :] = rows[:, :128]
        v_v[k1 : k1 + 192, :] = rows[:, 128:]

    def gather_rows(dest):
        pieces = []
        for i in range(ROW12):
            re = v_v[pl.ds(ROW12 * dest + i, 8, stride=192), :]
            im = v_v[pl.ds(H + ROW12 * dest + i, 8, stride=192), :]
            pieces.append(jnp.concatenate([re, im], axis=0)[:, :BS])
        return jnp.concatenate(pieces, axis=1).astype(BF16)

    def send3(d, _):
        other, dev = mate_of(d)
        p3_s[other] = gather_rows(other)
        remote(p3_s.at[other], p3_r.at[g], s3.at[other], r3.at[g], dev).start()
        return 0

    lax.fori_loop(1, 8, send3, 0)
    p3_r[g] = gather_rows(g)

    def wait3(d, _):
        other, dev = mate_of(d)
        remote(p3_s.at[other], p3_r.at[other], s3.at[other], r3.at[other], dev).wait_recv()
        return 0

    lax.fori_loop(1, 8, wait3, 0)

    field = dot(bw_ref[...], p3_r[...].reshape(128, MSG))
    p4_s[...] = field.reshape(NLON, 8, MSG).astype(BF16)

    def send4(d, _):
        dest = lax.rem(b + d, NLON)
        remote(p4_s.at[dest], p4_r.at[b], s4.at[dest], r4.at[b], (a, dest)).start()
        return 0

    lax.fori_loop(1, NLON, send4, 0)
    p4_r[b] = p4_s[b]

    def wait4(d, _):
        src = lax.rem(b + d, NLON)
        remote(p4_s.at[src], p4_r.at[src], s4.at[src], r4.at[src], (a, src)).wait_recv()
        return 0

    lax.fori_loop(1, NLON, wait4, 0)

    for smp in range(2):

        def join(part, _):
            msgs = [p4_r[part * 16 + smp * 8 + blk].astype(F32) for blk in range(NB)]
            for i in range(ROW12):
                plane = jnp.concatenate([m[:, BS * i : BS * i + BS] for m in msgs], axis=1)
                for tile in range(6):
                    nf_v[tile, smp, pl.ds(part * ROW12 + i, 8, stride=ROWS), :] = plane[
                        :, 128 * tile : 128 * tile + 128
                    ]
            return 0

        lax.fori_loop(0, 2, join, 0)
        rows = slice(144 * smp, 144 * smp + 144)
        field = jnp.concatenate([nf_v[tile, smp, :144] for tile in range(6)], axis=1)
        middle = (field + tn_v[rows, :]).astype(BF16).astype(F32)
        acc_v[rows, :] = middle
        nrm_v[rows, :] = norm(middle, g2_ref[...].reshape(1, C)).astype(BF16)

    c_up.wait()
    c_down.wait()

    def mlp(step, _):
        cols = pl.ds(pl.multiple_of(step * 256, 256), 256)
        hidden = dot(nrm_v[...], up_v[:, cols])
        hidden = 0.5 * hidden * (1.0 + lax.erf(hidden * (1.0 / math.sqrt(2.0))))
        acc_v[...] += dot(hidden.astype(BF16), down_v[cols, :])
        return 0

    lax.fori_loop(0, HID // 256, mlp, 0)
    out_ref[...] = acc_v[...].reshape(2, COLS, ROWS, C).astype(BF16)

    for copy in (east, west, south, north):
        copy.wait_send()

    def drain_lon(d, _):
        dest = lax.rem(b + d, NLON)
        remote(p1_s.at[dest], p1_r.at[b], s1.at[dest], r1.at[b], (a, dest)).wait_send()
        remote(p4_s.at[dest], p4_r.at[b], s4.at[dest], r4.at[b], (a, dest)).wait_send()
        return 0

    lax.fori_loop(1, NLON, drain_lon, 0)

    def drain_lat(d, _):
        other, dev = mate_of(d)
        remote(p2_s.at[other], p2_r.at[g], s2.at[other], r2.at[g], dev).wait_send()
        remote(p3_s.at[other], p3_r.at[g], s3.at[other], r3.at[g], dev).wait_send()
        return 0

    lax.fori_loop(1, 8, drain_lat, 0)


def local(
    grid, patch_weight, norm_gain_one, spectral_one, spectral_bias, spectral_two,
    norm_gain_two, fc_up, fc_down,
):
    fw, bw = lon_tables()
    fh, bh = lat_tables()
    const = lambda x: jnp.asarray(x, F32).astype(BF16)
    any_spec = pl.BlockSpec(memory_space=pl.ANY)
    vmem = pl.BlockSpec(memory_space=pltpu.VMEM)
    dma = pltpu.SemaphoreType.DMA
    out = pl.pallas_call(
        kernel,
        out_shape=jax.ShapeDtypeStruct((2, COLS, ROWS, C), BF16),
        in_specs=[any_spec] * 7 + [vmem] * 8,
        out_specs=vmem,
        scratch_shapes=[
            pltpu.VMEM((2, NV, 48, 192), BF16),
            pltpu.VMEM((5120, C), BF16),
            pltpu.VMEM((2, BS, BS), F32),
            pltpu.VMEM((2, BS, BS), F32),
            pltpu.VMEM((C, HID), BF16),
            pltpu.VMEM((HID, C), BF16),
            pltpu.VMEM((4, 160, 768), BF16),
            pltpu.VMEM((8, 288, 160), F32),
            pltpu.VMEM((2, 6, 2, COLS + 2, ROWS, 128), F32),
            pltpu.VMEM((2, 10, 480, 128), F32),
            pltpu.VMEM((2, 288, 1280), BF16),
            pltpu.VMEM((288, C), F32),
            pltpu.VMEM((6, 2, 192, 128), F32),
            pltpu.VMEM((288, C), F32),
            pltpu.VMEM((288, C), BF16),
            pltpu.VMEM((2, 2, 3, 2, ROWS, 128), BF16),
            pltpu.VMEM((2, 2, 3, 2, ROWS, 128), BF16),
            pltpu.VMEM((2, 16, 1280), BF16),
            pltpu.VMEM((2, 16, 1280), BF16),
            pltpu.VMEM((NLON, 8, MSG), BF16),
            pltpu.VMEM((NLON, 8, MSG), BF16),
            pltpu.VMEM((8, 16, MSG), BF16),
            pltpu.VMEM((8, 16, MSG), BF16),
            pltpu.VMEM((8, 16, MSG), BF16),
            pltpu.VMEM((8, 16, MSG), BF16),
            pltpu.VMEM((NLON, 8, MSG), BF16),
            pltpu.VMEM((NLON, 8, MSG), BF16),
            pltpu.VMEM((8 * 192, 128), F32),
            pltpu.VMEM((8 * 192, 128), F32),
            pltpu.VMEM((256, 256), BF16),
            pltpu.VMEM((256, 256), BF16),
            dma((8,)),
            dma((4,)),
            dma((4,)),
            dma((NLON,)),
            dma((NLON,)),
            dma((8,)),
            dma((8,)),
            dma((8,)),
            dma((8,)),
            dma((NLON,)),
            dma((NLON,)),
        ],
        compiler_params=pltpu.CompilerParams(
            collective_id=0, has_side_effects=True, vmem_limit_bytes=56 * 1024 * 1024
        ),
    )(
        grid.transpose(0, 1, 3, 2), patch_weight, spectral_one, spectral_two, fc_up, fc_down,
        const(feature_table()),
        norm_gain_one, spectral_bias, norm_gain_two,
        const(pick_table()), const(fw), const(bw), const(fh), const(bh),
    )
    return out.transpose(0, 2, 1, 3)


def solution(mesh):
    in_specs = (P(None, None, "lat", "lon"), P(), P(), P(), P(), P(), P(), P(), P())
    out_specs = P(None, "lat", "lon", None)
    return jax.shard_map(local, mesh=mesh, in_specs=in_specs, out_specs=out_specs, check_vma=False)
```

```python
import math

import jax
import jax.numpy as jnp
import numpy as np
from jax import lax
from jax.experimental import pallas as pl
from jax.experimental.pallas import tpu as pltpu
from jax.sharding import PartitionSpec as P

MESH = pl.DeviceIdType.MESH
F32 = jnp.float32
BF16 = jnp.bfloat16

NLAT, NLON = 4, 32
NV, C, HID, NB, BS = 20, 768, 3072, 8, 96
H, W, KW = 96, 192, 64
ROWS, COLS = 24, 6
ROW12 = 12
MSG = ROW12 * BS


def pick_table():
    sel = np.zeros((192, 192), np.float32)
    for r8 in range(8):
        for row in range(ROWS):
            sel[r8 * ROWS + row, 8 * row + r8] = 1.0
    return sel


def feature_table():
    table = np.zeros((4, 160, 768), np.float32)
    for r in range(4):
        for v in range(NV):
            for c8 in range(8):
                table[r, v * 8 + c8, (64, 384)[c8 // 4] + v * 16 + 4 * r + c8 % 4] = 1.0
    return table


def lon_tables():
    k = np.arange(KW)
    w = np.arange(W)
    angle = 2.0 * math.pi * ((k[:, None] * w[None, :]) % W) / W
    scale = 1.0 / math.sqrt(W)
    both = np.stack([np.cos(angle), -np.sin(angle)]) * scale
    fwd = both.reshape(2, 8, 8, NLON, COLS).transpose(1, 0, 2, 3, 4).reshape(128, NLON, COLS)
    fwd = np.pad(fwd, ((0, 0), (0, 0), (0, 2))).reshape(128, 256)
    weight = np.where(k == 0, 1.0, 2.0)
    back = both * weight[None, :, None]
    back = back.reshape(2, 8, 8, NLON, COLS).transpose(3, 4, 1, 0, 2).reshape(NLON, COLS, 128)
    back = np.pad(back, ((0, 0), (0, 2), (0, 0))).reshape(256, 128)
    return fwd, back


def lat_tables():
    h = np.arange(H)
    angle = 2.0 * math.pi * ((h[:, None] * h[None, :]) % H) / H
    cos, sin = np.cos(angle) / math.sqrt(H), np.sin(angle) / math.sqrt(H)
    fwd = np.block([[cos, sin], [-sin, cos]])
    back = np.block([[cos, -sin], [sin, cos]])
    return fwd, back


def norm(values, gain):
    centre = jnp.mean(values, axis=-1, keepdims=True)
    off = values - centre
    spread = jnp.mean(jnp.square(off), axis=-1, keepdims=True)
    return off * lax.rsqrt(spread + 1e-05) * gain


def dot(left, right):
    return jnp.dot(left, right, preferred_element_type=F32)


def kernel(
    grid_h, pw_h, one_h, two_h, up_h, down_h, tab_h,
    g1_ref, bias_ref, g2_ref, sel_ref, fw_ref, bw_ref, fh_ref, bh_ref,
    out_ref,
    grid_v, pw_v, one_v, two_v, up_v, down_v, tab_v,
    t_v, m_v, lhs_v, q0_v, q3_v, tot_v, acc_v, nf_v, tn_v, nrm_v,
    ew_s, ew_r, ns_s, ns_r,
    p1_s, p1_r, p2_s, p2_r, p3_s, p3_r, p4_s, p4_r,
    z_v, v_v, w1_v, w2_v,
    lsem, halo_ss, halo_rs, s1, r1, s2, r2, s3, r3, s4, r4,
):
    a = lax.axis_index("lat")
    b = lax.axis_index("lon")
    q = b // 16
    p = b % 16
    row_y = p // 4
    row_z = p % 4
    mine = (row_y + row_z) % 2
    n = 2 * row_y + row_z // 2
    g = 2 * a + q
    ways = [(da, db) for da in (1, 3) for db in (1, NLON - 1)]

    def load(index, src, dst):
        copy = pltpu.make_async_copy(src, dst, lsem.at[index])
        copy.start()
        return copy

    c_grid = load(0, grid_h, grid_v)
    c_tab = load(1, tab_h, tab_v)
    c_pw = load(3, pw_h, pw_v)
    c_one = load(4, one_h.at[:, n], one_v)
    c_two = load(5, two_h.at[:, n], two_v)
    c_up = load(6, up_h, up_v)
    c_down = load(7, down_h, down_v)

    barrier = pltpu.get_barrier_semaphore()

    def greet_lon(d, _):
        pl.semaphore_signal(
            barrier, inc=1, device_id=(a, lax.rem(b + d, NLON)), device_id_type=MESH
        )
        return 0

    lax.fori_loop(1, NLON, greet_lon, 0)

    def greet_lat(d, _):
        mate = lax.rem(a + 1 + d // 2, NLAT)
        pl.semaphore_signal(
            barrier, inc=1, device_id=(mate, (d % 2) * 16 + p), device_id_type=MESH
        )
        return 0

    lax.fori_loop(0, 6, greet_lat, 0)
    for da, db in ways:
        corner = (lax.rem(a + da, NLAT), lax.rem(b + db, NLON))
        pl.semaphore_signal(barrier, inc=1, device_id=corner, device_id_type=MESH)

    nf_v[:, :, 144:] = jnp.zeros((6, 2, 48, 128), F32)
    for slots in (slice(0, 2), slice(8, 10)):
        m_v[:, :, :, slots] = jnp.zeros((2, 6, 2, 2, ROWS, 128), F32)
    for tile in range(6):
        q0_v[tile, pl.ds(0, 16, stride=32), :] = jnp.zeros((16, 128), F32)
        q3_v[tile, pl.ds(31, 16, stride=32), :] = jnp.zeros((16, 128), F32)
    c_grid.wait()
    for smp in range(2):
        for lp in range(3):
            block = grid_v[smp, :, 16 * lp : 16 * lp + 16, :]
            block = block.astype(F32).reshape(NV, 2, 8, 192)
            for half in range(2):
                x = block[:, half].reshape(NV * 8, 192).astype(BF16)
                turned = lax.dot_general(
                    sel_ref[...], x, (((1,), (1,)), ((), ())), preferred_element_type=F32
                )
                first = (6 * smp + 2 * lp + half) * ROWS
                for r8 in range(8):
                    t_v[r8, first : first + ROWS, :] = turned[ROWS * r8 : ROWS * r8 + ROWS]

    c_tab.wait()
    for half in range(2):
        value = dot(t_v[4 * half].astype(BF16), tab_v[0])
        for r in range(1, 4):
            value = value + dot(t_v[4 * half + r].astype(BF16), tab_v[r])
        for tile in range(6):
            part = value[:, 128 * tile : 128 * tile + 128].reshape(2, COLS, ROWS, 128)
            for smp in range(2):
                m_v[half, tile, smp, 2 : 2 + COLS] = part[smp]

    for half in range(2):
        for tile in range(10):
            lane, slot = (
                (3, 0), (4, 0), (5, 0), (1, 1), (2, 1), (3, 1), (4, 1), (5, 1), (1, 2), (2, 2)
            )[tile]
            for smp in range(2):
                value = m_v[half, lane, smp, slot : slot + 8]
                if tile in (2, 7):
                    value = value + m_v[half, 0, smp, slot + 1 : slot + 9]
                lhs_v[half, 192 * smp : 192 * smp + 192, 128 * tile : 128 * tile + 128] = (
                    value.reshape(192, 128).astype(BF16)
                )

    c_pw.wait()
    for pair in range(3):
        cols = slice(256 * pair, 256 * pair + 256)
        weight = lambda off: pw_v[1280 * off : 1280 * off + 1280, cols]
        above = dot(lhs_v[1], weight(0))
        below = dot(lhs_v[0], weight(3))
        for lane in range(2):
            tile = 2 * pair + lane
            lanes = slice(128 * lane, 128 * lane + 128)
            for m in range(16):
                rows = slice(ROWS * m, ROWS * m + ROWS)
                q0_v[tile, 32 * m + 1 : 32 * m + 1 + ROWS, :] = above[rows, lanes]
                q3_v[tile, 32 * m + 7 : 32 * m + 7 + ROWS, :] = below[rows, lanes]
        value = dot(lhs_v[0], weight(1)) + dot(lhs_v[1], weight(2))
        for lane in range(2):
            tile = 2 * pair + lane
            lanes = slice(128 * lane, 128 * lane + 128)
            shifted = (
                q0_v[tile].reshape(16, 32, 128)[:, :ROWS] + q3_v[tile].reshape(16, 32, 128)[:, 8:]
            )
            tot_v[tile] = value[:, lanes] + shifted.reshape(384, 128)

    for tile in range(6):
        cols = slice(128 * tile, 128 * tile + 128)
        for smp in range(2):
            for way, slot in ((0, 7), (1, 0)):
                first = ROWS * (8 * smp + slot)
                ew_s[way, smp, :, cols] = tot_v[tile, first : first + ROWS, :].astype(BF16)
        ns_s[0, :, cols] = q0_v[tile, pl.ds(ROWS, 16, stride=32), :].astype(BF16)
        ns_s[1, :, cols] = q3_v[tile, pl.ds(7, 16, stride=32), :].astype(BF16)

    pl.semaphore_wait(barrier, NLON - 1 + 6 + 4)

    def remote(src, dst, ssem, rsem, dev):
        return pltpu.make_async_remote_copy(
            src_ref=src, dst_ref=dst, send_sem=ssem, recv_sem=rsem,
            device_id=dev, device_id_type=MESH,
        )

    halos = []
    for src, da in ((0, 1), (1, 3)):
        for side, db in enumerate((0, 1, NLON - 1)):
            slot = 3 * src + side
            halos.append((ns_s.at[src], ns_r.at[slot], 2 + slot, da, db))
    for src, db in ((0, 1), (1, NLON - 1)):
        halos.append((ew_s.at[src], ew_r.at[src], src, 0, db))
    halos = [
        remote(
            src, dst, halo_ss.at[sem], halo_rs.at[sem],
            (lax.rem(a + da, NLAT), lax.rem(b + db, NLON)),
        )
        for src, dst, sem, da, db in halos
    ]
    for copy in halos:
        copy.start()
    for copy in halos:
        copy.wait_recv()

    slot_ids = lax.broadcasted_iota(jnp.int32, (2, 8, 128), 1)

    def edge_row(first, cols):
        straight, west, east = [
            ns_r[first + k, :, cols].astype(F32).reshape(2, 8, 128) for k in range(3)
        ]
        west = jnp.concatenate([west[:, 6:], west[:, :6]], axis=1)
        east = jnp.concatenate([east[:, 2:], east[:, :2]], axis=1)
        straight = straight + jnp.where(slot_ids == 1, west, 0.0)
        return (straight + jnp.where(slot_ids == 6, east, 0.0)).reshape(16, 128)

    for tile in range(6):
        cols = slice(128 * tile, 128 * tile + 128)
        for smp in range(2):
            for way, slot in ((0, 1), (1, 6)):
                first = ROWS * (8 * smp + slot)
                tot_v[tile, first : first + ROWS, :] += ew_r[way, smp, :, cols].astype(F32)
        top, bottom = pl.ds(0, 16, stride=ROWS), pl.ds(ROWS - 1, 16, stride=ROWS)
        tot_v[tile, top, :] += jnp.where(a > 0, edge_row(0, cols), 0.0)
        tot_v[tile, bottom, :] += jnp.where(a < NLAT - 1, edge_row(3, cols), 0.0)

    def owner(part, smp, blk):
        return part * 16 + (blk // 2) * 4 + (blk % 2) * 2 + (smp + blk // 2) % 2

    for smp in range(2):
        rows = slice(144 * smp, 144 * smp + 144)
        first = ROWS * (8 * smp + 1)
        tok = jnp.concatenate([tot_v[t, first : first + 144, :] for t in range(6)], axis=1)
        tok = tok.astype(BF16).astype(F32)
        normed = norm(tok, g1_ref[...].reshape(1, C)).astype(BF16).astype(F32)
        tn_v[rows, :] = tok + normed
        for tile in range(6):
            nf_v[tile, smp, :144] = normed[:, 128 * tile : 128 * tile + 128]
        for part in range(2):
            planes = [
                jnp.concatenate(
                    [nf_v[t, smp, pl.ds(part * ROW12 + i, 8, stride=ROWS), :] for t in range(6)],
                    axis=1,
                )
                for i in range(ROW12)
            ]
            for blk in range(NB):
                msg = jnp.concatenate(
                    [plane[:, BS * blk : BS * blk + BS] for plane in planes], axis=1
                )
                p1_s[owner(part, smp, blk)] = msg.astype(BF16)
        odd = (smp + mine) % 2
        for dx in (1, 0):
            for dy in (2, 1, 3, 0):
                for dz in (2, 0):
                    dest = (
                        ((q + dx) % 2) * 16 + ((row_y + dy) % 4) * 4 + (row_z + dz + (odd + dy) % 2) % 4
                    )

                    def send(dest=dest):
                        remote(
                            p1_s.at[dest], p1_r.at[b], s1.at[dest], r1.at[b], (a, dest)
                        ).start()

                    if (dx, dy, dz) == (0, 0, 0):
                        pl.when(odd == 1)(send)
                    else:
                        send()
    p1_r[b] = p1_s[b]

    c_one.wait()
    c_two.wait()
    for src, dst in ((one_v, w1_v), (two_v, w2_v)):
        dst[...] = jnp.zeros_like(dst)
        dst[0:BS, 0:BS] = src[0].astype(BF16)
        dst[0:BS, 128 : 128 + BS] = src[1].astype(BF16)
        dst[128 : 128 + BS, 0:BS] = -src[1].astype(BF16)
        dst[128 : 128 + BS, 128 : 128 + BS] = src[0].astype(BF16)
    bias = jnp.zeros((1, 256), F32)
    for blk in range(NB):
        parts = []
        for ri in range(2):
            parts.append(bias_ref[ri : ri + 1, BS * blk : BS * blk + BS])
            parts.append(jnp.zeros((1, 32), F32))
        bias = bias + jnp.where(n == blk, jnp.concatenate(parts, axis=1), 0.0)

    def wait1(d, _):
        src = lax.rem(b + d, NLON)
        remote(p1_s.at[src], p1_r.at[src], s1.at[src], r1.at[src], (a, src)).wait_recv()
        return 0

    lax.fori_loop(1, NLON, wait1, 0)

    x = p1_r[...].astype(F32).reshape(256, MSG).astype(BF16)
    y = dot(fw_ref[...], x)
    p2_s[...] = y.reshape(8, 16, MSG).astype(BF16)

    def mate_of(d):
        other = lax.rem(g + d, 8)
        return other, (other // 2, (other % 2) * 16 + p)

    def send2(d, _):
        other, dev = mate_of(d)
        remote(p2_s.at[other], p2_r.at[g], s2.at[other], r2.at[g], dev).start()
        return 0

    lax.fori_loop(1, 8, send2, 0)

    def spread(src, value):
        for i in range(ROW12):
            piece = value[:, BS * i : BS * i + BS]
            piece = jnp.concatenate([piece, jnp.zeros((16, 128 - BS), F32)], axis=1)
            z_v[pl.ds(ROW12 * src + i, 8, stride=192), :] = piece[:8]
            z_v[pl.ds(H + ROW12 * src + i, 8, stride=192), :] = piece[8:]

    spread(g, p2_s[g].astype(F32))

    def take2(d, _):
        other, dev = mate_of(d)
        remote(p2_s.at[other], p2_r.at[other], s2.at[other], r2.at[other], dev).wait_recv()
        spread(other, p2_r[other].astype(F32))
        return 0

    lax.fori_loop(1, 8, take2, 0)

    for pair in range(4):
        k0, k1 = 384 * pair, 384 * pair + 192
        z = jnp.concatenate([z_v[k0 : k0 + 192, :], z_v[k1 : k1 + 192, :]], axis=1).astype(BF16)
        spec = dot(fh_ref[...], z)
        modes = jnp.concatenate(
            [
                jnp.concatenate([spec[:H, :128], spec[H:, :128]], axis=1),
                jnp.concatenate([spec[:H, 128:], spec[H:, 128:]], axis=1),
            ],
            axis=0,
        )
        mid = jnp.maximum(dot(modes.astype(BF16), w1_v[...]) + bias, 0.0)
        res = dot(mid.astype(BF16), w2_v[...])
        res = res - jnp.clip(res, -0.01, 0.01)
        back = jnp.concatenate(
            [
                jnp.concatenate([res[:H, :128], res[H:, :128]], axis=1),
                jnp.concatenate([res[:H, 128:], res[H:, 128:]], axis=1),
            ],
            axis=0,
        )
        rows = dot(bh_ref[...], back.astype(BF16))
        v_v[k0 : k0 + 192, :] = rows[:, :128]
        v_v[k1 : k1 + 192, :] = rows[:, 128:]

    def gather_rows(dest):
        pieces = []
        for i in range(ROW12):
            re = v_v[pl.ds(ROW12 * dest + i, 8, stride=192), :]
            im = v_v[pl.ds(H + ROW12 * dest + i, 8, stride=192), :]
            pieces.append(jnp.concatenate([re, im], axis=0)[:, :BS])
        return jnp.concatenate(pieces, axis=1).astype(BF16)

    def send3(d, _):
        other, dev = mate_of(d)
        p3_s[other] = gather_rows(other)
        remote(p3_s.at[other], p3_r.at[g], s3.at[other], r3.at[g], dev).start()
        return 0

    lax.fori_loop(1, 8, send3, 0)
    p3_r[g] = gather_rows(g)

    def wait3(d, _):
        other, dev = mate_of(d)
        remote(p3_s.at[other], p3_r.at[other], s3.at[other], r3.at[other], dev).wait_recv()
        return 0

    lax.fori_loop(1, 8, wait3, 0)

    field = dot(bw_ref[...], p3_r[...].reshape(128, MSG))
    p4_s[...] = field.reshape(NLON, 8, MSG).astype(BF16)

    steps = [(dx, dy, dz) for dx in range(2) for dy in range(4) for dz in range(4)]
    steps.sort(key=lambda t: -(t[0] + min(t[1], 4 - t[1]) + min(t[2], 4 - t[2])))
    for dx, dy, dz in steps[:-1]:
        dest = ((q + dx) % 2) * 16 + ((row_y + dy) % 4) * 4 + (row_z + dz) % 4
        remote(p4_s.at[dest], p4_r.at[b], s4.at[dest], r4.at[b], (a, dest)).start()
    p4_r[b] = p4_s[b]

    def wait4(d, _):
        src = lax.rem(b + d, NLON)
        remote(p4_s.at[src], p4_r.at[src], s4.at[src], r4.at[src], (a, src)).wait_recv()
        return 0

    lax.fori_loop(1, NLON, wait4, 0)

    for smp in range(2):

        def join(part, _):
            msgs = [p4_r[owner(part, smp, blk)].astype(F32) for blk in range(NB)]
            for i in range(ROW12):
                plane = jnp.concatenate([m[:, BS * i : BS * i + BS] for m in msgs], axis=1)
                for tile in range(6):
                    nf_v[tile, smp, pl.ds(part * ROW12 + i, 8, stride=ROWS), :] = plane[
                        :, 128 * tile : 128 * tile + 128
                    ]
            return 0

        lax.fori_loop(0, 2, join, 0)
        rows = slice(144 * smp, 144 * smp + 144)
        field = jnp.concatenate([nf_v[tile, smp, :144] for tile in range(6)], axis=1)
        middle = (field + tn_v[rows, :]).astype(BF16).astype(F32)
        acc_v[rows, :] = middle
        nrm_v[rows, :] = norm(middle, g2_ref[...].reshape(1, C)).astype(BF16)

    c_up.wait()
    c_down.wait()

    def mlp(step, _):
        cols = pl.ds(pl.multiple_of(step * 256, 256), 256)
        hidden = dot(nrm_v[...], up_v[:, cols])
        hidden = 0.5 * hidden * (1.0 + lax.erf(hidden * (1.0 / math.sqrt(2.0))))
        acc_v[...] += dot(hidden.astype(BF16), down_v[cols, :])
        return 0

    lax.fori_loop(0, HID // 256, mlp, 0)
    out_ref[...] = acc_v[...].reshape(2, COLS, ROWS, C).astype(BF16)

    for copy in halos:
        copy.wait_send()

    def drain_lon(d, _):
        dest = lax.rem(b + d, NLON)
        remote(p1_s.at[dest], p1_r.at[b], s1.at[dest], r1.at[b], (a, dest)).wait_send()
        remote(p4_s.at[dest], p4_r.at[b], s4.at[dest], r4.at[b], (a, dest)).wait_send()
        return 0

    lax.fori_loop(1, NLON, drain_lon, 0)

    def drain_lat(d, _):
        other, dev = mate_of(d)
        remote(p2_s.at[other], p2_r.at[g], s2.at[other], r2.at[g], dev).wait_send()
        remote(p3_s.at[other], p3_r.at[g], s3.at[other], r3.at[g], dev).wait_send()
        return 0

    lax.fori_loop(1, 8, drain_lat, 0)


def local(
    grid, patch_weight, norm_gain_one, spectral_one, spectral_bias, spectral_two,
    norm_gain_two, fc_up, fc_down,
):
    fw, bw = lon_tables()
    fh, bh = lat_tables()
    const = lambda x: jnp.asarray(x, F32).astype(BF16)
    any_spec = pl.BlockSpec(memory_space=pl.ANY)
    vmem = pl.BlockSpec(memory_space=pltpu.VMEM)
    dma = pltpu.SemaphoreType.DMA
    out = pl.pallas_call(
        kernel,
        out_shape=jax.ShapeDtypeStruct((2, COLS, ROWS, C), BF16),
        in_specs=[any_spec] * 7 + [vmem] * 8,
        out_specs=vmem,
        scratch_shapes=[
            pltpu.VMEM((2, NV, 48, 192), BF16),
            pltpu.VMEM((5120, C), BF16),
            pltpu.VMEM((2, BS, BS), F32),
            pltpu.VMEM((2, BS, BS), F32),
            pltpu.VMEM((C, HID), BF16),
            pltpu.VMEM((HID, C), BF16),
            pltpu.VMEM((4, 160, 768), BF16),
            pltpu.VMEM((8, 288, 160), F32),
            pltpu.VMEM((2, 6, 2, 10, ROWS, 128), F32),
            pltpu.VMEM((2, 384, 1280), BF16),
            pltpu.VMEM((6, 512, 128), F32),
            pltpu.VMEM((6, 512, 128), F32),
            pltpu.VMEM((6, 384, 128), F32),
            pltpu.VMEM((288, C), F32),
            pltpu.VMEM((6, 2, 192, 128), F32),
            pltpu.VMEM((288, C), F32),
            pltpu.VMEM((288, C), BF16),
            pltpu.VMEM((2, 2, ROWS, C), BF16),
            pltpu.VMEM((2, 2, ROWS, C), BF16),
            pltpu.VMEM((2, 16, C), BF16),
            pltpu.VMEM((6, 16, C), BF16),
            pltpu.VMEM((NLON, 8, MSG), BF16),
            pltpu.VMEM((NLON, 8, MSG), BF16),
            pltpu.VMEM((8, 16, MSG), BF16),
            pltpu.VMEM((8, 16, MSG), BF16),
            pltpu.VMEM((8, 16, MSG), BF16),
            pltpu.VMEM((8, 16, MSG), BF16),
            pltpu.VMEM((NLON, 8, MSG), BF16),
            pltpu.VMEM((NLON, 8, MSG), BF16),
            pltpu.VMEM((8 * 192, 128), F32),
            pltpu.VMEM((8 * 192, 128), F32),
            pltpu.VMEM((256, 256), BF16),
            pltpu.VMEM((256, 256), BF16),
            dma((8,)),
            dma((8,)),
            dma((8,)),
            dma((NLON,)),
            dma((NLON,)),
            dma((8,)),
            dma((8,)),
            dma((8,)),
            dma((8,)),
            dma((NLON,)),
            dma((NLON,)),
        ],
        compiler_params=pltpu.CompilerParams(
            collective_id=0, has_side_effects=True, vmem_limit_bytes=56 * 1024 * 1024
        ),
    )(
        grid.transpose(0, 1, 3, 2), patch_weight, spectral_one, spectral_two, fc_up, fc_down,
        const(feature_table()),
        norm_gain_one, spectral_bias, norm_gain_two,
        const(pick_table()), const(fw), const(bw), const(fh), const(bh),
    )
    return out.transpose(0, 2, 1, 3)


def solution(mesh):
    in_specs = (P(None, None, "lat", "lon"), P(), P(), P(), P(), P(), P(), P(), P())
    out_specs = P(None, "lat", "lon", None)
    return jax.shard_map(local, mesh=mesh, in_specs=in_specs, out_specs=out_specs, check_vma=False)
```

```python
import math

import jax
import jax.numpy as jnp
import numpy as np
from jax import lax
from jax.experimental import pallas as pl
from jax.experimental.pallas import tpu as pltpu
from jax.sharding import PartitionSpec as P

MESH = pl.DeviceIdType.MESH
F32 = jnp.float32
BF16 = jnp.bfloat16

NLAT, NLON = 4, 32
NV, C, HID, NB, BS = 20, 768, 3072, 8, 96
H, W, KW = 96, 192, 64
ROWS, COLS = 24, 6
ROW12 = 12
MSG = ROW12 * BS


def pick_table():
    sel = np.zeros((192, 192), np.float32)
    for r8 in range(8):
        for row in range(ROWS):
            sel[r8 * ROWS + row, 8 * row + r8] = 1.0
    return sel


def feature_table():
    table = np.zeros((4, 160, 768), np.float32)
    for r in range(4):
        for v in range(NV):
            for c8 in range(8):
                table[r, v * 8 + c8, (64, 384)[c8 // 4] + v * 16 + 4 * r + c8 % 4] = 1.0
    return table


def lon_tables():
    k = np.arange(KW)
    w = np.arange(W)
    angle = 2.0 * math.pi * ((k[:, None] * w[None, :]) % W) / W
    scale = 1.0 / math.sqrt(W)
    both = np.stack([np.cos(angle), -np.sin(angle)]) * scale
    fwd = both.reshape(2, 8, 2, 4, W).transpose(2, 1, 3, 0, 4).reshape(128, NLON, COLS)
    fwd = np.pad(fwd, ((0, 0), (0, 0), (0, 2))).reshape(128, 256)
    weight = np.where(k == 0, 1.0, 2.0)
    back = both * weight[None, :, None]
    back = back.reshape(2, 8, 2, 4, W).transpose(4, 2, 1, 3, 0).reshape(NLON, COLS, 128)
    back = np.pad(back, ((0, 0), (0, 2), (0, 0))).reshape(256, 128)
    return fwd, back


def lat_tables():
    h = np.arange(H)
    angle = 2.0 * math.pi * ((h[:, None] * h[None, :]) % H) / H
    cos, sin = np.cos(angle) / math.sqrt(H), np.sin(angle) / math.sqrt(H)
    fwd = np.block([[cos, sin], [-sin, cos]])
    back = np.block([[cos, -sin], [sin, cos]])
    return fwd, back


def norm(values, gain):
    centre = jnp.mean(values, axis=-1, keepdims=True)
    off = values - centre
    spread = jnp.mean(jnp.square(off), axis=-1, keepdims=True)
    return off * lax.rsqrt(spread + 1e-05) * gain


def dot(left, right):
    return jnp.dot(left, right, preferred_element_type=F32)


def kernel(
    grid_h, pw_h, one_h, two_h, up_h, down_h, tab_h,
    g1_ref, bias_ref, g2_ref, sel_ref, fw_ref, bw_ref, fh_ref, bh_ref,
    out_ref,
    grid_v, pw_v, one_v, two_v, up_v, down_v, tab_v,
    t_v, m_v, lhs_v, q0_v, q3_v, tot_v, acc_v, nf_v, tn_v, nrm_v,
    ew_s, ew_r, ns_s, ns_r,
    p1_s, p1_r, p2_s, p2_r, p3_s, p3_r, p4_s, p4_r,
    z_v, v_v, w1_v, w2_v, h0_v, h1_v,
    lsem, halo_ss, halo_rs, s1, r1, s2, r2, s3, r3, s4, r4,
):
    a = lax.axis_index("lat")
    b = lax.axis_index("lon")
    q = b // 16
    p = b % 16
    row_y = p // 4
    row_z = p % 4
    mine = (row_y + row_z) % 2
    n = 2 * row_y + row_z // 2
    g = 2 * a + q
    ways = [(da, db) for da in (1, 3) for db in (1, NLON - 1)]

    def load(index, src, dst):
        copy = pltpu.make_async_copy(src, dst, lsem.at[index])
        copy.start()
        return copy

    c_grid = load(0, grid_h, grid_v)
    c_tab = load(1, tab_h, tab_v)
    c_pw = {}
    for i, off in enumerate((1, 2, 0, 3)):
        part = pl.ds(1280 * off, 1280)
        c_pw[off] = load(2 + i, pw_h.at[part], pw_v.at[part])
    c_one = load(6, one_h.at[:, n], one_v)
    c_two = load(7, two_h.at[:, n], two_v)

    barrier = pltpu.get_barrier_semaphore()

    def greet_lon(d, _):
        pl.semaphore_signal(
            barrier, inc=1, device_id=(a, lax.rem(b + d, NLON)), device_id_type=MESH
        )
        return 0

    lax.fori_loop(1, NLON, greet_lon, 0)

    def greet_lat(d, _):
        mate = lax.rem(a + 1 + d // 2, NLAT)
        pl.semaphore_signal(
            barrier, inc=1, device_id=(mate, (d % 2) * 16 + p), device_id_type=MESH
        )
        return 0

    lax.fori_loop(0, 6, greet_lat, 0)
    for da, db in ways:
        corner = (lax.rem(a + da, NLAT), lax.rem(b + db, NLON))
        pl.semaphore_signal(barrier, inc=1, device_id=corner, device_id_type=MESH)

    nf_v[:, :, 144:] = jnp.zeros((6, 2, 48, 128), F32)
    for slots in (slice(0, 2), slice(8, 10)):
        m_v[:, :, :, slots] = jnp.zeros((2, 6, 2, 2, ROWS, 128), F32)
    for tile in range(6):
        q0_v[tile, pl.ds(0, 16, stride=32), :] = jnp.zeros((16, 128), F32)
        q3_v[tile, pl.ds(31, 16, stride=32), :] = jnp.zeros((16, 128), F32)
    c_grid.wait()
    for smp in range(2):
        for lp in range(3):
            block = grid_v[smp, :, 16 * lp : 16 * lp + 16, :]
            block = block.astype(F32).reshape(NV, 2, 8, 192)
            for half in range(2):
                x = block[:, half].reshape(NV * 8, 192).astype(BF16)
                turned = lax.dot_general(
                    sel_ref[...], x, (((1,), (1,)), ((), ())), preferred_element_type=F32
                )
                first = (6 * smp + 2 * lp + half) * ROWS
                for r8 in range(8):
                    t_v[r8, first : first + ROWS, :] = turned[ROWS * r8 : ROWS * r8 + ROWS]

    c_tab.wait()
    for half in range(2):
        value = dot(t_v[4 * half].astype(BF16), tab_v[0])
        for r in range(1, 4):
            value = value + dot(t_v[4 * half + r].astype(BF16), tab_v[r])
        for tile in range(6):
            part = value[:, 128 * tile : 128 * tile + 128].reshape(2, COLS, ROWS, 128)
            for smp in range(2):
                m_v[half, tile, smp, 2 : 2 + COLS] = part[smp]

    for half in range(2):
        for tile in range(10):
            lane, slot = (
                (3, 0), (4, 0), (5, 0), (1, 1), (2, 1), (3, 1), (4, 1), (5, 1), (1, 2), (2, 2)
            )[tile]
            for smp in range(2):
                value = m_v[half, lane, smp, slot : slot + 8]
                if tile in (2, 7):
                    value = value + m_v[half, 0, smp, slot + 1 : slot + 9]
                lhs_v[half, 192 * smp : 192 * smp + 192, 128 * tile : 128 * tile + 128] = (
                    value.reshape(192, 128).astype(BF16)
                )

    def weight(off, pair):
        return pw_v[1280 * off : 1280 * off + 1280, 256 * pair : 256 * pair + 256]

    c_pw[1].wait()
    c_pw[2].wait()
    for pair in range(3):
        value = dot(lhs_v[0], weight(1, pair)) + dot(lhs_v[1], weight(2, pair))
        tot_v[2 * pair] = value[:, :128]
        tot_v[2 * pair + 1] = value[:, 128:]
    for off, half, out_v, lead in ((0, 1, q0_v, 1), (3, 0, q3_v, 7)):
        c_pw[off].wait()
        for pair in range(3):
            value = dot(lhs_v[half], weight(off, pair))
            for lane in range(2):
                lanes = slice(128 * lane, 128 * lane + 128)
                for m in range(16):
                    out_v[2 * pair + lane, 32 * m + lead : 32 * m + lead + ROWS, :] = value[
                        ROWS * m : ROWS * m + ROWS, lanes
                    ]
    c_up = load(8, up_h, up_v)
    c_down = load(9, down_h, down_v)
    for tile in range(6):
        shifted = q0_v[tile].reshape(16, 32, 128)[:, :ROWS] + q3_v[tile].reshape(16, 32, 128)[:, 8:]
        tot_v[tile] += shifted.reshape(384, 128)

    for tile in range(6):
        cols = slice(128 * tile, 128 * tile + 128)
        for smp in range(2):
            for way, slot in ((0, 7), (1, 0)):
                first = ROWS * (8 * smp + slot)
                ew_s[way, smp, :, cols] = tot_v[tile, first : first + ROWS, :].astype(BF16)
        ns_s[0, :, cols] = q0_v[tile, pl.ds(ROWS, 16, stride=32), :].astype(BF16)
        ns_s[1, :, cols] = q3_v[tile, pl.ds(7, 16, stride=32), :].astype(BF16)

    pl.semaphore_wait(barrier, NLON - 1 + 6 + 4)

    def remote(src, dst, ssem, rsem, dev):
        return pltpu.make_async_remote_copy(
            src_ref=src, dst_ref=dst, send_sem=ssem, recv_sem=rsem,
            device_id=dev, device_id_type=MESH,
        )

    halos = []
    for src, da in ((0, 1), (1, 3)):
        for side, db in enumerate((0, 1, NLON - 1)):
            slot = 3 * src + side
            halos.append((ns_s.at[src], ns_r.at[slot], 2 + slot, da, db))
    for src, db in ((0, 1), (1, NLON - 1)):
        halos.append((ew_s.at[src], ew_r.at[src], src, 0, db))
    halos = [
        remote(
            src, dst, halo_ss.at[sem], halo_rs.at[sem],
            (lax.rem(a + da, NLAT), lax.rem(b + db, NLON)),
        )
        for src, dst, sem, da, db in halos
    ]
    for copy in halos:
        copy.start()
    for copy in halos:
        copy.wait_recv()

    slot_ids = lax.broadcasted_iota(jnp.int32, (2, 8, 128), 1)

    def edge_row(first, cols):
        straight, west, east = [
            ns_r[first + k, :, cols].astype(F32).reshape(2, 8, 128) for k in range(3)
        ]
        west = jnp.concatenate([west[:, 6:], west[:, :6]], axis=1)
        east = jnp.concatenate([east[:, 2:], east[:, :2]], axis=1)
        straight = straight + jnp.where(slot_ids == 1, west, 0.0)
        return (straight + jnp.where(slot_ids == 6, east, 0.0)).reshape(16, 128)

    for tile in range(6):
        cols = slice(128 * tile, 128 * tile + 128)
        for smp in range(2):
            for way, slot in ((0, 1), (1, 6)):
                first = ROWS * (8 * smp + slot)
                tot_v[tile, first : first + ROWS, :] += ew_r[way, smp, :, cols].astype(F32)
        top, bottom = pl.ds(0, 16, stride=ROWS), pl.ds(ROWS - 1, 16, stride=ROWS)
        tot_v[tile, top, :] += jnp.where(a > 0, edge_row(0, cols), 0.0)
        tot_v[tile, bottom, :] += jnp.where(a < NLAT - 1, edge_row(3, cols), 0.0)

    def owner(part, smp, blk):
        return part * 16 + (blk // 2) * 4 + (blk % 2) * 2 + (smp + blk // 2) % 2

    for smp in range(2):
        rows = slice(144 * smp, 144 * smp + 144)
        first = ROWS * (8 * smp + 1)
        tok = jnp.concatenate([tot_v[t, first : first + 144, :] for t in range(6)], axis=1)
        tok = tok.astype(BF16).astype(F32)
        normed = norm(tok, g1_ref[...].reshape(1, C)).astype(BF16).astype(F32)
        tn_v[rows, :] = tok + normed
        for tile in range(6):
            nf_v[tile, smp, :144] = normed[:, 128 * tile : 128 * tile + 128]
        for part in range(2):
            planes = [
                jnp.concatenate(
                    [nf_v[t, smp, pl.ds(part * ROW12 + i, 8, stride=ROWS), :] for t in range(6)],
                    axis=1,
                )
                for i in range(ROW12)
            ]
            for blk in range(NB):
                msg = jnp.concatenate(
                    [plane[:, BS * blk : BS * blk + BS] for plane in planes], axis=1
                )
                p1_s[owner(part, smp, blk)] = msg.astype(BF16)
        odd = (smp + mine) % 2
        for dx in (1, 0):
            for dy in (2, 1, 3, 0):
                for dz in (2, 0):
                    dest = (
                        ((q + dx) % 2) * 16 + ((row_y + dy) % 4) * 4 + (row_z + dz + (odd + dy) % 2) % 4
                    )

                    def send(dest=dest):
                        remote(
                            p1_s.at[dest], p1_r.at[b], s1.at[dest], r1.at[b], (a, dest)
                        ).start()

                    if (dx, dy, dz) == (0, 0, 0):
                        pl.when(odd == 1)(send)
                    else:
                        send()
    p1_r[b] = p1_s[b]

    c_one.wait()
    c_two.wait()
    for src, dst in ((one_v, w1_v), (two_v, w2_v)):
        dst[...] = jnp.zeros_like(dst)
        dst[0:BS, 0:BS] = src[0].astype(BF16)
        dst[0:BS, 128 : 128 + BS] = src[1].astype(BF16)
        dst[128 : 128 + BS, 0:BS] = -src[1].astype(BF16)
        dst[128 : 128 + BS, 128 : 128 + BS] = src[0].astype(BF16)
    bias = jnp.zeros((1, 256), F32)
    for blk in range(NB):
        parts = []
        for ri in range(2):
            parts.append(bias_ref[ri : ri + 1, BS * blk : BS * blk + BS])
            parts.append(jnp.zeros((1, 32), F32))
        bias = bias + jnp.where(n == blk, jnp.concatenate(parts, axis=1), 0.0)

    def wait1(d, _):
        src = lax.rem(b + d, NLON)
        remote(p1_s.at[src], p1_r.at[src], s1.at[src], r1.at[src], (a, src)).wait_recv()
        return 0

    lax.fori_loop(1, NLON, wait1, 0)

    def mate_of(d):
        other = lax.rem(g + d, 8)
        return other, (other // 2, (other % 2) * 16 + p)

    x = p1_r[...].astype(F32).reshape(256, MSG).astype(BF16)
    for kh in range(2):
        part = dot(fw_ref[64 * kh : 64 * kh + 64, :], x)
        p2_s[kh] = part.reshape(8, 8, MSG).astype(BF16)
        for d in range(1, 8):
            other, dev = mate_of(d)
            remote(
                p2_s.at[kh, other], p2_r.at[kh, g], s2.at[kh, other], r2.at[kh, g], dev
            ).start()

    def spread(kh, src, value):
        for i in range(ROW12):
            piece = value[:, BS * i : BS * i + BS]
            piece = jnp.concatenate([piece, jnp.zeros((8, 128 - BS), F32)], axis=1)
            z_v[pl.ds(768 * kh + ROW12 * src + i, 8, stride=H), :] = piece

    def gather(kh, dest):
        pieces = [
            v_v[pl.ds(768 * kh + ROW12 * dest + i, 8, stride=H), :][:, :BS] for i in range(ROW12)
        ]
        return jnp.concatenate(pieces, axis=1).astype(BF16)

    for kh in range(2):
        spread(kh, g, p2_s[kh, g].astype(F32))

        def take2(d, _):
            other, dev = mate_of(d)
            remote(
                p2_s.at[kh, other], p2_r.at[kh, other], s2.at[kh, other], r2.at[kh, other], dev
            ).wait_recv()
            spread(kh, other, p2_r[kh, other].astype(F32))
            return 0

        lax.fori_loop(1, 8, take2, 0)

        for pair in (2 * kh, 2 * kh + 1):
            k0, k1 = 384 * pair, 384 * pair + 192
            z = jnp.concatenate([z_v[k0 : k0 + 192, :], z_v[k1 : k1 + 192, :]], axis=1)
            spec = dot(fh_ref[...], z.astype(BF16))
            modes = jnp.concatenate(
                [
                    jnp.concatenate([spec[:H, :128], spec[H:, :128]], axis=1),
                    jnp.concatenate([spec[:H, 128:], spec[H:, 128:]], axis=1),
                ],
                axis=0,
            )
            mid = jnp.maximum(dot(modes.astype(BF16), w1_v[...]) + bias, 0.0)
            res = dot(mid.astype(BF16), w2_v[...])
            res = res - jnp.clip(res, -0.01, 0.01)
            back = jnp.concatenate(
                [
                    jnp.concatenate([res[:H, :128], res[H:, :128]], axis=1),
                    jnp.concatenate([res[:H, 128:], res[H:, 128:]], axis=1),
                ],
                axis=0,
            )
            rows = dot(bh_ref[...], back.astype(BF16))
            v_v[k0 : k0 + 192, :] = rows[:, :128]
            v_v[k1 : k1 + 192, :] = rows[:, 128:]

        def send3(d, _):
            other, dev = mate_of(d)
            p3_s[kh, other] = gather(kh, other)
            remote(
                p3_s.at[kh, other], p3_r.at[kh, g], s3.at[kh, other], r3.at[kh, g], dev
            ).start()
            return 0

        lax.fori_loop(1, 8, send3, 0)
        p3_r[kh, g] = gather(kh, g)

    def wait3(d, _):
        other, dev = mate_of(d)
        for kh in range(2):
            remote(
                p3_s.at[kh, other], p3_r.at[kh, other], s3.at[kh, other], r3.at[kh, other], dev
            ).wait_recv()
        return 0

    lax.fori_loop(1, 8, wait3, 0)

    field = dot(bw_ref[...], p3_r[...].astype(F32).reshape(128, MSG).astype(BF16))
    p4_s[...] = field.reshape(NLON, 8, MSG).astype(BF16)
    steps = [(dx, dy, dz) for dx in range(2) for dy in range(4) for dz in range(4)]
    steps.sort(key=lambda t: -(t[0] + min(t[1], 4 - t[1]) + min(t[2], 4 - t[2])))
    for dx, dy, dz in steps[:-1]:
        dest = ((q + dx) % 2) * 16 + ((row_y + dy) % 4) * 4 + (row_z + dz) % 4
        remote(p4_s.at[dest], p4_r.at[b], s4.at[dest], r4.at[b], (a, dest)).start()
    p4_r[b] = p4_s[b]

    def wait4(d, _):
        src = lax.rem(b + d, NLON)
        remote(p4_s.at[src], p4_r.at[src], s4.at[src], r4.at[src], (a, src)).wait_recv()
        return 0

    lax.fori_loop(1, NLON, wait4, 0)

    for smp in range(2):

        def join(part, _):
            msgs = [p4_r[owner(part, smp, blk)].astype(F32) for blk in range(NB)]
            for i in range(ROW12):
                plane = jnp.concatenate([m[:, BS * i : BS * i + BS] for m in msgs], axis=1)
                for tile in range(6):
                    nf_v[tile, smp, pl.ds(part * ROW12 + i, 8, stride=ROWS), :] = plane[
                        :, 128 * tile : 128 * tile + 128
                    ]
            return 0

        lax.fori_loop(0, 2, join, 0)
        rows = slice(144 * smp, 144 * smp + 144)
        field = jnp.concatenate([nf_v[tile, smp, :144] for tile in range(6)], axis=1)
        middle = (field + tn_v[rows, :]).astype(BF16).astype(F32)
        acc_v[rows, :] = middle
        nrm_v[rows, :] = norm(middle, g2_ref[...].reshape(1, C)).astype(BF16)

    c_up.wait()
    c_down.wait()

    def up(step):
        return dot(nrm_v[...], up_v[:, pl.ds(pl.multiple_of(step * 256, 256), 256)])

    def down(hidden, step):
        hidden = 0.5 * hidden * (1.0 + lax.erf(hidden * (1.0 / math.sqrt(2.0))))
        rows = pl.ds(pl.multiple_of(step * 256, 256), 256)
        return dot(hidden.astype(BF16), down_v[rows, :])

    h0_v[...] = up(0)

    def mlp(it, _):
        step = 2 * it
        h1_v[...] = up(step + 1)
        acc_v[...] += down(h0_v[...], step)
        h0_v[...] = up(jnp.minimum(step + 2, HID // 256 - 1))
        acc_v[...] += down(h1_v[...], step + 1)
        return 0

    lax.fori_loop(0, HID // 512, mlp, 0)
    out_ref[...] = acc_v[...].reshape(2, COLS, ROWS, C).astype(BF16)

    for copy in halos:
        copy.wait_send()

    def drain_lon(d, _):
        dest = lax.rem(b + d, NLON)
        remote(p1_s.at[dest], p1_r.at[b], s1.at[dest], r1.at[b], (a, dest)).wait_send()
        remote(p4_s.at[dest], p4_r.at[b], s4.at[dest], r4.at[b], (a, dest)).wait_send()
        return 0

    lax.fori_loop(1, NLON, drain_lon, 0)

    def drain_lat(d, _):
        other, dev = mate_of(d)
        for kh in range(2):
            remote(
                p2_s.at[kh, other], p2_r.at[kh, g], s2.at[kh, other], r2.at[kh, g], dev
            ).wait_send()
            remote(
                p3_s.at[kh, other], p3_r.at[kh, g], s3.at[kh, other], r3.at[kh, g], dev
            ).wait_send()
        return 0

    lax.fori_loop(1, 8, drain_lat, 0)


def local(
    grid, patch_weight, norm_gain_one, spectral_one, spectral_bias, spectral_two,
    norm_gain_two, fc_up, fc_down,
):
    fw, bw = lon_tables()
    fh, bh = lat_tables()
    const = lambda x: jnp.asarray(x, F32).astype(BF16)
    any_spec = pl.BlockSpec(memory_space=pl.ANY)
    vmem = pl.BlockSpec(memory_space=pltpu.VMEM)
    dma = pltpu.SemaphoreType.DMA
    out = pl.pallas_call(
        kernel,
        out_shape=jax.ShapeDtypeStruct((2, COLS, ROWS, C), BF16),
        in_specs=[any_spec] * 7 + [vmem] * 8,
        out_specs=vmem,
        scratch_shapes=[
            pltpu.VMEM((2, NV, 48, 192), BF16),
            pltpu.VMEM((5120, C), BF16),
            pltpu.VMEM((2, BS, BS), F32),
            pltpu.VMEM((2, BS, BS), F32),
            pltpu.VMEM((C, HID), BF16),
            pltpu.VMEM((HID, C), BF16),
            pltpu.VMEM((4, 160, 768), BF16),
            pltpu.VMEM((8, 288, 160), F32),
            pltpu.VMEM((2, 6, 2, 10, ROWS, 128), F32),
            pltpu.VMEM((2, 384, 1280), BF16),
            pltpu.VMEM((6, 512, 128), F32),
            pltpu.VMEM((6, 512, 128), F32),
            pltpu.VMEM((6, 384, 128), F32),
            pltpu.VMEM((288, C), F32),
            pltpu.VMEM((6, 2, 192, 128), F32),
            pltpu.VMEM((288, C), F32),
            pltpu.VMEM((288, C), BF16),
            pltpu.VMEM((2, 2, ROWS, C), BF16),
            pltpu.VMEM((2, 2, ROWS, C), BF16),
            pltpu.VMEM((2, 16, C), BF16),
            pltpu.VMEM((6, 16, C), BF16),
            pltpu.VMEM((NLON, 8, MSG), BF16),
            pltpu.VMEM((NLON, 8, MSG), BF16),
            pltpu.VMEM((2, 8, 8, MSG), BF16),
            pltpu.VMEM((2, 8, 8, MSG), BF16),
            pltpu.VMEM((2, 8, 8, MSG), BF16),
            pltpu.VMEM((2, 8, 8, MSG), BF16),
            pltpu.VMEM((NLON, 8, MSG), BF16),
            pltpu.VMEM((NLON, 8, MSG), BF16),
            pltpu.VMEM((8 * 192, 128), F32),
            pltpu.VMEM((8 * 192, 128), F32),
            pltpu.VMEM((256, 256), BF16),
            pltpu.VMEM((256, 256), BF16),
            pltpu.VMEM((288, 256), F32),
            pltpu.VMEM((288, 256), F32),
            dma((10,)),
            dma((8,)),
            dma((8,)),
            dma((NLON,)),
            dma((NLON,)),
            dma((2, 8)),
            dma((2, 8)),
            dma((2, 8)),
            dma((2, 8)),
            dma((NLON,)),
            dma((NLON,)),
        ],
        compiler_params=pltpu.CompilerParams(
            collective_id=0, has_side_effects=True, vmem_limit_bytes=56 * 1024 * 1024
        ),
    )(
        grid.transpose(0, 1, 3, 2), patch_weight, spectral_one, spectral_two, fc_up, fc_down,
        const(feature_table()),
        norm_gain_one, spectral_bias, norm_gain_two,
        const(pick_table()), const(fw), const(bw), const(fh), const(bh),
    )
    return out.transpose(0, 2, 1, 3)


def solution(mesh):
    in_specs = (P(None, None, "lat", "lon"), P(), P(), P(), P(), P(), P(), P(), P())
    out_specs = P(None, "lat", "lon", None)
    return jax.shard_map(local, mesh=mesh, in_specs=in_specs, out_specs=out_specs, check_vma=False)
```

```python
import math

import jax
import jax.numpy as jnp
import numpy as np
from jax import lax
from jax.experimental import pallas as pl
from jax.experimental.pallas import tpu as pltpu
from jax.sharding import PartitionSpec as P

MESH = pl.DeviceIdType.MESH
F32 = jnp.float32
BF16 = jnp.bfloat16

NLAT, NLON = 4, 32
NV, C, HID, NB, BS = 20, 768, 3072, 8, 96
H, W, KW = 96, 192, 64
ROWS, COLS = 24, 6
ROW12 = 12
MSG = ROW12 * BS


def pick_table():
    sel = np.zeros((192, 192), np.float32)
    for r8 in range(8):
        for row in range(ROWS):
            sel[r8 * ROWS + row, 8 * row + r8] = 1.0
    return sel


def feature_table():
    table = np.zeros((4, 160, 768), np.float32)
    for r in range(4):
        for v in range(NV):
            for c8 in range(8):
                table[r, v * 8 + c8, (64, 384)[c8 // 4] + v * 16 + 4 * r + c8 % 4] = 1.0
    return table


def lon_tables():
    k = np.arange(KW)
    w = np.arange(W)
    angle = 2.0 * math.pi * ((k[:, None] * w[None, :]) % W) / W
    scale = 1.0 / math.sqrt(W)
    both = np.stack([np.cos(angle), -np.sin(angle)]) * scale
    fwd = both.reshape(2, 8, 2, 4, W).transpose(2, 1, 3, 0, 4).reshape(128, NLON, COLS)
    fwd = np.pad(fwd, ((0, 0), (0, 0), (0, 2))).reshape(128, 256)
    weight = np.where(k == 0, 1.0, 2.0)
    back = both * weight[None, :, None]
    back = back.reshape(2, 8, 2, 4, W).transpose(4, 2, 1, 3, 0).reshape(NLON, COLS, 128)
    back = np.pad(back, ((0, 0), (0, 2), (0, 0))).reshape(256, 128)
    return fwd, back


def lat_tables():
    h = np.arange(H)
    angle = 2.0 * math.pi * ((h[:, None] * h[None, :]) % H) / H
    cos, sin = np.cos(angle) / math.sqrt(H), np.sin(angle) / math.sqrt(H)
    fwd = np.block([[cos, sin], [-sin, cos]])
    back = np.block([[cos, -sin], [sin, cos]])
    return fwd, back


def norm(values, gain):
    centre = jnp.mean(values, axis=-1, keepdims=True)
    off = values - centre
    spread = jnp.mean(jnp.square(off), axis=-1, keepdims=True)
    return off * lax.rsqrt(spread + 1e-05) * gain


def fold(msg):
    row = lax.broadcasted_iota(jnp.int32, msg.shape[:-1] + (128,), msg.ndim - 2)
    tiles = []
    for u in range(7):
        tile = msg[..., 128 * u : 128 * u + 128]
        if u < COLS:
            tile = jnp.where(row == 6, msg[..., u : u + 1, 896:1024], tile)
            tile = jnp.where(row == 7, msg[..., u : u + 1, 1024:], tile)
        tiles.append(tile)
    return jnp.concatenate(tiles, axis=-1)


def unfold(msg):
    row = lax.broadcasted_iota(jnp.int32, msg.shape[:-1] + (128,), msg.ndim - 2)
    last = [jnp.zeros(row.shape, F32)] * 2
    for u in range(COLS):
        for i in range(2):
            piece = msg[..., 6 + i : 7 + i, 128 * u : 128 * u + 128]
            last[i] = jnp.where(row == u, piece, last[i])
    return jnp.concatenate([msg] + last, axis=-1)


def dot(left, right):
    return jnp.dot(left, right, preferred_element_type=F32)


def kernel(
    grid_h, pw_h, one_h, two_h, up_h, down_h, tab_h, sq_h, fw_h, bw_h, g1_h, bias_h, g2_h,
    out_ref,
    sq_v, fw_ref, bw_ref, g1_ref, bias_ref, g2_ref,
    grid_v, pw_v, one_v, two_v, up_v, down_v, tab_v,
    t_v, m_v, lhs_v, q0_v, q3_v, tot_v, acc_v, nf_v, tn_v, nrm_v,
    ew_s, ew_r, ns_s, ns_r,
    p1_s, p1_r, p2_s, p2_r, p3_s, p3_r, p4_s, p4_r,
    z_v, v_v, w1_v, w2_v, h0_v, h1_v,
    lsem, halo_ss, halo_rs, s1, r1, s2, r2, s3, r3, s4, r4,
):
    a = lax.axis_index("lat")
    b = lax.axis_index("lon")
    q = b // 16
    p = b % 16
    row_y = p // 4
    row_z = p % 4
    mine = (row_y + row_z) % 2
    n = 2 * row_y + row_z // 2
    g = 2 * a + q

    barrier = pltpu.get_barrier_semaphore()

    def greet_lon(d, _):
        pl.semaphore_signal(
            barrier, inc=1, device_id=(a, lax.rem(b + d, NLON)), device_id_type=MESH
        )
        return 0

    lax.fori_loop(1, NLON, greet_lon, 0)

    def greet_lat(d, _):
        mate = lax.rem(a + 1 + d // 2, NLAT)
        pl.semaphore_signal(
            barrier, inc=1, device_id=(mate, (d % 2) * 16 + p), device_id_type=MESH
        )
        return 0

    lax.fori_loop(0, 6, greet_lat, 0)
    def load(index, src, dst):
        copy = pltpu.make_async_copy(src, dst, lsem.at[index])
        copy.start()
        return copy

    c_grid = load(0, grid_h, grid_v)
    c_sq = load(10, sq_h, sq_v)
    c_tab = load(1, tab_h, tab_v)
    c_pw = {}
    for i, off in enumerate((0, 3, 1, 2)):
        part = pl.ds(1280 * off, 1280)
        c_pw[off] = load(2 + i, pw_h.at[part], pw_v.at[part])
    c_one = load(6, one_h.at[:, n], one_v)
    c_two = load(7, two_h.at[:, n], two_v)
    small = [
        load(11 + i, src, dst)
        for i, (src, dst) in enumerate(
            ((g1_h, g1_ref), (bias_h, bias_ref), (g2_h, g2_ref), (fw_h, fw_ref), (bw_h, bw_ref))
        )
    ]

    nf_v[:, :, 144:] = jnp.zeros((6, 2, 48, 128), F32)
    for slots in (slice(0, 2), slice(8, 10)):
        m_v[:, :, :, slots] = jnp.zeros((2, 6, 2, 2, ROWS, 128), F32)
    for tile in range(6):
        q0_v[tile, pl.ds(0, 16, stride=32), :] = jnp.zeros((16, 128), F32)
        q3_v[tile, pl.ds(31, 16, stride=32), :] = jnp.zeros((16, 128), F32)
    c_grid.wait()
    c_sq.wait()
    for smp in range(2):
        for lp in range(3):
            block = grid_v[smp, :, 16 * lp : 16 * lp + 16, :]
            block = block.astype(F32).reshape(NV, 2, 8, 192)
            for half in range(2):
                x = block[:, half].reshape(NV * 8, 192).astype(BF16)
                turned = lax.dot_general(
                    sq_v[0], x, (((1,), (1,)), ((), ())), preferred_element_type=F32
                )
                first = (6 * smp + 2 * lp + half) * ROWS
                for r8 in range(8):
                    t_v[r8, first : first + ROWS, :] = turned[ROWS * r8 : ROWS * r8 + ROWS]

    c_tab.wait()
    for half in range(2):
        value = dot(t_v[4 * half].astype(BF16), tab_v[0])
        for r in range(1, 4):
            value = value + dot(t_v[4 * half + r].astype(BF16), tab_v[r])
        for tile in range(6):
            part = value[:, 128 * tile : 128 * tile + 128].reshape(2, COLS, ROWS, 128)
            for smp in range(2):
                m_v[half, tile, smp, 2 : 2 + COLS] = part[smp]

    for half in range(2):
        for tile in range(10):
            lane, slot = (
                (3, 0), (4, 0), (5, 0), (1, 1), (2, 1), (3, 1), (4, 1), (5, 1), (1, 2), (2, 2)
            )[tile]
            for smp in range(2):
                value = m_v[half, lane, smp, slot : slot + 8]
                if tile in (2, 7):
                    value = value + m_v[half, 0, smp, slot + 1 : slot + 9]
                lhs_v[half, 192 * smp : 192 * smp + 192, 128 * tile : 128 * tile + 128] = (
                    value.reshape(192, 128).astype(BF16)
                )

    def weight(off, pair):
        return pw_v[1280 * off : 1280 * off + 1280, 256 * pair : 256 * pair + 256]

    for off, half, out_v, lead in ((0, 1, q0_v, 1), (3, 0, q3_v, 7)):
        c_pw[off].wait()
        for pair in range(3):
            value = dot(lhs_v[half], weight(off, pair))
            for lane in range(2):
                lanes = slice(128 * lane, 128 * lane + 128)
                for m in range(16):
                    out_v[2 * pair + lane, 32 * m + lead : 32 * m + lead + ROWS, :] = value[
                        ROWS * m : ROWS * m + ROWS, lanes
                    ]
    for tile in range(6):
        cols = slice(128 * tile, 128 * tile + 128)
        ns_s[0, :, cols] = q0_v[tile, pl.ds(ROWS, 16, stride=32), :].astype(BF16)
        ns_s[1, :, cols] = q3_v[tile, pl.ds(7, 16, stride=32), :].astype(BF16)

    pl.semaphore_wait(barrier, NLON - 1 + 6)

    def remote(src, dst, ssem, rsem, dev):
        return pltpu.make_async_remote_copy(
            src_ref=src, dst_ref=dst, send_sem=ssem, recv_sem=rsem,
            device_id=dev, device_id_type=MESH,
        )

    halos = [
        remote(
            src.at[i], dst.at[i], halo_ss.at[sem + i], halo_rs.at[sem + i],
            (lax.rem(a + da, NLAT), lax.rem(b + db, NLON)),
        )
        for src, dst, sem, ways in (
            (ns_s, ns_r, 0, ((1, 0), (NLAT - 1, 0))),
            (ew_s, ew_r, 2, ((0, 1), (0, NLON - 1))),
        )
        for i, (da, db) in enumerate(ways)
    ]
    halos[0].start()
    halos[1].start()

    c_pw[1].wait()
    c_pw[2].wait()
    for pair in range(3):
        value = dot(lhs_v[0], weight(1, pair)) + dot(lhs_v[1], weight(2, pair))
        for lane in range(2):
            tile = 2 * pair + lane
            shifted = (
                q0_v[tile].reshape(16, 32, 128)[:, :ROWS] + q3_v[tile].reshape(16, 32, 128)[:, 8:]
            )
            tot_v[tile] = value[:, 128 * lane : 128 * lane + 128] + shifted.reshape(384, 128)
    c_up = load(8, up_h, up_v)
    c_down = load(9, down_h, down_v)

    halos[0].wait_recv()
    halos[1].wait_recv()
    for tile in range(6):
        cols = slice(128 * tile, 128 * tile + 128)
        top, bottom = pl.ds(0, 16, stride=ROWS), pl.ds(ROWS - 1, 16, stride=ROWS)
        tot_v[tile, top, :] += jnp.where(a > 0, ns_r[0, :, cols].astype(F32), 0.0)
        tot_v[tile, bottom, :] += jnp.where(a < NLAT - 1, ns_r[1, :, cols].astype(F32), 0.0)
        for smp in range(2):
            for way, slot in ((0, 7), (1, 0)):
                first = ROWS * (8 * smp + slot)
                ew_s[way, smp, :, cols] = tot_v[tile, first : first + ROWS, :].astype(BF16)
    halos[2].start()
    halos[3].start()
    halos[2].wait_recv()
    halos[3].wait_recv()
    for tile in range(6):
        cols = slice(128 * tile, 128 * tile + 128)
        for smp in range(2):
            for way, slot in ((0, 1), (1, 6)):
                first = ROWS * (8 * smp + slot)
                tot_v[tile, first : first + ROWS, :] += ew_r[way, smp, :, cols].astype(F32)
    for copy in small:
        copy.wait()

    def owner(part, smp, blk):
        return part * 16 + (blk // 2) * 4 + (blk % 2) * 2 + (smp + blk // 2) % 2

    for smp in range(2):
        rows = slice(144 * smp, 144 * smp + 144)
        first = ROWS * (8 * smp + 1)
        tok = jnp.concatenate([tot_v[t, first : first + 144, :] for t in range(6)], axis=1)
        tok = tok.astype(BF16).astype(F32)
        normed = norm(tok, g1_ref[...].reshape(1, C)).astype(BF16).astype(F32)
        tn_v[rows, :] = tok + normed
        for tile in range(6):
            nf_v[tile, smp, :144] = normed[:, 128 * tile : 128 * tile + 128]
        for part in range(2):
            planes = [
                jnp.concatenate(
                    [nf_v[t, smp, pl.ds(part * ROW12 + i, 8, stride=ROWS), :] for t in range(6)],
                    axis=1,
                )
                for i in range(ROW12)
            ]
            for blk in range(NB):
                msg = jnp.concatenate(
                    [plane[:, BS * blk : BS * blk + BS] for plane in planes], axis=1
                )
                p1_s[owner(part, smp, blk)] = fold(msg).astype(BF16)
        odd = (smp + mine) % 2
        for dx in (1, 0):
            for dy in (2, 1, 3, 0):
                for dz in (2, 0):
                    dest = (
                        ((q + dx) % 2) * 16 + ((row_y + dy) % 4) * 4 + (row_z + dz + (odd + dy) % 2) % 4
                    )

                    def send(dest=dest):
                        remote(
                            p1_s.at[dest], p1_r.at[b], s1.at[dest], r1.at[b], (a, dest)
                        ).start()

                    if (dx, dy, dz) == (0, 0, 0):
                        pl.when(odd == 1)(send)
                    else:
                        send()
    p1_r[b] = p1_s[b]

    c_one.wait()
    c_two.wait()
    for src, dst in ((one_v, w1_v), (two_v, w2_v)):
        dst[...] = jnp.zeros_like(dst)
        dst[0:BS, 0:BS] = src[0].astype(BF16)
        dst[0:BS, 128 : 128 + BS] = src[1].astype(BF16)
        dst[128 : 128 + BS, 0:BS] = -src[1].astype(BF16)
        dst[128 : 128 + BS, 128 : 128 + BS] = src[0].astype(BF16)
    bias = jnp.zeros((1, 256), F32)
    for blk in range(NB):
        parts = []
        for ri in range(2):
            parts.append(bias_ref[ri : ri + 1, BS * blk : BS * blk + BS])
            parts.append(jnp.zeros((1, 32), F32))
        bias = bias + jnp.where(n == blk, jnp.concatenate(parts, axis=1), 0.0)

    def wait1(d, _):
        src = lax.rem(b + d, NLON)
        remote(p1_s.at[src], p1_r.at[src], s1.at[src], r1.at[src], (a, src)).wait_recv()
        return 0

    lax.fori_loop(1, NLON, wait1, 0)

    def mate_of(d):
        other = lax.rem(g + d, 8)
        return other, (other // 2, (other % 2) * 16 + p)

    x = unfold(p1_r[...].astype(F32)).reshape(256, MSG).astype(BF16)
    for kh in range(2):
        part = dot(fw_ref[64 * kh : 64 * kh + 64, :], x)
        p2_s[kh] = part.reshape(8, 8, MSG).astype(BF16)
        for d in range(1, 8):
            other, dev = mate_of(d)
            remote(
                p2_s.at[kh, other], p2_r.at[kh, g], s2.at[kh, other], r2.at[kh, g], dev
            ).start()

    def spread(kh, src, value):
        for i in range(ROW12):
            piece = value[:, BS * i : BS * i + BS]
            piece = jnp.concatenate([piece, jnp.zeros((8, 128 - BS), F32)], axis=1)
            z_v[pl.ds(768 * kh + ROW12 * src + i, 8, stride=H), :] = piece

    def gather(kh, dest):
        pieces = [
            v_v[pl.ds(768 * kh + ROW12 * dest + i, 8, stride=H), :][:, :BS] for i in range(ROW12)
        ]
        return jnp.concatenate(pieces, axis=1).astype(BF16)

    for kh in range(2):
        spread(kh, g, p2_s[kh, g].astype(F32))

        def take2(d, _):
            other, dev = mate_of(d)
            remote(
                p2_s.at[kh, other], p2_r.at[kh, other], s2.at[kh, other], r2.at[kh, other], dev
            ).wait_recv()
            spread(kh, other, p2_r[kh, other].astype(F32))
            return 0

        lax.fori_loop(1, 8, take2, 0)

        for pair in (2 * kh, 2 * kh + 1):
            k0, k1 = 384 * pair, 384 * pair + 192
            z = jnp.concatenate([z_v[k0 : k0 + 192, :], z_v[k1 : k1 + 192, :]], axis=1)
            spec = dot(sq_v[1], z.astype(BF16))
            modes = jnp.concatenate(
                [
                    jnp.concatenate([spec[:H, :128], spec[H:, :128]], axis=1),
                    jnp.concatenate([spec[:H, 128:], spec[H:, 128:]], axis=1),
                ],
                axis=0,
            )
            mid = jnp.maximum(dot(modes.astype(BF16), w1_v[...]) + bias, 0.0)
            res = dot(mid.astype(BF16), w2_v[...])
            res = res - jnp.clip(res, -0.01, 0.01)
            back = jnp.concatenate(
                [
                    jnp.concatenate([res[:H, :128], res[H:, :128]], axis=1),
                    jnp.concatenate([res[:H, 128:], res[H:, 128:]], axis=1),
                ],
                axis=0,
            )
            rows = dot(sq_v[2], back.astype(BF16))
            v_v[k0 : k0 + 192, :] = rows[:, :128]
            v_v[k1 : k1 + 192, :] = rows[:, 128:]

        def send3(d, _):
            other, dev = mate_of(d)
            p3_s[kh, other] = gather(kh, other)
            remote(
                p3_s.at[kh, other], p3_r.at[kh, g], s3.at[kh, other], r3.at[kh, g], dev
            ).start()
            return 0

        lax.fori_loop(1, 8, send3, 0)
        p3_r[kh, g] = gather(kh, g)

    def wait3(d, _):
        other, dev = mate_of(d)
        for kh in range(2):
            remote(
                p3_s.at[kh, other], p3_r.at[kh, other], s3.at[kh, other], r3.at[kh, other], dev
            ).wait_recv()
        return 0

    lax.fori_loop(1, 8, wait3, 0)

    field = dot(bw_ref[...], p3_r[...].astype(F32).reshape(128, MSG).astype(BF16))
    p4_s[...] = fold(field.reshape(NLON, 8, MSG)).astype(BF16)
    steps = [(dx, dy, dz) for dx in range(2) for dy in range(4) for dz in range(4)]
    steps.sort(key=lambda t: -(t[0] + min(t[1], 4 - t[1]) + min(t[2], 4 - t[2])))
    for dx, dy, dz in steps[:-1]:
        dest = ((q + dx) % 2) * 16 + ((row_y + dy) % 4) * 4 + (row_z + dz) % 4
        remote(p4_s.at[dest], p4_r.at[b], s4.at[dest], r4.at[b], (a, dest)).start()
    p4_r[b] = p4_s[b]

    def wait4(d, _):
        src = lax.rem(b + d, NLON)
        remote(p4_s.at[src], p4_r.at[src], s4.at[src], r4.at[src], (a, src)).wait_recv()
        return 0

    lax.fori_loop(1, NLON, wait4, 0)

    for smp in range(2):

        def join(part, _):
            msgs = [unfold(p4_r[owner(part, smp, blk)].astype(F32)) for blk in range(NB)]
            for i in range(ROW12):
                plane = jnp.concatenate([m[:, BS * i : BS * i + BS] for m in msgs], axis=1)
                for tile in range(6):
                    nf_v[tile, smp, pl.ds(part * ROW12 + i, 8, stride=ROWS), :] = plane[
                        :, 128 * tile : 128 * tile + 128
                    ]
            return 0

        lax.fori_loop(0, 2, join, 0)
        rows = slice(144 * smp, 144 * smp + 144)
        field = jnp.concatenate([nf_v[tile, smp, :144] for tile in range(6)], axis=1)
        middle = (field + tn_v[rows, :]).astype(BF16).astype(F32)
        acc_v[rows, :] = middle
        nrm_v[rows, :] = norm(middle, g2_ref[...].reshape(1, C)).astype(BF16)

    c_up.wait()
    c_down.wait()

    def up(step):
        return dot(nrm_v[...], up_v[:, pl.ds(pl.multiple_of(step * 256, 256), 256)])

    def down(hidden, step):
        hidden = 0.5 * hidden * (1.0 + lax.erf(hidden * (1.0 / math.sqrt(2.0))))
        rows = pl.ds(pl.multiple_of(step * 256, 256), 256)
        return dot(hidden.astype(BF16), down_v[rows, :])

    h0_v[...] = up(0)

    def mlp(it, _):
        step = 2 * it
        h1_v[...] = up(step + 1)
        acc_v[...] += down(h0_v[...], step)
        h0_v[...] = up(jnp.minimum(step + 2, HID // 256 - 1))
        acc_v[...] += down(h1_v[...], step + 1)
        return 0

    lax.fori_loop(0, HID // 512, mlp, 0)
    out_ref[...] = acc_v[...].reshape(2, COLS, ROWS, C).astype(BF16)

    for copy in halos:
        copy.wait_send()

    def drain_lon(d, _):
        dest = lax.rem(b + d, NLON)
        remote(p1_s.at[dest], p1_r.at[b], s1.at[dest], r1.at[b], (a, dest)).wait_send()
        remote(p4_s.at[dest], p4_r.at[b], s4.at[dest], r4.at[b], (a, dest)).wait_send()
        return 0

    lax.fori_loop(1, NLON, drain_lon, 0)

    def drain_lat(d, _):
        other, dev = mate_of(d)
        for kh in range(2):
            remote(
                p2_s.at[kh, other], p2_r.at[kh, g], s2.at[kh, other], r2.at[kh, g], dev
            ).wait_send()
            remote(
                p3_s.at[kh, other], p3_r.at[kh, g], s3.at[kh, other], r3.at[kh, g], dev
            ).wait_send()
        return 0

    lax.fori_loop(1, 8, drain_lat, 0)


def local(
    grid, patch_weight, norm_gain_one, spectral_one, spectral_bias, spectral_two,
    norm_gain_two, fc_up, fc_down,
):
    fw, bw = lon_tables()
    fh, bh = lat_tables()
    const = lambda x: jnp.asarray(x, F32).astype(BF16)
    any_spec = pl.BlockSpec(memory_space=pl.ANY)
    vmem = pl.BlockSpec(memory_space=pltpu.VMEM)
    dma = pltpu.SemaphoreType.DMA
    out = pl.pallas_call(
        kernel,
        out_shape=jax.ShapeDtypeStruct((2, COLS, ROWS, C), BF16),
        in_specs=[any_spec] * 13,
        out_specs=vmem,
        scratch_shapes=[
            pltpu.VMEM((3, 192, 192), BF16),
            pltpu.VMEM((128, 256), BF16),
            pltpu.VMEM((256, 128), BF16),
            pltpu.VMEM((C,), F32),
            pltpu.VMEM((2, C), F32),
            pltpu.VMEM((C,), F32),
            pltpu.VMEM((2, NV, 48, 192), BF16),
            pltpu.VMEM((5120, C), BF16),
            pltpu.VMEM((2, BS, BS), F32),
            pltpu.VMEM((2, BS, BS), F32),
            pltpu.VMEM((C, HID), BF16),
            pltpu.VMEM((HID, C), BF16),
            pltpu.VMEM((4, 160, 768), BF16),
            pltpu.VMEM((8, 288, 160), F32),
            pltpu.VMEM((2, 6, 2, 10, ROWS, 128), F32),
            pltpu.VMEM((2, 384, 1280), BF16),
            pltpu.VMEM((6, 512, 128), F32),
            pltpu.VMEM((6, 512, 128), F32),
            pltpu.VMEM((6, 384, 128), F32),
            pltpu.VMEM((288, C), F32),
            pltpu.VMEM((6, 2, 192, 128), F32),
            pltpu.VMEM((288, C), F32),
            pltpu.VMEM((288, C), BF16),
            pltpu.VMEM((2, 2, ROWS, C), BF16),
            pltpu.VMEM((2, 2, ROWS, C), BF16),
            pltpu.VMEM((2, 16, C), BF16),
            pltpu.VMEM((2, 16, C), BF16),
            pltpu.VMEM((NLON, 8, 896), BF16),
            pltpu.VMEM((NLON, 8, 896), BF16),
            pltpu.VMEM((2, 8, 8, MSG), BF16),
            pltpu.VMEM((2, 8, 8, MSG), BF16),
            pltpu.VMEM((2, 8, 8, MSG), BF16),
            pltpu.VMEM((2, 8, 8, MSG), BF16),
            pltpu.VMEM((NLON, 8, 896), BF16),
            pltpu.VMEM((NLON, 8, 896), BF16),
            pltpu.VMEM((8 * 192, 128), F32),
            pltpu.VMEM((8 * 192, 128), F32),
            pltpu.VMEM((256, 256), BF16),
            pltpu.VMEM((256, 256), BF16),
            pltpu.VMEM((288, 256), F32),
            pltpu.VMEM((288, 256), F32),
            dma((16,)),
            dma((4,)),
            dma((4,)),
            dma((NLON,)),
            dma((NLON,)),
            dma((2, 8)),
            dma((2, 8)),
            dma((2, 8)),
            dma((2, 8)),
            dma((NLON,)),
            dma((NLON,)),
        ],
        compiler_params=pltpu.CompilerParams(
            collective_id=0, has_side_effects=True, vmem_limit_bytes=56 * 1024 * 1024
        ),
    )(
        grid.transpose(0, 1, 3, 2), patch_weight, spectral_one, spectral_two, fc_up, fc_down,
        const(feature_table()),
        const(np.stack([pick_table(), fh, bh])), const(fw), const(bw),
        norm_gain_one, spectral_bias, norm_gain_two,
    )
    return out.transpose(0, 2, 1, 3)


def solution(mesh):
    in_specs = (P(None, None, "lat", "lon"), P(), P(), P(), P(), P(), P(), P(), P())
    out_specs = P(None, "lat", "lon", None)
    return jax.shard_map(local, mesh=mesh, in_specs=in_specs, out_specs=out_specs, check_vma=False)
```

```python
import math

import jax
import jax.numpy as jnp
import numpy as np
from jax import lax
from jax.experimental import pallas as pl
from jax.experimental.pallas import tpu as pltpu
from jax.sharding import PartitionSpec as P

MESH = pl.DeviceIdType.MESH
F32 = jnp.float32
BF16 = jnp.bfloat16

NLAT, NLON = 4, 32
NV, C, HID, NB, BS = 20, 768, 3072, 8, 96
H, W, KW = 96, 192, 64
ROWS, COLS = 24, 6
ROW12 = 12
MSG = ROW12 * BS


def pick_table():
    sel = np.zeros((192, 192), np.float32)
    for r8 in range(8):
        for row in range(ROWS):
            sel[r8 * ROWS + row, 8 * row + r8] = 1.0
    return sel


def feature_table():
    table = np.zeros((4, 160, 768), np.float32)
    for r in range(4):
        for v in range(NV):
            for c8 in range(8):
                table[r, v * 8 + c8, (64, 384)[c8 // 4] + v * 16 + 4 * r + c8 % 4] = 1.0
    return table


def lon_tables():
    k = np.arange(KW)
    w = np.arange(W)
    angle = 2.0 * math.pi * ((k[:, None] * w[None, :]) % W) / W
    scale = 1.0 / math.sqrt(W)
    both = np.stack([np.cos(angle), -np.sin(angle)]) * scale
    fwd = both.reshape(2, 8, 2, 4, W).transpose(2, 1, 3, 0, 4).reshape(128, NLON, COLS)
    fwd = np.pad(fwd, ((0, 0), (0, 0), (0, 2))).reshape(128, 256)
    weight = np.where(k == 0, 1.0, 2.0)
    back = both * weight[None, :, None]
    back = back.reshape(2, 8, 2, 4, W).transpose(4, 2, 1, 3, 0).reshape(NLON, COLS, 128)
    back = np.pad(back, ((0, 0), (0, 2), (0, 0))).reshape(256, 128)
    return fwd, back


def lat_tables():
    h = np.arange(H)
    angle = 2.0 * math.pi * ((h[:, None] * h[None, :]) % H) / H
    cos, sin = np.cos(angle) / math.sqrt(H), np.sin(angle) / math.sqrt(H)
    fwd = np.block([[cos, sin], [-sin, cos]])
    back = np.block([[cos, -sin], [sin, cos]])
    return fwd, back


def norm(values, gain):
    centre = jnp.mean(values, axis=-1, keepdims=True)
    off = values - centre
    spread = jnp.mean(jnp.square(off), axis=-1, keepdims=True)
    return off * lax.rsqrt(spread + 1e-05) * gain


def fold(msg):
    row = lax.broadcasted_iota(jnp.int32, msg.shape[:-1] + (128,), msg.ndim - 2)
    tiles = []
    for u in range(7):
        tile = msg[..., 128 * u : 128 * u + 128]
        if u < COLS:
            tile = jnp.where(row == 6, msg[..., u : u + 1, 896:1024], tile)
            tile = jnp.where(row == 7, msg[..., u : u + 1, 1024:], tile)
        tiles.append(tile)
    return jnp.concatenate(tiles, axis=-1)


def unfold(msg):
    row = lax.broadcasted_iota(jnp.int32, msg.shape[:-1] + (128,), msg.ndim - 2)
    last = [jnp.zeros(row.shape, F32)] * 2
    for u in range(COLS):
        for i in range(2):
            piece = msg[..., 6 + i : 7 + i, 128 * u : 128 * u + 128]
            last[i] = jnp.where(row == u, piece, last[i])
    return jnp.concatenate([msg] + last, axis=-1)


def dot(left, right):
    return jnp.dot(left, right, preferred_element_type=F32)


def kernel(
    grid_h, pw_h, one_h, two_h, up_h, down_h, tab_h, sq_h, fw_h, bw_h, g1_h, bias_h, g2_h,
    out_ref,
    sq_v, fw_ref, bw_ref, g1_ref, bias_ref, g2_ref,
    grid_v, pw_v, one_v, two_v, up_v, down_v, tab_v,
    t_v, m_v, lhs_v, side_v, rim_v, te_v, q0_v, q3_v, tot_v, acc_v, nf_v, tn_v, nrm_v,
    ew_s, ew_r, ns_s, ns_r,
    p1_s, p1_r, p2_s, p2_r, p3_s, p3_r, p4_s, p4_r,
    z_v, v_v, w1_v, w2_v, h0_v, h1_v,
    lsem, halo_ss, halo_rs, s1, r1, s2, r2, s3, r3, s4, r4,
):
    a = lax.axis_index("lat")
    b = lax.axis_index("lon")
    q = b // 16
    p = b % 16
    row_y = p // 4
    row_z = p % 4
    mine = (row_y + row_z) % 2
    n = 2 * row_y + row_z // 2
    g = 2 * a + q

    barrier = pltpu.get_barrier_semaphore()

    def greet_lon(d, _):
        pl.semaphore_signal(
            barrier, inc=1, device_id=(a, lax.rem(b + d, NLON)), device_id_type=MESH
        )
        return 0

    lax.fori_loop(1, NLON, greet_lon, 0)

    def greet_lat(d, _):
        mate = lax.rem(a + 1 + d // 2, NLAT)
        pl.semaphore_signal(
            barrier, inc=1, device_id=(mate, (d % 2) * 16 + p), device_id_type=MESH
        )
        return 0

    lax.fori_loop(0, 6, greet_lat, 0)
    def load(index, src, dst):
        copy = pltpu.make_async_copy(src, dst, lsem.at[index])
        copy.start()
        return copy

    c_grid = load(0, grid_h, grid_v)
    c_sq = load(10, sq_h, sq_v)
    c_tab = load(1, tab_h, tab_v)
    c_pw = {}
    for i, off in enumerate((0, 3, 1, 2)):
        part = pl.ds(1280 * off, 1280)
        c_pw[off] = load(2 + i, pw_h.at[part], pw_v.at[part])
    c_one = load(6, one_h.at[:, n], one_v)
    c_two = load(7, two_h.at[:, n], two_v)
    small = [
        load(11 + i, src, dst)
        for i, (src, dst) in enumerate(
            ((g1_h, g1_ref), (bias_h, bias_ref), (g2_h, g2_ref), (fw_h, fw_ref), (bw_h, bw_ref))
        )
    ]

    nf_v[:, :, 144:] = jnp.zeros((6, 2, 48, 128), F32)
    for smp in range(2):
        for first in (240 * smp, 240 * smp + 192):
            m_v[:, :, first : first + 48] = jnp.zeros((2, 6, 48, 128), F32)
    for tile in range(6):
        q0_v[tile, pl.ds(0, 12, stride=32), :] = jnp.zeros((12, 128), F32)
        q3_v[tile, pl.ds(31, 12, stride=32), :] = jnp.zeros((12, 128), F32)
    c_grid.wait()
    c_sq.wait()
    for smp in range(2):
        for lp in range(3):
            block = grid_v[smp, :, 16 * lp : 16 * lp + 16, :]
            block = block.astype(F32).reshape(NV, 2, 8, 192)
            for half in range(2):
                x = block[:, half].reshape(NV * 8, 192).astype(BF16)
                turned = lax.dot_general(
                    sq_v[0], x, (((1,), (1,)), ((), ())), preferred_element_type=F32
                )
                first = (6 * smp + 2 * lp + half) * ROWS
                for r8 in range(8):
                    t_v[r8, first : first + ROWS, :] = turned[ROWS * r8 : ROWS * r8 + ROWS]

    c_tab.wait()
    for half in range(2):
        value = dot(t_v[4 * half].astype(BF16), tab_v[0])
        for r in range(1, 4):
            value = value + dot(t_v[4 * half + r].astype(BF16), tab_v[r])
        for tile in range(6):
            lanes = slice(128 * tile, 128 * tile + 128)
            for smp in range(2):
                m_v[half, tile, 240 * smp + 48 : 240 * smp + 192] = value[
                    144 * smp : 144 * smp + 144, lanes
                ]

    places = ((3, 0), (4, 0), (5, 0), (1, 1), (2, 1), (3, 1), (4, 1), (5, 1), (1, 2), (2, 2))
    for half in range(2):
        for tile, (lane, slot) in enumerate(places):
            cols = slice(128 * tile, 128 * tile + 128)
            outer = []
            for smp in range(2):
                first = (10 * smp + slot) * ROWS
                rim = first + (0, ROWS - 1)[half]
                value = m_v[half, lane, first : first + 192, :]
                row = m_v[half, lane, pl.ds(rim, 8, stride=ROWS), :]
                if tile in (2, 7):
                    value = value + m_v[half, 0, first + ROWS : first + ROWS + 192, :]
                    row = row + m_v[half, 0, pl.ds(rim + ROWS, 8, stride=ROWS), :]
                outer.append(row)
                lhs_v[half, 144 * smp : 144 * smp + 144, cols] = value[ROWS:168].astype(BF16)
                side = jnp.concatenate([value[:ROWS], value[168:]], axis=0)
                side_v[half, 48 * smp : 48 * smp + 48, cols] = side.astype(BF16)
            rim_v[half, :, cols] = jnp.concatenate(outer, axis=0).astype(BF16)

    def weight(off, pair):
        return pw_v[1280 * off : 1280 * off + 1280, 256 * pair : 256 * pair + 256]

    for way, (off, half) in enumerate(((0, 1), (3, 0))):
        c_pw[off].wait()
        for pair in range(3):
            value = dot(rim_v[half], weight(off, pair))
            ns_s[way, :, 256 * pair : 256 * pair + 256] = value.astype(BF16)

    pl.semaphore_wait(barrier, NLON - 1 + 6)

    def remote(src, dst, ssem, rsem, dev):
        return pltpu.make_async_remote_copy(
            src_ref=src, dst_ref=dst, send_sem=ssem, recv_sem=rsem,
            device_id=dev, device_id_type=MESH,
        )

    halos = [
        remote(
            src.at[i], dst.at[i], halo_ss.at[sem + i], halo_rs.at[sem + i],
            (lax.rem(a + da, NLAT), lax.rem(b + db, NLON)),
        )
        for src, dst, sem, ways in (
            (ns_s, ns_r, 0, ((1, 0), (NLAT - 1, 0))),
            (ew_s, ew_r, 2, ((0, 1), (0, NLON - 1))),
        )
        for i, (da, db) in enumerate(ways)
    ]
    halos[0].start()
    halos[1].start()

    c_pw[1].wait()
    c_pw[2].wait()
    none = jnp.zeros((4, 1, 256), F32)
    for pair in range(3):
        value = dot(side_v[0], weight(1, pair)) + dot(side_v[1], weight(2, pair))
        above = dot(side_v[1], weight(0, pair)).reshape(4, ROWS, 256)
        below = dot(side_v[0], weight(3, pair)).reshape(4, ROWS, 256)
        above = jnp.concatenate([none, above[:, :-1]], axis=1)
        below = jnp.concatenate([below[:, 1:], none], axis=1)
        value = value + (above + below).reshape(96, 256)
        te_v[2 * pair] = value[:, :128]
        te_v[2 * pair + 1] = value[:, 128:]

    def rim_rows(way, cols, picks):
        rows = ns_r[way, :, cols].astype(F32)
        rows = jnp.concatenate([rows[lo:hi] for lo, hi in picks], axis=0)
        return jnp.where((a > 0, a < NLAT - 1)[way], rows, 0.0)

    halos[0].wait_recv()
    halos[1].wait_recv()
    for tile in range(6):
        cols = slice(128 * tile, 128 * tile + 128)
        for way in range(2):
            at = pl.ds((0, ROWS - 1)[way], 4, stride=ROWS)
            te_v[tile, at, :] += rim_rows(way, cols, ((0, 1), (7, 8), (8, 9), (15, 16)))
        for smp in range(2):
            for way in range(2):
                first = ROWS * (2 * smp + 1 - way)
                ew_s[way, smp, :, cols] = te_v[tile, first : first + ROWS, :].astype(BF16)
    halos[2].start()
    halos[3].start()

    for pair in range(3):
        for off, half, out_v, lead in ((0, 1, q0_v, 1), (3, 0, q3_v, 7)):
            value = dot(lhs_v[half], weight(off, pair))
            for lane in range(2):
                lanes = slice(128 * lane, 128 * lane + 128)
                for m in range(12):
                    out_v[2 * pair + lane, 32 * m + lead : 32 * m + lead + ROWS, :] = value[
                        ROWS * m : ROWS * m + ROWS, lanes
                    ]
        value = dot(lhs_v[0], weight(1, pair)) + dot(lhs_v[1], weight(2, pair))
        for lane in range(2):
            tile = 2 * pair + lane
            shifted = (
                q0_v[tile].reshape(12, 32, 128)[:, :ROWS] + q3_v[tile].reshape(12, 32, 128)[:, 8:]
            )
            tot_v[tile] = value[:, 128 * lane : 128 * lane + 128] + shifted.reshape(288, 128)
    c_up = load(8, up_h, up_v)
    c_down = load(9, down_h, down_v)
    for tile in range(6):
        cols = slice(128 * tile, 128 * tile + 128)
        for way in range(2):
            at = pl.ds((0, ROWS - 1)[way], 12, stride=ROWS)
            tot_v[tile, at, :] += rim_rows(way, cols, ((1, 7), (9, 15)))
    halos[2].wait_recv()
    halos[3].wait_recv()
    for tile in range(6):
        cols = slice(128 * tile, 128 * tile + 128)
        for smp in range(2):
            for way, j in ((0, 0), (1, COLS - 1)):
                first = ROWS * (COLS * smp + j)
                tot_v[tile, first : first + ROWS, :] += ew_r[way, smp, :, cols].astype(F32)
    for copy in small:
        copy.wait()

    def owner(part, smp, blk):
        return part * 16 + (blk // 2) * 4 + (blk % 2) * 2 + (smp + blk // 2) % 2

    for smp in range(2):
        rows = slice(144 * smp, 144 * smp + 144)
        tok = jnp.concatenate([tot_v[t, rows, :] for t in range(6)], axis=1)
        tok = tok.astype(BF16).astype(F32)
        normed = norm(tok, g1_ref[...].reshape(1, C)).astype(BF16).astype(F32)
        tn_v[rows, :] = tok + normed
        for tile in range(6):
            nf_v[tile, smp, :144] = normed[:, 128 * tile : 128 * tile + 128]
        for part in range(2):
            planes = [
                jnp.concatenate(
                    [nf_v[t, smp, pl.ds(part * ROW12 + i, 8, stride=ROWS), :] for t in range(6)],
                    axis=1,
                )
                for i in range(ROW12)
            ]
            for blk in range(NB):
                msg = jnp.concatenate(
                    [plane[:, BS * blk : BS * blk + BS] for plane in planes], axis=1
                )
                p1_s[owner(part, smp, blk)] = fold(msg).astype(BF16)
        odd = (smp + mine) % 2
        for dx in (1, 0):
            for dy in (2, 1, 3, 0):
                for dz in (2, 0):
                    dest = (
                        ((q + dx) % 2) * 16 + ((row_y + dy) % 4) * 4 + (row_z + dz + (odd + dy) % 2) % 4
                    )

                    def send(dest=dest):
                        remote(
                            p1_s.at[dest], p1_r.at[b], s1.at[dest], r1.at[b], (a, dest)
                        ).start()

                    if (dx, dy, dz) == (0, 0, 0):
                        pl.when(odd == 1)(send)
                    else:
                        send()
    p1_r[b] = p1_s[b]

    c_one.wait()
    c_two.wait()
    for src, dst in ((one_v, w1_v), (two_v, w2_v)):
        dst[...] = jnp.zeros_like(dst)
        dst[0:BS, 0:BS] = src[0].astype(BF16)
        dst[0:BS, 128 : 128 + BS] = src[1].astype(BF16)
        dst[128 : 128 + BS, 0:BS] = -src[1].astype(BF16)
        dst[128 : 128 + BS, 128 : 128 + BS] = src[0].astype(BF16)
    bias = jnp.zeros((1, 256), F32)
    for blk in range(NB):
        parts = []
        for ri in range(2):
            parts.append(bias_ref[ri : ri + 1, BS * blk : BS * blk + BS])
            parts.append(jnp.zeros((1, 32), F32))
        bias = bias + jnp.where(n == blk, jnp.concatenate(parts, axis=1), 0.0)

    def wait1(d, _):
        src = lax.rem(b + d, NLON)
        remote(p1_s.at[src], p1_r.at[src], s1.at[src], r1.at[src], (a, src)).wait_recv()
        return 0

    lax.fori_loop(1, NLON, wait1, 0)

    def mate_of(d):
        other = lax.rem(g + d, 8)
        return other, (other // 2, (other % 2) * 16 + p)

    x = unfold(p1_r[...].astype(F32)).reshape(256, MSG).astype(BF16)
    for kh in range(2):
        part = dot(fw_ref[64 * kh : 64 * kh + 64, :], x)
        p2_s[kh] = part.reshape(8, 8, MSG).astype(BF16)
        for d in range(1, 8):
            other, dev = mate_of(d)
            remote(
                p2_s.at[kh, other], p2_r.at[kh, g], s2.at[kh, other], r2.at[kh, g], dev
            ).start()

    def spread(kh, src, value):
        for i in range(ROW12):
            piece = value[:, BS * i : BS * i + BS]
            piece = jnp.concatenate([piece, jnp.zeros((8, 128 - BS), F32)], axis=1)
            z_v[pl.ds(768 * kh + ROW12 * src + i, 8, stride=H), :] = piece

    def gather(kh, dest):
        pieces = [
            v_v[pl.ds(768 * kh + ROW12 * dest + i, 8, stride=H), :][:, :BS] for i in range(ROW12)
        ]
        return jnp.concatenate(pieces, axis=1).astype(BF16)

    for kh in range(2):
        spread(kh, g, p2_s[kh, g].astype(F32))

        def take2(d, _):
            other, dev = mate_of(d)
            remote(
                p2_s.at[kh, other], p2_r.at[kh, other], s2.at[kh, other], r2.at[kh, other], dev
            ).wait_recv()
            spread(kh, other, p2_r[kh, other].astype(F32))
            return 0

        lax.fori_loop(1, 8, take2, 0)

        base = 768 * kh
        z = jnp.concatenate(
            [z_v[base + 192 * k : base + 192 * k + 192, :] for k in range(4)], axis=1
        )
        spec = dot(sq_v[1], z.astype(BF16))
        modes = jnp.concatenate(
            [
                jnp.concatenate(
                    [spec[:H, 128 * k : 128 * k + 128], spec[H:, 128 * k : 128 * k + 128]], axis=1
                )
                for k in range(4)
            ],
            axis=0,
        )
        mid = jnp.maximum(dot(modes.astype(BF16), w1_v[...]) + bias, 0.0)
        res = dot(mid.astype(BF16), w2_v[...])
        res = res - jnp.clip(res, -0.01, 0.01)
        back = jnp.concatenate(
            [
                jnp.concatenate(
                    [res[H * k : H * k + H, :128], res[H * k : H * k + H, 128:]], axis=0
                )
                for k in range(4)
            ],
            axis=1,
        )
        rows = dot(sq_v[2], back.astype(BF16))
        for k in range(4):
            v_v[base + 192 * k : base + 192 * k + 192, :] = rows[:, 128 * k : 128 * k + 128]

        def send3(d, _):
            other, dev = mate_of(d)
            p3_s[kh, other] = gather(kh, other)
            remote(
                p3_s.at[kh, other], p3_r.at[kh, g], s3.at[kh, other], r3.at[kh, g], dev
            ).start()
            return 0

        lax.fori_loop(1, 8, send3, 0)
        p3_r[kh, g] = gather(kh, g)

    def wait3(d, _):
        other, dev = mate_of(d)
        for kh in range(2):
            remote(
                p3_s.at[kh, other], p3_r.at[kh, other], s3.at[kh, other], r3.at[kh, other], dev
            ).wait_recv()
        return 0

    lax.fori_loop(1, 8, wait3, 0)

    spectra = p3_r[...].astype(F32).reshape(128, MSG).astype(BF16)
    for dx in (1, 0):
        other = (q + dx) % 2
        field = dot(bw_ref[pl.ds(pl.multiple_of(128 * other, 128), 128), :], spectra)
        p4_s[pl.ds(16 * other, 16)] = fold(field.reshape(16, 8, MSG)).astype(BF16)
        steps = [(dy, dz) for dy in range(4) for dz in range(4)]
        steps.sort(key=lambda t: -(min(t[0], 4 - t[0]) + min(t[1], 4 - t[1])))
        for dy, dz in steps:
            if (dx, dy, dz) != (0, 0, 0):
                dest = 16 * other + ((row_y + dy) % 4) * 4 + (row_z + dz) % 4
                remote(p4_s.at[dest], p4_r.at[b], s4.at[dest], r4.at[b], (a, dest)).start()
    p4_r[b] = p4_s[b]

    def wait4(d, _):
        src = lax.rem(b + d, NLON)
        remote(p4_s.at[src], p4_r.at[src], s4.at[src], r4.at[src], (a, src)).wait_recv()
        return 0

    lax.fori_loop(1, NLON, wait4, 0)

    for smp in range(2):

        def join(part, _):
            msgs = [unfold(p4_r[owner(part, smp, blk)].astype(F32)) for blk in range(NB)]
            for i in range(ROW12):
                plane = jnp.concatenate([m[:, BS * i : BS * i + BS] for m in msgs], axis=1)
                for tile in range(6):
                    nf_v[tile, smp, pl.ds(part * ROW12 + i, 8, stride=ROWS), :] = plane[
                        :, 128 * tile : 128 * tile + 128
                    ]
            return 0

        lax.fori_loop(0, 2, join, 0)
        rows = slice(144 * smp, 144 * smp + 144)
        field = jnp.concatenate([nf_v[tile, smp, :144] for tile in range(6)], axis=1)
        middle = (field + tn_v[rows, :]).astype(BF16).astype(F32)
        acc_v[rows, :] = middle
        nrm_v[rows, :] = norm(middle, g2_ref[...].reshape(1, C)).astype(BF16)

    c_up.wait()
    c_down.wait()

    def up(step):
        return dot(nrm_v[...], up_v[:, pl.ds(pl.multiple_of(step * 256, 256), 256)])

    def down(hidden, step):
        hidden = 0.5 * hidden * (1.0 + lax.erf(hidden * (1.0 / math.sqrt(2.0))))
        rows = pl.ds(pl.multiple_of(step * 256, 256), 256)
        return dot(hidden.astype(BF16), down_v[rows, :])

    h0_v[...] = up(0)

    def mlp(it, _):
        step = 2 * it
        h1_v[...] = up(step + 1)
        acc_v[...] += down(h0_v[...], step)
        h0_v[...] = up(jnp.minimum(step + 2, HID // 256 - 1))
        acc_v[...] += down(h1_v[...], step + 1)
        return 0

    lax.fori_loop(0, HID // 512, mlp, 0)
    out_ref[...] = acc_v[...].reshape(2, COLS, ROWS, C).astype(BF16)

    for copy in halos:
        copy.wait_send()

    def drain_lon(d, _):
        dest = lax.rem(b + d, NLON)
        remote(p1_s.at[dest], p1_r.at[b], s1.at[dest], r1.at[b], (a, dest)).wait_send()
        remote(p4_s.at[dest], p4_r.at[b], s4.at[dest], r4.at[b], (a, dest)).wait_send()
        return 0

    lax.fori_loop(1, NLON, drain_lon, 0)

    def drain_lat(d, _):
        other, dev = mate_of(d)
        for kh in range(2):
            remote(
                p2_s.at[kh, other], p2_r.at[kh, g], s2.at[kh, other], r2.at[kh, g], dev
            ).wait_send()
            remote(
                p3_s.at[kh, other], p3_r.at[kh, g], s3.at[kh, other], r3.at[kh, g], dev
            ).wait_send()
        return 0

    lax.fori_loop(1, 8, drain_lat, 0)


def local(
    grid, patch_weight, norm_gain_one, spectral_one, spectral_bias, spectral_two,
    norm_gain_two, fc_up, fc_down,
):
    fw, bw = lon_tables()
    fh, bh = lat_tables()
    const = lambda x: jnp.asarray(x, F32).astype(BF16)
    any_spec = pl.BlockSpec(memory_space=pl.ANY)
    vmem = pl.BlockSpec(memory_space=pltpu.VMEM)
    dma = pltpu.SemaphoreType.DMA
    out = pl.pallas_call(
        kernel,
        out_shape=jax.ShapeDtypeStruct((2, COLS, ROWS, C), BF16),
        in_specs=[any_spec] * 13,
        out_specs=vmem,
        scratch_shapes=[
            pltpu.VMEM((3, 192, 192), BF16),
            pltpu.VMEM((128, 256), BF16),
            pltpu.VMEM((256, 128), BF16),
            pltpu.VMEM((C,), F32),
            pltpu.VMEM((2, C), F32),
            pltpu.VMEM((C,), F32),
            pltpu.VMEM((2, NV, 48, 192), BF16),
            pltpu.VMEM((5120, C), BF16),
            pltpu.VMEM((2, BS, BS), F32),
            pltpu.VMEM((2, BS, BS), F32),
            pltpu.VMEM((C, HID), BF16),
            pltpu.VMEM((HID, C), BF16),
            pltpu.VMEM((4, 160, 768), BF16),
            pltpu.VMEM((8, 288, 160), F32),
            pltpu.VMEM((2, 6, 480, 128), F32),
            pltpu.VMEM((2, 288, 1280), BF16),
            pltpu.VMEM((2, 96, 1280), BF16),
            pltpu.VMEM((2, 16, 1280), BF16),
            pltpu.VMEM((6, 96, 128), F32),
            pltpu.VMEM((6, 384, 128), F32),
            pltpu.VMEM((6, 384, 128), F32),
            pltpu.VMEM((6, 288, 128), F32),
            pltpu.VMEM((288, C), F32),
            pltpu.VMEM((6, 2, 192, 128), F32),
            pltpu.VMEM((288, C), F32),
            pltpu.VMEM((288, C), BF16),
            pltpu.VMEM((2, 2, ROWS, C), BF16),
            pltpu.VMEM((2, 2, ROWS, C), BF16),
            pltpu.VMEM((2, 16, C), BF16),
            pltpu.VMEM((2, 16, C), BF16),
            pltpu.VMEM((NLON, 8, 896), BF16),
            pltpu.VMEM((NLON, 8, 896), BF16),
            pltpu.VMEM((2, 8, 8, MSG), BF16),
            pltpu.VMEM((2, 8, 8, MSG), BF16),
            pltpu.VMEM((2, 8, 8, MSG), BF16),
            pltpu.VMEM((2, 8, 8, MSG), BF16),
            pltpu.VMEM((NLON, 8, 896), BF16),
            pltpu.VMEM((NLON, 8, 896), BF16),
            pltpu.VMEM((8 * 192, 128), F32),
            pltpu.VMEM((8 * 192, 128), F32),
            pltpu.VMEM((256, 256), BF16),
            pltpu.VMEM((256, 256), BF16),
            pltpu.VMEM((288, 256), F32),
            pltpu.VMEM((288, 256), F32),
            dma((16,)),
            dma((4,)),
            dma((4,)),
            dma((NLON,)),
            dma((NLON,)),
            dma((2, 8)),
            dma((2, 8)),
            dma((2, 8)),
            dma((2, 8)),
            dma((NLON,)),
            dma((NLON,)),
        ],
        compiler_params=pltpu.CompilerParams(
            collective_id=0, has_side_effects=True, vmem_limit_bytes=56 * 1024 * 1024
        ),
    )(
        grid.transpose(0, 1, 3, 2), patch_weight, spectral_one, spectral_two, fc_up, fc_down,
        const(feature_table()),
        const(np.stack([pick_table(), fh, bh])), const(fw), const(bw),
        norm_gain_one, spectral_bias, norm_gain_two,
    )
    return out.transpose(0, 2, 1, 3)


def solution(mesh):
    in_specs = (P(None, None, "lat", "lon"), P(), P(), P(), P(), P(), P(), P(), P())
    out_specs = P(None, "lat", "lon", None)
    return jax.shard_map(local, mesh=mesh, in_specs=in_specs, out_specs=out_specs, check_vma=False)
```

```python
import math

import jax
import jax.numpy as jnp
import numpy as np
from jax import lax
from jax.experimental import pallas as pl
from jax.experimental.pallas import tpu as pltpu
from jax.sharding import PartitionSpec as P

MESH = pl.DeviceIdType.MESH
F32 = jnp.float32
BF16 = jnp.bfloat16

NLAT, NLON = 4, 32
NV, C, HID, NB, BS = 20, 768, 3072, 8, 96
H, W, KW = 96, 192, 64
ROWS, COLS = 24, 6
ROW12 = 12
MSG = ROW12 * BS


def pick_table():
    sel = np.zeros((192, 192), np.float32)
    for r8 in range(8):
        for row in range(ROWS):
            sel[r8 * ROWS + row, 8 * row + r8] = 1.0
    return sel


def feature_table():
    table = np.zeros((4, 160, 768), np.float32)
    for r in range(4):
        for v in range(NV):
            for c8 in range(8):
                table[r, v * 8 + c8, (64, 384)[c8 // 4] + v * 16 + 4 * r + c8 % 4] = 1.0
    return table


def lon_tables():
    k = np.arange(KW)
    w = np.arange(W)
    angle = 2.0 * math.pi * ((k[:, None] * w[None, :]) % W) / W
    scale = 1.0 / math.sqrt(W)
    both = np.stack([np.cos(angle), -np.sin(angle)]) * scale
    fwd = both.reshape(2, 8, 2, 4, W).transpose(2, 1, 3, 0, 4).reshape(128, NLON, COLS)
    fwd = np.pad(fwd, ((0, 0), (0, 0), (0, 2))).reshape(128, 256)
    weight = np.where(k == 0, 1.0, 2.0)
    back = both * weight[None, :, None]
    back = back.reshape(2, 8, 2, 4, W).transpose(4, 2, 1, 3, 0).reshape(NLON, COLS, 128)
    back = np.pad(back, ((0, 0), (0, 2), (0, 0))).reshape(256, 128)
    return fwd, back


def lat_tables():
    h = np.arange(H)
    angle = 2.0 * math.pi * ((h[:, None] * h[None, :]) % H) / H
    cos, sin = np.cos(angle) / math.sqrt(H), np.sin(angle) / math.sqrt(H)
    fwd = np.block([[cos, sin], [-sin, cos]])
    back = np.block([[cos, -sin], [sin, cos]])
    return fwd, back


def norm(values, gain):
    centre = jnp.mean(values, axis=-1, keepdims=True)
    off = values - centre
    spread = jnp.mean(jnp.square(off), axis=-1, keepdims=True)
    return off * lax.rsqrt(spread + 1e-05) * gain


def fold(msg):
    row = lax.broadcasted_iota(jnp.int32, msg.shape[:-1] + (128,), msg.ndim - 2)
    tiles = []
    for u in range(7):
        tile = msg[..., 128 * u : 128 * u + 128]
        if u < COLS:
            tile = jnp.where(row == 6, msg[..., u : u + 1, 896:1024], tile)
            tile = jnp.where(row == 7, msg[..., u : u + 1, 1024:], tile)
        tiles.append(tile)
    return jnp.concatenate(tiles, axis=-1)


def unfold(msg):
    row = lax.broadcasted_iota(jnp.int32, msg.shape[:-1] + (128,), msg.ndim - 2)
    last = [jnp.zeros(row.shape, F32)] * 2
    for u in range(COLS):
        for i in range(2):
            piece = msg[..., 6 + i : 7 + i, 128 * u : 128 * u + 128]
            last[i] = jnp.where(row == u, piece, last[i])
    return jnp.concatenate([msg] + last, axis=-1)


def dot(left, right):
    return jnp.dot(left, right, preferred_element_type=F32)


def kernel(
    grid_h, pw_h, one_h, two_h, up_h, down_h, tab_h, sq_h, fw_h, bw_h, g1_h, bias_h, g2_h,
    out_ref,
    sq_v, fw_ref, bw_ref, g1_ref, bias_ref, g2_ref,
    grid_v, pw_v, one_v, two_v, up_v, down_v, tab_v,
    t_v, m_v, lhs_v, side_v, rim_v, te_v, q0_v, q3_v, tot_v, acc_v, nf_v, tn_v, nrm_v,
    ew_s, ew_r, ns_s, ns_r,
    p1_s, p1_r, p2_s, p2_r, p3_s, p3_r, p4_s, p4_r,
    z_v, v_v, w1_v, w2_v, h0_v, h1_v, res_v,
    lsem, halo_ss, halo_rs, s1, r1, s2, r2, s3, r3, s4, r4,
):
    a = lax.axis_index("lat")
    b = lax.axis_index("lon")
    q = b // 16
    p = b % 16
    row_y = p // 4
    row_z = p % 4
    mine = (row_y + row_z) % 2
    n = 2 * row_y + row_z // 2
    g = 2 * a + q

    barrier = pltpu.get_barrier_semaphore()

    def greet_lon(d, _):
        pl.semaphore_signal(
            barrier, inc=1, device_id=(a, lax.rem(b + d, NLON)), device_id_type=MESH
        )
        return 0

    lax.fori_loop(1, NLON, greet_lon, 0)

    def greet_lat(d, _):
        mate = lax.rem(a + 1 + d // 2, NLAT)
        pl.semaphore_signal(
            barrier, inc=1, device_id=(mate, (d % 2) * 16 + p), device_id_type=MESH
        )
        return 0

    lax.fori_loop(0, 6, greet_lat, 0)
    def load(index, src, dst):
        copy = pltpu.make_async_copy(src, dst, lsem.at[index])
        copy.start()
        return copy

    c_grid = load(0, grid_h, grid_v)
    c_sq = load(10, sq_h, sq_v)
    c_tab = load(1, tab_h, tab_v)
    c_pw = {}
    for i, off in enumerate((0, 3, 1, 2)):
        part = pl.ds(1280 * off, 1280)
        c_pw[off] = load(2 + i, pw_h.at[part], pw_v.at[part])
    c_one = load(6, one_h.at[:, n], one_v)
    c_two = load(7, two_h.at[:, n], two_v)
    small = [
        load(11 + i, src, dst)
        for i, (src, dst) in enumerate(
            ((g1_h, g1_ref), (bias_h, bias_ref), (g2_h, g2_ref), (fw_h, fw_ref), (bw_h, bw_ref))
        )
    ]

    nf_v[:, :, 144:] = jnp.zeros((6, 2, 48, 128), F32)
    for smp in range(2):
        for first in (240 * smp, 240 * smp + 192):
            m_v[:, :, first : first + 48] = jnp.zeros((2, 6, 48, 128), F32)
    for tile in range(6):
        q0_v[tile, pl.ds(0, 12, stride=32), :] = jnp.zeros((12, 128), F32)
        q3_v[tile, pl.ds(31, 12, stride=32), :] = jnp.zeros((12, 128), F32)
    c_grid.wait()
    c_sq.wait()
    for smp in range(2):
        for lp in range(3):
            block = grid_v[smp, :, 16 * lp : 16 * lp + 16, :]
            block = block.astype(F32).reshape(NV, 2, 8, 192)
            for half in range(2):
                x = block[:, half].reshape(NV * 8, 192).astype(BF16)
                turned = lax.dot_general(
                    sq_v[0], x, (((1,), (1,)), ((), ())), preferred_element_type=F32
                )
                first = (6 * smp + 2 * lp + half) * ROWS
                for r8 in range(8):
                    t_v[r8, first : first + ROWS, :] = turned[ROWS * r8 : ROWS * r8 + ROWS]

    c_tab.wait()
    for half in range(2):
        value = dot(t_v[4 * half].astype(BF16), tab_v[0])
        for r in range(1, 4):
            value = value + dot(t_v[4 * half + r].astype(BF16), tab_v[r])
        for tile in range(6):
            lanes = slice(128 * tile, 128 * tile + 128)
            for smp in range(2):
                m_v[half, tile, 240 * smp + 48 : 240 * smp + 192] = value[
                    144 * smp : 144 * smp + 144, lanes
                ]

    places = ((3, 0), (4, 0), (5, 0), (1, 1), (2, 1), (3, 1), (4, 1), (5, 1), (1, 2), (2, 2))
    for half in range(2):
        for tile, (lane, slot) in enumerate(places):
            cols = slice(128 * tile, 128 * tile + 128)
            outer = []
            for smp in range(2):
                first = (10 * smp + slot) * ROWS
                rim = first + (0, ROWS - 1)[half]
                value = m_v[half, lane, first : first + 192, :]
                row = m_v[half, lane, pl.ds(rim, 8, stride=ROWS), :]
                if tile in (2, 7):
                    value = value + m_v[half, 0, first + ROWS : first + ROWS + 192, :]
                    row = row + m_v[half, 0, pl.ds(rim + ROWS, 8, stride=ROWS), :]
                outer.append(row)
                lhs_v[half, 144 * smp : 144 * smp + 144, cols] = value[ROWS:168].astype(BF16)
                side = jnp.concatenate([value[:ROWS], value[168:]], axis=0)
                side_v[half, 48 * smp : 48 * smp + 48, cols] = side.astype(BF16)
            rim_v[half, :, cols] = jnp.concatenate(outer, axis=0).astype(BF16)

    def weight(off, pair):
        return pw_v[1280 * off : 1280 * off + 1280, 256 * pair : 256 * pair + 256]

    for way, (off, half) in enumerate(((0, 1), (3, 0))):
        c_pw[off].wait()
        for pair in range(3):
            value = dot(rim_v[half], weight(off, pair))
            ns_s[way, :, 256 * pair : 256 * pair + 256] = value.astype(BF16)

    pl.semaphore_wait(barrier, NLON - 1 + 6)

    def remote(src, dst, ssem, rsem, dev):
        return pltpu.make_async_remote_copy(
            src_ref=src, dst_ref=dst, send_sem=ssem, recv_sem=rsem,
            device_id=dev, device_id_type=MESH,
        )

    halos = [
        remote(
            src.at[i], dst.at[i], halo_ss.at[sem + i], halo_rs.at[sem + i],
            (lax.rem(a + da, NLAT), lax.rem(b + db, NLON)),
        )
        for src, dst, sem, ways in (
            (ns_s, ns_r, 0, ((1, 0), (NLAT - 1, 0))),
            (ew_s, ew_r, 2, ((0, 1), (0, NLON - 1))),
        )
        for i, (da, db) in enumerate(ways)
    ]
    halos[0].start()
    halos[1].start()

    c_pw[1].wait()
    c_pw[2].wait()
    none = jnp.zeros((4, 1, 256), F32)
    for pair in range(3):
        value = dot(side_v[0], weight(1, pair)) + dot(side_v[1], weight(2, pair))
        above = dot(side_v[1], weight(0, pair)).reshape(4, ROWS, 256)
        below = dot(side_v[0], weight(3, pair)).reshape(4, ROWS, 256)
        above = jnp.concatenate([none, above[:, :-1]], axis=1)
        below = jnp.concatenate([below[:, 1:], none], axis=1)
        value = value + (above + below).reshape(96, 256)
        te_v[2 * pair] = value[:, :128]
        te_v[2 * pair + 1] = value[:, 128:]

    def rim_rows(way, cols, picks):
        rows = ns_r[way, :, cols].astype(F32)
        rows = jnp.concatenate([rows[lo:hi] for lo, hi in picks], axis=0)
        return jnp.where((a > 0, a < NLAT - 1)[way], rows, 0.0)

    halos[0].wait_recv()
    halos[1].wait_recv()
    for tile in range(6):
        cols = slice(128 * tile, 128 * tile + 128)
        for way in range(2):
            at = pl.ds((0, ROWS - 1)[way], 4, stride=ROWS)
            te_v[tile, at, :] += rim_rows(way, cols, ((0, 1), (7, 8), (8, 9), (15, 16)))
        for smp in range(2):
            for way in range(2):
                first = ROWS * (2 * smp + 1 - way)
                ew_s[way, smp, :, cols] = te_v[tile, first : first + ROWS, :].astype(BF16)
    halos[2].start()
    halos[3].start()

    for pair in range(3):
        for off, half, out_v, lead in ((0, 1, q0_v, 1), (3, 0, q3_v, 7)):
            value = dot(lhs_v[half], weight(off, pair))
            for lane in range(2):
                lanes = slice(128 * lane, 128 * lane + 128)
                for m in range(12):
                    out_v[2 * pair + lane, 32 * m + lead : 32 * m + lead + ROWS, :] = value[
                        ROWS * m : ROWS * m + ROWS, lanes
                    ]
        value = dot(lhs_v[0], weight(1, pair)) + dot(lhs_v[1], weight(2, pair))
        for lane in range(2):
            tile = 2 * pair + lane
            shifted = (
                q0_v[tile].reshape(12, 32, 128)[:, :ROWS] + q3_v[tile].reshape(12, 32, 128)[:, 8:]
            )
            tot_v[tile] = value[:, 128 * lane : 128 * lane + 128] + shifted.reshape(288, 128)
    c_up = load(8, up_h, up_v)
    c_down = load(9, down_h, down_v)
    for tile in range(6):
        cols = slice(128 * tile, 128 * tile + 128)
        for way in range(2):
            at = pl.ds((0, ROWS - 1)[way], 12, stride=ROWS)
            tot_v[tile, at, :] += rim_rows(way, cols, ((1, 7), (9, 15)))
    halos[2].wait_recv()
    halos[3].wait_recv()
    for tile in range(6):
        cols = slice(128 * tile, 128 * tile + 128)
        for smp in range(2):
            for way, j in ((0, 0), (1, COLS - 1)):
                first = ROWS * (COLS * smp + j)
                tot_v[tile, first : first + ROWS, :] += ew_r[way, smp, :, cols].astype(F32)
    for copy in small:
        copy.wait()

    def owner(part, smp, blk):
        return part * 16 + (blk // 2) * 4 + (blk % 2) * 2 + (smp + blk // 2) % 2

    for smp in range(2):
        rows = slice(144 * smp, 144 * smp + 144)
        tok = jnp.concatenate([tot_v[t, rows, :] for t in range(6)], axis=1)
        tok = tok.astype(BF16).astype(F32)
        normed = norm(tok, g1_ref[...].reshape(1, C)).astype(BF16).astype(F32)
        tn_v[rows, :] = tok + normed
        for tile in range(6):
            nf_v[tile, smp, :144] = normed[:, 128 * tile : 128 * tile + 128]
        for part in range(2):
            planes = [
                jnp.concatenate(
                    [nf_v[t, smp, pl.ds(part * ROW12 + i, 8, stride=ROWS), :] for t in range(6)],
                    axis=1,
                )
                for i in range(ROW12)
            ]
            for blk in range(NB):
                msg = jnp.concatenate(
                    [plane[:, BS * blk : BS * blk + BS] for plane in planes], axis=1
                )
                p1_s[owner(part, smp, blk)] = fold(msg).astype(BF16)
        odd = (smp + mine) % 2
        for dx in (1, 0):
            for dy in (2, 1, 3, 0):
                for dz in (2, 0):
                    dest = (
                        ((q + dx) % 2) * 16 + ((row_y + dy) % 4) * 4 + (row_z + dz + (odd + dy) % 2) % 4
                    )

                    def send(dest=dest):
                        remote(
                            p1_s.at[dest], p1_r.at[b], s1.at[dest], r1.at[b], (a, dest)
                        ).start()

                    if (dx, dy, dz) == (0, 0, 0):
                        pl.when(odd == 1)(send)
                    else:
                        send()
    p1_r[b] = p1_s[b]

    c_one.wait()
    c_two.wait()
    for src, dst in ((one_v, w1_v), (two_v, w2_v)):
        dst[...] = jnp.zeros_like(dst)
        dst[0:BS, 0:BS] = src[0].astype(BF16)
        dst[0:BS, 128 : 128 + BS] = src[1].astype(BF16)
        dst[128 : 128 + BS, 0:BS] = -src[1].astype(BF16)
        dst[128 : 128 + BS, 128 : 128 + BS] = src[0].astype(BF16)
    bias = jnp.zeros((1, 256), F32)
    for blk in range(NB):
        parts = []
        for ri in range(2):
            parts.append(bias_ref[ri : ri + 1, BS * blk : BS * blk + BS])
            parts.append(jnp.zeros((1, 32), F32))
        bias = bias + jnp.where(n == blk, jnp.concatenate(parts, axis=1), 0.0)

    def wait1(d, _):
        src = lax.rem(b + d, NLON)
        remote(p1_s.at[src], p1_r.at[src], s1.at[src], r1.at[src], (a, src)).wait_recv()
        return 0

    lax.fori_loop(1, NLON, wait1, 0)

    def mate_of(d):
        other = lax.rem(g + d, 8)
        return other, (other // 2, (other % 2) * 16 + p)

    x = unfold(p1_r[...].astype(F32)).reshape(256, MSG).astype(BF16)
    for kh in range(2):
        part = dot(fw_ref[64 * kh : 64 * kh + 64, :], x)
        p2_s[kh] = part.reshape(8, 8, MSG).astype(BF16)
        for d in range(1, 8):
            other, dev = mate_of(d)
            remote(
                p2_s.at[kh, other], p2_r.at[kh, g], s2.at[kh, other], r2.at[kh, g], dev
            ).start()

    def spread(kh, src, value):
        for i in range(ROW12):
            piece = value[:, BS * i : BS * i + BS]
            piece = jnp.concatenate([piece, jnp.zeros((8, 128 - BS), F32)], axis=1)
            z_v[pl.ds(768 * kh + ROW12 * src + i, 8, stride=H), :] = piece

    def gather(kh, dest):
        pieces = [
            v_v[pl.ds(768 * kh + ROW12 * dest + i, 8, stride=H), :][:, :BS] for i in range(ROW12)
        ]
        return jnp.concatenate(pieces, axis=1).astype(BF16)

    for kh in range(2):
        spread(kh, g, p2_s[kh, g].astype(F32))

        def take2(d, _):
            other, dev = mate_of(d)
            remote(
                p2_s.at[kh, other], p2_r.at[kh, other], s2.at[kh, other], r2.at[kh, other], dev
            ).wait_recv()
            spread(kh, other, p2_r[kh, other].astype(F32))
            return 0

        lax.fori_loop(1, 8, take2, 0)

        base = 768 * kh
        z = jnp.concatenate(
            [z_v[base + 192 * k : base + 192 * k + 192, :] for k in range(4)], axis=1
        )
        spec = dot(sq_v[1], z.astype(BF16))
        modes = jnp.concatenate(
            [
                jnp.concatenate(
                    [spec[:H, 128 * k : 128 * k + 128], spec[H:, 128 * k : 128 * k + 128]], axis=1
                )
                for k in range(4)
            ],
            axis=0,
        )
        mid = jnp.maximum(dot(modes.astype(BF16), w1_v[...]) + bias, 0.0)
        res = dot(mid.astype(BF16), w2_v[...])
        res = res - jnp.clip(res, -0.01, 0.01)
        back = jnp.concatenate(
            [
                jnp.concatenate(
                    [res[H * k : H * k + H, :128], res[H * k : H * k + H, 128:]], axis=0
                )
                for k in range(4)
            ],
            axis=1,
        )
        rows = dot(sq_v[2], back.astype(BF16))
        for k in range(4):
            v_v[base + 192 * k : base + 192 * k + 192, :] = rows[:, 128 * k : 128 * k + 128]

        def send3(d, _):
            other, dev = mate_of(d)
            p3_s[kh, other] = gather(kh, other)
            remote(
                p3_s.at[kh, other], p3_r.at[kh, g], s3.at[kh, other], r3.at[kh, g], dev
            ).start()
            return 0

        lax.fori_loop(1, 8, send3, 0)
        p3_r[kh, g] = gather(kh, g)

    def wait3(d, _):
        other, dev = mate_of(d)
        for kh in range(2):
            remote(
                p3_s.at[kh, other], p3_r.at[kh, other], s3.at[kh, other], r3.at[kh, other], dev
            ).wait_recv()
        return 0

    lax.fori_loop(1, 8, wait3, 0)

    spectra = p3_r[...].astype(F32).reshape(128, MSG).astype(BF16)
    for dx in (1, 0):
        other = (q + dx) % 2
        field = dot(bw_ref[pl.ds(pl.multiple_of(128 * other, 128), 128), :], spectra)
        p4_s[pl.ds(16 * other, 16)] = fold(field.reshape(16, 8, MSG)).astype(BF16)
        steps = [(dy, dz) for dy in range(4) for dz in range(4)]
        steps.sort(key=lambda t: -(min(t[0], 4 - t[0]) + min(t[1], 4 - t[1])))
        for dy, dz in steps:
            if (dx, dy, dz) != (0, 0, 0):
                dest = 16 * other + ((row_y + dy) % 4) * 4 + (row_z + dz) % 4
                remote(p4_s.at[dest], p4_r.at[b], s4.at[dest], r4.at[b], (a, dest)).start()
    p4_r[b] = p4_s[b]

    c_up.wait()
    c_down.wait()
    results = []
    for smp in range(2):
        for part in range(2):
            for blk in range(NB):
                src = owner(part, smp, blk)

                @pl.when(src != b)
                def _(src=src):
                    remote(
                        p4_s.at[src], p4_r.at[src], s4.at[src], r4.at[src], (a, src)
                    ).wait_recv()

        def join(part, _):
            msgs = [unfold(p4_r[owner(part, smp, blk)].astype(F32)) for blk in range(NB)]
            for i in range(ROW12):
                plane = jnp.concatenate([m[:, BS * i : BS * i + BS] for m in msgs], axis=1)
                for tile in range(6):
                    nf_v[tile, smp, pl.ds(part * ROW12 + i, 8, stride=ROWS), :] = plane[
                        :, 128 * tile : 128 * tile + 128
                    ]
            return 0

        lax.fori_loop(0, 2, join, 0)
        rows = slice(144 * smp, 144 * smp + 144)
        field = jnp.concatenate([nf_v[tile, smp, :144] for tile in range(6)], axis=1)
        middle = (field + tn_v[rows, :]).astype(BF16).astype(F32)
        acc_v[rows, :] = middle
        nrm_v[rows, :] = norm(middle, g2_ref[...].reshape(1, C)).astype(BF16)

        def up(step):
            return dot(nrm_v[rows, :], up_v[:, pl.ds(pl.multiple_of(step * 512, 512), 512)])

        def down(hidden, step):
            hidden = 0.5 * hidden * (1.0 + lax.erf(hidden * (1.0 / math.sqrt(2.0))))
            part = pl.ds(pl.multiple_of(step * 512, 512), 512)
            return dot(hidden.astype(BF16), down_v[part, :])

        h0_v[...] = up(0)

        def mlp(it, _):
            step = 2 * it
            h1_v[...] = up(step + 1)
            acc_v[rows, :] += down(h0_v[...], step)
            h0_v[...] = up(jnp.minimum(step + 2, HID // 512 - 1))
            acc_v[rows, :] += down(h1_v[...], step + 1)
            return 0

        lax.fori_loop(0, HID // 1024, mlp, 0)
        res_v[smp] = acc_v[rows, :].reshape(COLS, ROWS, C).astype(BF16)
        results.append(load(16 + smp, res_v.at[smp], out_ref.at[smp]))

    for copy in halos:
        copy.wait_send()

    def drain_lon(d, _):
        dest = lax.rem(b + d, NLON)
        remote(p1_s.at[dest], p1_r.at[b], s1.at[dest], r1.at[b], (a, dest)).wait_send()
        remote(p4_s.at[dest], p4_r.at[b], s4.at[dest], r4.at[b], (a, dest)).wait_send()
        return 0

    lax.fori_loop(1, NLON, drain_lon, 0)

    def drain_lat(d, _):
        other, dev = mate_of(d)
        for kh in range(2):
            remote(
                p2_s.at[kh, other], p2_r.at[kh, g], s2.at[kh, other], r2.at[kh, g], dev
            ).wait_send()
            remote(
                p3_s.at[kh, other], p3_r.at[kh, g], s3.at[kh, other], r3.at[kh, g], dev
            ).wait_send()
        return 0

    lax.fori_loop(1, 8, drain_lat, 0)
    for copy in results:
        copy.wait()


def local(
    grid, patch_weight, norm_gain_one, spectral_one, spectral_bias, spectral_two,
    norm_gain_two, fc_up, fc_down,
):
    fw, bw = lon_tables()
    fh, bh = lat_tables()
    const = lambda x: jnp.asarray(x, F32).astype(BF16)
    any_spec = pl.BlockSpec(memory_space=pl.ANY)
    dma = pltpu.SemaphoreType.DMA
    out = pl.pallas_call(
        kernel,
        out_shape=jax.ShapeDtypeStruct((2, COLS, ROWS, C), BF16),
        in_specs=[any_spec] * 13,
        out_specs=any_spec,
        scratch_shapes=[
            pltpu.VMEM((3, 192, 192), BF16),
            pltpu.VMEM((128, 256), BF16),
            pltpu.VMEM((256, 128), BF16),
            pltpu.VMEM((C,), F32),
            pltpu.VMEM((2, C), F32),
            pltpu.VMEM((C,), F32),
            pltpu.VMEM((2, NV, 48, 192), BF16),
            pltpu.VMEM((5120, C), BF16),
            pltpu.VMEM((2, BS, BS), F32),
            pltpu.VMEM((2, BS, BS), F32),
            pltpu.VMEM((C, HID), BF16),
            pltpu.VMEM((HID, C), BF16),
            pltpu.VMEM((4, 160, 768), BF16),
            pltpu.VMEM((8, 288, 160), F32),
            pltpu.VMEM((2, 6, 480, 128), F32),
            pltpu.VMEM((2, 288, 1280), BF16),
            pltpu.VMEM((2, 96, 1280), BF16),
            pltpu.VMEM((2, 16, 1280), BF16),
            pltpu.VMEM((6, 96, 128), F32),
            pltpu.VMEM((6, 384, 128), F32),
            pltpu.VMEM((6, 384, 128), F32),
            pltpu.VMEM((6, 288, 128), F32),
            pltpu.VMEM((288, C), F32),
            pltpu.VMEM((6, 2, 192, 128), F32),
            pltpu.VMEM((288, C), F32),
            pltpu.VMEM((288, C), BF16),
            pltpu.VMEM((2, 2, ROWS, C), BF16),
            pltpu.VMEM((2, 2, ROWS, C), BF16),
            pltpu.VMEM((2, 16, C), BF16),
            pltpu.VMEM((2, 16, C), BF16),
            pltpu.VMEM((NLON, 8, 896), BF16),
            pltpu.VMEM((NLON, 8, 896), BF16),
            pltpu.VMEM((2, 8, 8, MSG), BF16),
            pltpu.VMEM((2, 8, 8, MSG), BF16),
            pltpu.VMEM((2, 8, 8, MSG), BF16),
            pltpu.VMEM((2, 8, 8, MSG), BF16),
            pltpu.VMEM((NLON, 8, 896), BF16),
            pltpu.VMEM((NLON, 8, 896), BF16),
            pltpu.VMEM((8 * 192, 128), F32),
            pltpu.VMEM((8 * 192, 128), F32),
            pltpu.VMEM((256, 256), BF16),
            pltpu.VMEM((256, 256), BF16),
            pltpu.VMEM((144, 512), F32),
            pltpu.VMEM((144, 512), F32),
            pltpu.VMEM((2, COLS, ROWS, C), BF16),
            dma((18,)),
            dma((4,)),
            dma((4,)),
            dma((NLON,)),
            dma((NLON,)),
            dma((2, 8)),
            dma((2, 8)),
            dma((2, 8)),
            dma((2, 8)),
            dma((NLON,)),
            dma((NLON,)),
        ],
        compiler_params=pltpu.CompilerParams(
            collective_id=0, has_side_effects=True, vmem_limit_bytes=56 * 1024 * 1024
        ),
    )(
        grid.transpose(0, 1, 3, 2), patch_weight, spectral_one, spectral_two, fc_up, fc_down,
        const(feature_table()),
        const(np.stack([pick_table(), fh, bh])), const(fw), const(bw),
        norm_gain_one, spectral_bias, norm_gain_two,
    )
    return out.transpose(0, 2, 1, 3)


def solution(mesh):
    in_specs = (P(None, None, "lat", "lon"), P(), P(), P(), P(), P(), P(), P(), P())
    out_specs = P(None, "lat", "lon", None)
    return jax.shard_map(local, mesh=mesh, in_specs=in_specs, out_specs=out_specs, check_vma=False)
```

```python
import math

import jax
import jax.numpy as jnp
import numpy as np
from jax import lax
from jax.experimental import pallas as pl
from jax.experimental.pallas import tpu as pltpu
from jax.sharding import PartitionSpec as P

MESH = pl.DeviceIdType.MESH
F32 = jnp.float32
BF16 = jnp.bfloat16

NLAT, NLON = 4, 32
NV, C, HID, NB, BS = 20, 768, 3072, 8, 96
H, W, KW = 96, 192, 64
ROWS, COLS = 24, 6
ROW12 = 12
MSG = ROW12 * BS


def pick_table():
    sel = np.zeros((192, 192), np.float32)
    for r8 in range(8):
        for row in range(ROWS):
            sel[r8 * ROWS + row, 8 * row + r8] = 1.0
    return sel


def feature_table():
    table = np.zeros((4, 160, 768), np.float32)
    for r in range(4):
        for v in range(NV):
            for c8 in range(8):
                table[r, v * 8 + c8, (64, 384)[c8 // 4] + v * 16 + 4 * r + c8 % 4] = 1.0
    return table


def lon_tables():
    k = np.arange(KW)
    w = np.arange(W)
    angle = 2.0 * math.pi * ((k[:, None] * w[None, :]) % W) / W
    scale = 1.0 / math.sqrt(W)
    both = np.stack([np.cos(angle), -np.sin(angle)]) * scale
    fwd = both.reshape(2, 8, 2, 4, W).transpose(2, 1, 3, 0, 4).reshape(128, NLON, COLS)
    fwd = np.pad(fwd, ((0, 0), (0, 0), (0, 2))).reshape(128, 256)
    weight = np.where(k == 0, 1.0, 2.0)
    back = both * weight[None, :, None]
    back = back.reshape(2, 8, 2, 4, W).transpose(4, 2, 1, 3, 0).reshape(NLON, COLS, 128)
    back = np.pad(back, ((0, 0), (0, 2), (0, 0))).reshape(256, 128)
    return fwd, back


def lat_tables():
    h = np.arange(H)
    angle = 2.0 * math.pi * ((h[:, None] * h[None, :]) % H) / H
    cos, sin = np.cos(angle) / math.sqrt(H), np.sin(angle) / math.sqrt(H)
    fwd = np.block([[cos, sin], [-sin, cos]])
    back = np.block([[cos, -sin], [sin, cos]])
    return fwd, back


def norm(values, gain):
    centre = jnp.mean(values, axis=-1, keepdims=True)
    off = values - centre
    spread = jnp.mean(jnp.square(off), axis=-1, keepdims=True)
    return off * lax.rsqrt(spread + 1e-05) * gain


def fold(msg):
    row = lax.broadcasted_iota(jnp.int32, msg.shape[:-1] + (128,), msg.ndim - 2)
    tiles = []
    for u in range(7):
        tile = msg[..., 128 * u : 128 * u + 128]
        if u < COLS:
            tile = jnp.where(row == 6, msg[..., u : u + 1, 896:1024], tile)
            tile = jnp.where(row == 7, msg[..., u : u + 1, 1024:], tile)
        tiles.append(tile)
    return jnp.concatenate(tiles, axis=-1)


def unfold(msg):
    row = lax.broadcasted_iota(jnp.int32, msg.shape[:-1] + (128,), msg.ndim - 2)
    last = [jnp.zeros(row.shape, F32)] * 2
    for u in range(COLS):
        for i in range(2):
            piece = msg[..., 6 + i : 7 + i, 128 * u : 128 * u + 128]
            last[i] = jnp.where(row == u, piece, last[i])
    return jnp.concatenate([msg] + last, axis=-1)


def dot(left, right):
    return jnp.dot(left, right, preferred_element_type=F32)


def kernel(
    grid_h, pw_h, one_h, two_h, up_h, down_h, tab_h, sq_h, fw_h, bw_h, g1_h, bias_h, g2_h,
    out_ref,
    sq_v, fw_ref, bw_ref, g1_ref, bias_ref, g2_ref,
    grid_v, pw_v, one_v, two_v, up_v, down_v, tab_v,
    t_v, m_v, lhs_v, side_v, rim_v, te_v, q0_v, q3_v, tot_v, acc_v, nf_v, tn_v, nrm_v,
    ew_s, ew_r, ns_s, ns_r,
    p1_s, p1_r, p2_s, p2_r, p3_s, p3_r, p4_s, p4_r,
    z_v, v_v, w1_v, w2_v, h0_v, h1_v, res_v, x_v,
    lsem, halo_ss, halo_rs, s1, r1, s2, r2, s3, r3, s4, r4,
):
    a = lax.axis_index("lat")
    b = lax.axis_index("lon")
    q = b // 16
    p = b % 16
    row_y = p // 4
    row_z = p % 4
    mine = (row_y + row_z) % 2
    n = 2 * row_y + row_z // 2
    g = 2 * a + q

    barrier = pltpu.get_barrier_semaphore()

    def greet_lon(d, _):
        pl.semaphore_signal(
            barrier, inc=1, device_id=(a, lax.rem(b + d, NLON)), device_id_type=MESH
        )
        return 0

    lax.fori_loop(1, NLON, greet_lon, 0)

    def greet_lat(d, _):
        mate = lax.rem(a + 1 + d // 2, NLAT)
        pl.semaphore_signal(
            barrier, inc=1, device_id=(mate, (d % 2) * 16 + p), device_id_type=MESH
        )
        return 0

    lax.fori_loop(0, 6, greet_lat, 0)
    def load(index, src, dst):
        copy = pltpu.make_async_copy(src, dst, lsem.at[index])
        copy.start()
        return copy

    c_grid = load(0, grid_h, grid_v)
    c_sq = load(10, sq_h, sq_v)
    c_tab = load(1, tab_h, tab_v)
    c_pw = {}
    for i, off in enumerate((0, 3, 1, 2)):
        part = pl.ds(1280 * off, 1280)
        c_pw[off] = load(2 + i, pw_h.at[part], pw_v.at[part])
    c_one = load(6, one_h.at[:, n], one_v)
    c_two = load(7, two_h.at[:, n], two_v)
    small = [
        load(11 + i, src, dst)
        for i, (src, dst) in enumerate(
            ((g1_h, g1_ref), (bias_h, bias_ref), (g2_h, g2_ref), (fw_h, fw_ref), (bw_h, bw_ref))
        )
    ]

    nf_v[:, :, 144:] = jnp.zeros((6, 2, 48, 128), F32)
    for smp in range(2):
        for first in (240 * smp, 240 * smp + 192):
            m_v[:, :, first : first + 48] = jnp.zeros((2, 6, 48, 128), F32)
    for tile in range(6):
        q0_v[tile, pl.ds(0, 12, stride=32), :] = jnp.zeros((12, 128), F32)
        q3_v[tile, pl.ds(31, 12, stride=32), :] = jnp.zeros((12, 128), F32)
    c_grid.wait()
    c_sq.wait()
    for smp in range(2):
        for lp in range(3):
            block = grid_v[smp, :, 16 * lp : 16 * lp + 16, :]
            block = block.astype(F32).reshape(NV, 2, 8, 192)
            for half in range(2):
                x = block[:, half].reshape(NV * 8, 192).astype(BF16)
                turned = lax.dot_general(
                    sq_v[0], x, (((1,), (1,)), ((), ())), preferred_element_type=F32
                )
                first = (6 * smp + 2 * lp + half) * ROWS
                for r8 in range(8):
                    t_v[r8, first : first + ROWS, :] = turned[ROWS * r8 : ROWS * r8 + ROWS]

    c_tab.wait()
    for half in range(2):
        value = dot(t_v[4 * half].astype(BF16), tab_v[0])
        for r in range(1, 4):
            value = value + dot(t_v[4 * half + r].astype(BF16), tab_v[r])
        for tile in range(6):
            lanes = slice(128 * tile, 128 * tile + 128)
            for smp in range(2):
                m_v[half, tile, 240 * smp + 48 : 240 * smp + 192] = value[
                    144 * smp : 144 * smp + 144, lanes
                ]

    places = ((3, 0), (4, 0), (5, 0), (1, 1), (2, 1), (3, 1), (4, 1), (5, 1), (1, 2), (2, 2))
    for half in range(2):
        for tile, (lane, slot) in enumerate(places):
            cols = slice(128 * tile, 128 * tile + 128)
            outer = []
            for smp in range(2):
                first = (10 * smp + slot) * ROWS
                rim = first + (0, ROWS - 1)[half]
                value = m_v[half, lane, first : first + 192, :]
                row = m_v[half, lane, pl.ds(rim, 8, stride=ROWS), :]
                if tile in (2, 7):
                    value = value + m_v[half, 0, first + ROWS : first + ROWS + 192, :]
                    row = row + m_v[half, 0, pl.ds(rim + ROWS, 8, stride=ROWS), :]
                outer.append(row)
                lhs_v[half, 144 * smp : 144 * smp + 144, cols] = value[ROWS:168].astype(BF16)
                side = jnp.concatenate([value[:ROWS], value[168:]], axis=0)
                side_v[half, 48 * smp : 48 * smp + 48, cols] = side.astype(BF16)
            rim_v[half, :, cols] = jnp.concatenate(outer, axis=0).astype(BF16)

    def weight(off, pair):
        return pw_v[1280 * off : 1280 * off + 1280, 256 * pair : 256 * pair + 256]

    for way, (off, half) in enumerate(((0, 1), (3, 0))):
        c_pw[off].wait()
        for pair in range(3):
            value = dot(rim_v[half], weight(off, pair))
            ns_s[way, :, 256 * pair : 256 * pair + 256] = value.astype(BF16)

    pl.semaphore_wait(barrier, NLON - 1 + 6)

    def remote(src, dst, ssem, rsem, dev):
        return pltpu.make_async_remote_copy(
            src_ref=src, dst_ref=dst, send_sem=ssem, recv_sem=rsem,
            device_id=dev, device_id_type=MESH,
        )

    halos = [
        remote(
            src, dst, halo_ss.at[sem], halo_rs.at[sem],
            (lax.rem(a + da, NLAT), lax.rem(b + db, NLON)),
        )
        for src, dst, sem, da, db in (
            [(ns_s.at[i], ns_r.at[i], i, (1, NLAT - 1)[i], 0) for i in range(2)]
            + [
                (ew_s.at[i, smp], ew_r.at[i, smp], 2 + 2 * smp + i, 0, (1, NLON - 1)[i])
                for smp in range(2)
                for i in range(2)
            ]
        )
    ]
    halos[0].start()
    halos[1].start()

    c_pw[1].wait()
    c_pw[2].wait()
    none = jnp.zeros((4, 1, 256), F32)
    for pair in range(3):
        value = dot(side_v[0], weight(1, pair)) + dot(side_v[1], weight(2, pair))
        above = dot(side_v[1], weight(0, pair)).reshape(4, ROWS, 256)
        below = dot(side_v[0], weight(3, pair)).reshape(4, ROWS, 256)
        above = jnp.concatenate([none, above[:, :-1]], axis=1)
        below = jnp.concatenate([below[:, 1:], none], axis=1)
        value = value + (above + below).reshape(96, 256)
        te_v[2 * pair] = value[:, :128]
        te_v[2 * pair + 1] = value[:, 128:]

    def rim_rows(way, cols, picks):
        rows = ns_r[way, :, cols].astype(F32)
        rows = jnp.concatenate([rows[lo:hi] for lo, hi in picks], axis=0)
        return jnp.where((a > 0, a < NLAT - 1)[way], rows, 0.0)

    halos[0].wait_recv()
    halos[1].wait_recv()
    for tile in range(6):
        cols = slice(128 * tile, 128 * tile + 128)
        for way in range(2):
            at = pl.ds((0, ROWS - 1)[way], 4, stride=ROWS)
            te_v[tile, at, :] += rim_rows(way, cols, ((0, 1), (7, 8), (8, 9), (15, 16)))
    for smp in range(2):
        for way in range(2):
            first = ROWS * (2 * smp + 1 - way)
            for tile in range(6):
                cols = slice(128 * tile, 128 * tile + 128)
                ew_s[way, smp, :, cols] = te_v[tile, first : first + ROWS, :].astype(BF16)
            halos[2 + 2 * smp + way].start()

    for pair in range(3):
        for off, half, out_v, lead in ((0, 1, q0_v, 1), (3, 0, q3_v, 7)):
            value = dot(lhs_v[half], weight(off, pair))
            for lane in range(2):
                lanes = slice(128 * lane, 128 * lane + 128)
                for m in range(12):
                    out_v[2 * pair + lane, 32 * m + lead : 32 * m + lead + ROWS, :] = value[
                        ROWS * m : ROWS * m + ROWS, lanes
                    ]
        value = dot(lhs_v[0], weight(1, pair)) + dot(lhs_v[1], weight(2, pair))
        for lane in range(2):
            tile = 2 * pair + lane
            shifted = (
                q0_v[tile].reshape(12, 32, 128)[:, :ROWS] + q3_v[tile].reshape(12, 32, 128)[:, 8:]
            )
            tot_v[tile] = value[:, 128 * lane : 128 * lane + 128] + shifted.reshape(288, 128)
    c_up = load(8, up_h, up_v)
    c_down = load(9, down_h, down_v)
    for tile in range(6):
        cols = slice(128 * tile, 128 * tile + 128)
        for way in range(2):
            at = pl.ds((0, ROWS - 1)[way], 12, stride=ROWS)
            tot_v[tile, at, :] += rim_rows(way, cols, ((1, 7), (9, 15)))
    for copy in small:
        copy.wait()

    def owner(part, smp, blk):
        return part * 16 + (blk // 2) * 4 + (blk % 2) * 2 + (smp + blk // 2) % 2

    for smp in range(2):
        rows = slice(144 * smp, 144 * smp + 144)
        for way, j in ((0, 0), (1, COLS - 1)):
            halos[2 + 2 * smp + way].wait_recv()
            first = ROWS * (COLS * smp + j)
            for tile in range(6):
                cols = slice(128 * tile, 128 * tile + 128)
                tot_v[tile, first : first + ROWS, :] += ew_r[way, smp, :, cols].astype(F32)
        tok = jnp.concatenate([tot_v[t, rows, :] for t in range(6)], axis=1)
        tok = tok.astype(BF16).astype(F32)
        normed = norm(tok, g1_ref[...].reshape(1, C)).astype(BF16).astype(F32)
        tn_v[rows, :] = tok + normed
        for tile in range(6):
            nf_v[tile, smp, :144] = normed[:, 128 * tile : 128 * tile + 128]
        for part in range(2):
            planes = [
                jnp.concatenate(
                    [nf_v[t, smp, pl.ds(part * ROW12 + i, 8, stride=ROWS), :] for t in range(6)],
                    axis=1,
                )
                for i in range(ROW12)
            ]
            for blk in range(NB):
                msg = jnp.concatenate(
                    [plane[:, BS * blk : BS * blk + BS] for plane in planes], axis=1
                )
                p1_s[owner(part, smp, blk)] = fold(msg).astype(BF16)
        odd = (smp + mine) % 2
        for dx in (1, 0):
            for dy in (2, 1, 3, 0):
                for dz in (2, 0):
                    dest = (
                        ((q + dx) % 2) * 16 + ((row_y + dy) % 4) * 4 + (row_z + dz + (odd + dy) % 2) % 4
                    )

                    def send(dest=dest):
                        remote(
                            p1_s.at[dest], p1_r.at[b], s1.at[dest], r1.at[b], (a, dest)
                        ).start()

                    if (dx, dy, dz) == (0, 0, 0):
                        pl.when(odd == 1)(send)
                    else:
                        send()
    p1_r[b] = p1_s[b]

    c_one.wait()
    c_two.wait()
    for src, dst in ((one_v, w1_v), (two_v, w2_v)):
        dst[...] = jnp.zeros_like(dst)
        dst[0:BS, 0:BS] = src[0].astype(BF16)
        dst[0:BS, 128 : 128 + BS] = src[1].astype(BF16)
        dst[128 : 128 + BS, 0:BS] = -src[1].astype(BF16)
        dst[128 : 128 + BS, 128 : 128 + BS] = src[0].astype(BF16)
    bias = jnp.zeros((1, 256), F32)
    for blk in range(NB):
        parts = []
        for ri in range(2):
            parts.append(bias_ref[ri : ri + 1, BS * blk : BS * blk + BS])
            parts.append(jnp.zeros((1, 32), F32))
        bias = bias + jnp.where(n == blk, jnp.concatenate(parts, axis=1), 0.0)

    def take1(d, _):
        src = lax.rem(b + d, NLON)

        @pl.when(d > 0)
        def _():
            remote(p1_s.at[src], p1_r.at[src], s1.at[src], r1.at[src], (a, src)).wait_recv()

        at = pl.ds(pl.multiple_of(8 * src, 8), 8)
        x_v[at, :] = unfold(p1_r[src].astype(F32))
        return 0

    lax.fori_loop(0, NLON, take1, 0)

    def mate_of(d):
        other = lax.rem(g + d, 8)
        return other, (other // 2, (other % 2) * 16 + p)

    x = x_v[...].astype(BF16)
    for kh in range(2):
        part = dot(fw_ref[64 * kh : 64 * kh + 64, :], x)
        p2_s[kh] = part.reshape(8, 8, MSG).astype(BF16)
        for d in range(1, 8):
            other, dev = mate_of(d)
            remote(
                p2_s.at[kh, other], p2_r.at[kh, g], s2.at[kh, other], r2.at[kh, g], dev
            ).start()

    def spread(kh, src, value):
        for i in range(ROW12):
            piece = value[:, BS * i : BS * i + BS]
            piece = jnp.concatenate([piece, jnp.zeros((8, 128 - BS), F32)], axis=1)
            z_v[pl.ds(768 * kh + ROW12 * src + i, 8, stride=H), :] = piece

    def gather(kh, dest):
        pieces = [
            v_v[pl.ds(768 * kh + ROW12 * dest + i, 8, stride=H), :][:, :BS] for i in range(ROW12)
        ]
        return jnp.concatenate(pieces, axis=1).astype(BF16)

    for kh in range(2):
        spread(kh, g, p2_s[kh, g].astype(F32))

        def take2(d, _):
            other, dev = mate_of(d)
            remote(
                p2_s.at[kh, other], p2_r.at[kh, other], s2.at[kh, other], r2.at[kh, other], dev
            ).wait_recv()
            spread(kh, other, p2_r[kh, other].astype(F32))
            return 0

        lax.fori_loop(1, 8, take2, 0)

        base = 768 * kh
        z = jnp.concatenate(
            [z_v[base + 192 * k : base + 192 * k + 192, :] for k in range(4)], axis=1
        )
        spec = dot(sq_v[1], z.astype(BF16))
        modes = jnp.concatenate(
            [
                jnp.concatenate(
                    [spec[:H, 128 * k : 128 * k + 128], spec[H:, 128 * k : 128 * k + 128]], axis=1
                )
                for k in range(4)
            ],
            axis=0,
        )
        mid = jnp.maximum(dot(modes.astype(BF16), w1_v[...]) + bias, 0.0)
        res = dot(mid.astype(BF16), w2_v[...])
        res = res - jnp.clip(res, -0.01, 0.01)
        back = jnp.concatenate(
            [
                jnp.concatenate(
                    [res[H * k : H * k + H, :128], res[H * k : H * k + H, 128:]], axis=0
                )
                for k in range(4)
            ],
            axis=1,
        )
        rows = dot(sq_v[2], back.astype(BF16))
        for k in range(4):
            v_v[base + 192 * k : base + 192 * k + 192, :] = rows[:, 128 * k : 128 * k + 128]

        def send3(d, _):
            other, dev = mate_of(d)
            p3_s[kh, other] = gather(kh, other)
            remote(
                p3_s.at[kh, other], p3_r.at[kh, g], s3.at[kh, other], r3.at[kh, g], dev
            ).start()
            return 0

        lax.fori_loop(1, 8, send3, 0)
        p3_r[kh, g] = gather(kh, g)

    def wait3(d, _):
        other, dev = mate_of(d)
        for kh in range(2):
            remote(
                p3_s.at[kh, other], p3_r.at[kh, other], s3.at[kh, other], r3.at[kh, other], dev
            ).wait_recv()
        return 0

    lax.fori_loop(1, 8, wait3, 0)

    spectra = p3_r[...].astype(F32).reshape(128, MSG).astype(BF16)
    for dx in (1, 0):
        other = (q + dx) % 2
        field = dot(bw_ref[pl.ds(pl.multiple_of(128 * other, 128), 128), :], spectra)
        p4_s[pl.ds(16 * other, 16)] = fold(field.reshape(16, 8, MSG)).astype(BF16)
        steps = [(dy, dz) for dy in range(4) for dz in range(4)]
        steps.sort(key=lambda t: -(min(t[0], 4 - t[0]) + min(t[1], 4 - t[1])))
        for dy, dz in steps:
            if (dx, dy, dz) != (0, 0, 0):
                dest = 16 * other + ((row_y + dy) % 4) * 4 + (row_z + dz) % 4
                remote(p4_s.at[dest], p4_r.at[b], s4.at[dest], r4.at[b], (a, dest)).start()
    p4_r[b] = p4_s[b]

    for copy in halos:
        copy.wait_send()

    def drain1(d, _):
        dest = lax.rem(b + d, NLON)
        remote(p1_s.at[dest], p1_r.at[b], s1.at[dest], r1.at[b], (a, dest)).wait_send()
        return 0

    lax.fori_loop(1, NLON, drain1, 0)

    def drain_lat(d, _):
        other, dev = mate_of(d)
        for kh in range(2):
            remote(
                p2_s.at[kh, other], p2_r.at[kh, g], s2.at[kh, other], r2.at[kh, g], dev
            ).wait_send()
            remote(
                p3_s.at[kh, other], p3_r.at[kh, g], s3.at[kh, other], r3.at[kh, g], dev
            ).wait_send()
        return 0

    lax.fori_loop(1, 8, drain_lat, 0)
    c_up.wait()
    c_down.wait()
    results = []
    for smp in range(2):
        def join(part, _):
            for blk in range(NB):
                src = owner(part, smp, blk)

                @pl.when(src != b)
                def _(src=src):
                    remote(
                        p4_s.at[src], p4_r.at[src], s4.at[src], r4.at[src], (a, src)
                    ).wait_recv()

            msgs = [unfold(p4_r[owner(part, smp, blk)].astype(F32)) for blk in range(NB)]
            for i in range(ROW12):
                plane = jnp.concatenate([m[:, BS * i : BS * i + BS] for m in msgs], axis=1)
                for tile in range(6):
                    nf_v[tile, smp, pl.ds(part * ROW12 + i, 8, stride=ROWS), :] = plane[
                        :, 128 * tile : 128 * tile + 128
                    ]
            return 0

        lax.fori_loop(0, 2, join, 0)
        rows = slice(144 * smp, 144 * smp + 144)
        field = jnp.concatenate([nf_v[tile, smp, :144] for tile in range(6)], axis=1)
        middle = (field + tn_v[rows, :]).astype(BF16).astype(F32)
        acc_v[rows, :] = middle
        nrm_v[rows, :] = norm(middle, g2_ref[...].reshape(1, C)).astype(BF16)

        def up(step):
            return dot(nrm_v[rows, :], up_v[:, pl.ds(pl.multiple_of(step * 512, 512), 512)])

        def down(hidden, step):
            hidden = 0.5 * hidden * (1.0 + lax.erf(hidden * (1.0 / math.sqrt(2.0))))
            part = pl.ds(pl.multiple_of(step * 512, 512), 512)
            return dot(hidden.astype(BF16), down_v[part, :])

        h0_v[...] = up(0)

        def mlp(it, _):
            step = 2 * it
            h1_v[...] = up(step + 1)
            acc_v[rows, :] += down(h0_v[...], step)
            h0_v[...] = up(jnp.minimum(step + 2, HID // 512 - 1))
            acc_v[rows, :] += down(h1_v[...], step + 1)
            return 0

        lax.fori_loop(0, HID // 1024, mlp, 0)
        res_v[smp] = acc_v[rows, :].reshape(COLS, ROWS, C).astype(BF16)
        results.append(load(16 + smp, res_v.at[smp], out_ref.at[smp]))

    def drain4(d, _):
        dest = lax.rem(b + d, NLON)
        remote(p4_s.at[dest], p4_r.at[b], s4.at[dest], r4.at[b], (a, dest)).wait_send()
        return 0

    lax.fori_loop(1, NLON, drain4, 0)
    for copy in results:
        copy.wait()


def local(
    grid, patch_weight, norm_gain_one, spectral_one, spectral_bias, spectral_two,
    norm_gain_two, fc_up, fc_down,
):
    fw, bw = lon_tables()
    fh, bh = lat_tables()
    const = lambda x: jnp.asarray(x, F32).astype(BF16)
    any_spec = pl.BlockSpec(memory_space=pl.ANY)
    dma = pltpu.SemaphoreType.DMA
    out = pl.pallas_call(
        kernel,
        out_shape=jax.ShapeDtypeStruct((2, COLS, ROWS, C), BF16),
        in_specs=[any_spec] * 13,
        out_specs=any_spec,
        scratch_shapes=[
            pltpu.VMEM((3, 192, 192), BF16),
            pltpu.VMEM((128, 256), BF16),
            pltpu.VMEM((256, 128), BF16),
            pltpu.VMEM((C,), F32),
            pltpu.VMEM((2, C), F32),
            pltpu.VMEM((C,), F32),
            pltpu.VMEM((2, NV, 48, 192), BF16),
            pltpu.VMEM((5120, C), BF16),
            pltpu.VMEM((2, BS, BS), F32),
            pltpu.VMEM((2, BS, BS), F32),
            pltpu.VMEM((C, HID), BF16),
            pltpu.VMEM((HID, C), BF16),
            pltpu.VMEM((4, 160, 768), BF16),
            pltpu.VMEM((8, 288, 160), F32),
            pltpu.VMEM((2, 6, 480, 128), F32),
            pltpu.VMEM((2, 288, 1280), BF16),
            pltpu.VMEM((2, 96, 1280), BF16),
            pltpu.VMEM((2, 16, 1280), BF16),
            pltpu.VMEM((6, 96, 128), F32),
            pltpu.VMEM((6, 384, 128), F32),
            pltpu.VMEM((6, 384, 128), F32),
            pltpu.VMEM((6, 288, 128), F32),
            pltpu.VMEM((288, C), F32),
            pltpu.VMEM((6, 2, 192, 128), F32),
            pltpu.VMEM((288, C), F32),
            pltpu.VMEM((288, C), BF16),
            pltpu.VMEM((2, 2, ROWS, C), BF16),
            pltpu.VMEM((2, 2, ROWS, C), BF16),
            pltpu.VMEM((2, 16, C), BF16),
            pltpu.VMEM((2, 16, C), BF16),
            pltpu.VMEM((NLON, 8, 896), BF16),
            pltpu.VMEM((NLON, 8, 896), BF16),
            pltpu.VMEM((2, 8, 8, MSG), BF16),
            pltpu.VMEM((2, 8, 8, MSG), BF16),
            pltpu.VMEM((2, 8, 8, MSG), BF16),
            pltpu.VMEM((2, 8, 8, MSG), BF16),
            pltpu.VMEM((NLON, 8, 896), BF16),
            pltpu.VMEM((NLON, 8, 896), BF16),
            pltpu.VMEM((8 * 192, 128), F32),
            pltpu.VMEM((8 * 192, 128), F32),
            pltpu.VMEM((256, 256), BF16),
            pltpu.VMEM((256, 256), BF16),
            pltpu.VMEM((144, 512), F32),
            pltpu.VMEM((144, 512), F32),
            pltpu.VMEM((2, COLS, ROWS, C), BF16),
            pltpu.VMEM((256, MSG), F32),
            dma((18,)),
            dma((6,)),
            dma((6,)),
            dma((NLON,)),
            dma((NLON,)),
            dma((2, 8)),
            dma((2, 8)),
            dma((2, 8)),
            dma((2, 8)),
            dma((NLON,)),
            dma((NLON,)),
        ],
        compiler_params=pltpu.CompilerParams(
            collective_id=0, has_side_effects=True, vmem_limit_bytes=56 * 1024 * 1024
        ),
    )(
        grid.transpose(0, 1, 3, 2), patch_weight, spectral_one, spectral_two, fc_up, fc_down,
        const(feature_table()),
        const(np.stack([pick_table(), fh, bh])), const(fw), const(bw),
        norm_gain_one, spectral_bias, norm_gain_two,
    )
    return out.transpose(0, 2, 1, 3)


def solution(mesh):
    in_specs = (P(None, None, "lat", "lon"), P(), P(), P(), P(), P(), P(), P(), P())
    out_specs = P(None, "lat", "lon", None)
    return jax.shard_map(local, mesh=mesh, in_specs=in_specs, out_specs=out_specs, check_vma=False)
```

```python
import math

import jax
import jax.numpy as jnp
import numpy as np
from jax import lax
from jax.experimental import pallas as pl
from jax.experimental.pallas import tpu as pltpu
from jax.sharding import PartitionSpec as P

MESH = pl.DeviceIdType.MESH
F32 = jnp.float32
BF16 = jnp.bfloat16

NLAT, NLON = 4, 32
NV, C, HID, NB, BS = 20, 768, 3072, 8, 96
H, W, KW = 96, 192, 64
ROWS, COLS = 24, 6
ROW12 = 12
MSG = ROW12 * BS


def pick_table():
    sel = np.zeros((192, 192), np.float32)
    for r8 in range(8):
        for row in range(ROWS):
            sel[r8 * ROWS + row, 8 * row + r8] = 1.0
    return sel


def feature_table():
    table = np.zeros((4, 160, 768), np.float32)
    for r in range(4):
        for v in range(NV):
            for c8 in range(8):
                table[r, v * 8 + c8, (64, 384)[c8 // 4] + v * 16 + 4 * r + c8 % 4] = 1.0
    return table


def lon_tables():
    k = np.arange(KW)
    w = np.arange(W)
    angle = 2.0 * math.pi * ((k[:, None] * w[None, :]) % W) / W
    scale = 1.0 / math.sqrt(W)
    both = np.stack([np.cos(angle), -np.sin(angle)]) * scale
    fwd = both.reshape(2, 8, 2, 4, W).transpose(2, 1, 3, 0, 4).reshape(128, NLON, COLS)
    fwd = np.pad(fwd, ((0, 0), (0, 0), (0, 2))).reshape(128, 256)
    weight = np.where(k == 0, 1.0, 2.0)
    back = both * weight[None, :, None]
    back = back.reshape(2, 8, 2, 4, W).transpose(4, 2, 1, 3, 0).reshape(NLON, COLS, 128)
    back = np.pad(back, ((0, 0), (0, 2), (0, 0))).reshape(256, 128)
    return fwd, back


def lat_tables():
    h = np.arange(H)
    angle = 2.0 * math.pi * ((h[:, None] * h[None, :]) % H) / H
    cos, sin = np.cos(angle) / math.sqrt(H), np.sin(angle) / math.sqrt(H)
    fwd = np.block([[cos, sin], [-sin, cos]])
    back = np.block([[cos, -sin], [sin, cos]])
    return fwd, back


def norm(values, gain):
    centre = jnp.mean(values, axis=-1, keepdims=True)
    off = values - centre
    spread = jnp.mean(jnp.square(off), axis=-1, keepdims=True)
    return off * lax.rsqrt(spread + 1e-05) * gain


def fold(msg):
    row = lax.broadcasted_iota(jnp.int32, msg.shape[:-1] + (128,), msg.ndim - 2)
    tiles = []
    for u in range(7):
        tile = msg[..., 128 * u : 128 * u + 128]
        if u < COLS:
            tile = jnp.where(row == 6, msg[..., u : u + 1, 896:1024], tile)
            tile = jnp.where(row == 7, msg[..., u : u + 1, 1024:], tile)
        tiles.append(tile)
    return jnp.concatenate(tiles, axis=-1)


def unfold(msg):
    row = lax.broadcasted_iota(jnp.int32, msg.shape[:-1] + (128,), msg.ndim - 2)
    last = [jnp.zeros(row.shape, F32)] * 2
    for u in range(COLS):
        for i in range(2):
            piece = msg[..., 6 + i : 7 + i, 128 * u : 128 * u + 128]
            last[i] = jnp.where(row == u, piece, last[i])
    return jnp.concatenate([msg] + last, axis=-1)


def dot(left, right):
    return jnp.dot(left, right, preferred_element_type=F32)


def kernel(
    grid_h, pw_h, one_h, two_h, up_h, down_h, tab_h, sq_h, fw_h, bw_h, g1_h, bias_h, g2_h,
    out_ref,
    sq_v, fw_ref, bw_ref, g1_ref, bias_ref, g2_ref,
    grid_v, pw_v, one_v, two_v, up_v, down_v, tab_v,
    t_v, m_v, lhs_v, side_v, rim_v, q0_v, q3_v, tot_v, acc_v, nf_v, tn_v, nrm_v,
    ew_s, ew_r, ns_s, ns_r,
    p1_s, p1_r, p2_s, p2_r, p3_s, p3_r, p4_s, p4_r,
    z_v, v_v, w1_v, w2_v, h0_v, h1_v, res_v, x_v,
    lsem, halo_ss, halo_rs, s1, r1, s2, r2, s3, r3, s4, r4,
):
    a = lax.axis_index("lat")
    b = lax.axis_index("lon")
    q = b // 16
    p = b % 16
    row_y = p // 4
    row_z = p % 4
    mine = (row_y + row_z) % 2
    n = 2 * row_y + row_z // 2
    g = 2 * a + q

    barrier = pltpu.get_barrier_semaphore()

    def greet_lon(d, _):
        pl.semaphore_signal(
            barrier, inc=1, device_id=(a, lax.rem(b + d, NLON)), device_id_type=MESH
        )
        return 0

    lax.fori_loop(1, NLON, greet_lon, 0)

    def greet_lat(d, _):
        mate = lax.rem(a + 1 + d // 2, NLAT)
        pl.semaphore_signal(
            barrier, inc=1, device_id=(mate, (d % 2) * 16 + p), device_id_type=MESH
        )
        return 0

    lax.fori_loop(0, 6, greet_lat, 0)
    for da in (1, NLAT - 1):
        for db in (1, NLON - 1):
            corner = (lax.rem(a + da, NLAT), lax.rem(b + db, NLON))
            pl.semaphore_signal(barrier, inc=1, device_id=corner, device_id_type=MESH)
    def load(index, src, dst):
        copy = pltpu.make_async_copy(src, dst, lsem.at[index])
        copy.start()
        return copy

    c_grid = load(0, grid_h, grid_v)
    c_sq = load(10, sq_h, sq_v)
    c_tab = load(1, tab_h, tab_v)
    c_pw = {}
    for i, off in enumerate((0, 3, 1, 2)):
        part = pl.ds(1280 * off, 1280)
        c_pw[off] = load(2 + i, pw_h.at[part], pw_v.at[part])
    c_one = load(6, one_h.at[:, n], one_v)
    c_two = load(7, two_h.at[:, n], two_v)
    small = [
        load(11 + i, src, dst)
        for i, (src, dst) in enumerate(
            ((g1_h, g1_ref), (bias_h, bias_ref), (g2_h, g2_ref), (fw_h, fw_ref), (bw_h, bw_ref))
        )
    ]

    nf_v[:, :, 144:] = jnp.zeros((6, 2, 48, 128), F32)
    for smp in range(2):
        for first in (240 * smp, 240 * smp + 192):
            m_v[:, :, first : first + 48] = jnp.zeros((2, 6, 48, 128), F32)
    for tile in range(6):
        q0_v[tile, pl.ds(0, 12, stride=32), :] = jnp.zeros((12, 128), F32)
        q3_v[tile, pl.ds(31, 12, stride=32), :] = jnp.zeros((12, 128), F32)
    c_grid.wait()
    c_sq.wait()
    for smp in range(2):
        for lp in range(3):
            block = grid_v[smp, :, 16 * lp : 16 * lp + 16, :]
            block = block.astype(F32).reshape(NV, 2, 8, 192)
            for half in range(2):
                x = block[:, half].reshape(NV * 8, 192).astype(BF16)
                turned = lax.dot_general(
                    sq_v[0], x, (((1,), (1,)), ((), ())), preferred_element_type=F32
                )
                first = (6 * smp + 2 * lp + half) * ROWS
                for r8 in range(8):
                    t_v[r8, first : first + ROWS, :] = turned[ROWS * r8 : ROWS * r8 + ROWS]

    c_tab.wait()
    for half in range(2):
        value = dot(t_v[4 * half].astype(BF16), tab_v[0])
        for r in range(1, 4):
            value = value + dot(t_v[4 * half + r].astype(BF16), tab_v[r])
        for tile in range(6):
            lanes = slice(128 * tile, 128 * tile + 128)
            for smp in range(2):
                m_v[half, tile, 240 * smp + 48 : 240 * smp + 192] = value[
                    144 * smp : 144 * smp + 144, lanes
                ]

    places = ((3, 0), (4, 0), (5, 0), (1, 1), (2, 1), (3, 1), (4, 1), (5, 1), (1, 2), (2, 2))
    for half in range(2):
        for tile, (lane, slot) in enumerate(places):
            cols = slice(128 * tile, 128 * tile + 128)
            outer = []
            for smp in range(2):
                first = (10 * smp + slot) * ROWS
                rim = first + (0, ROWS - 1)[half]
                value = m_v[half, lane, first : first + 192, :]
                row = m_v[half, lane, pl.ds(rim, 8, stride=ROWS), :]
                if tile in (2, 7):
                    value = value + m_v[half, 0, first + ROWS : first + ROWS + 192, :]
                    row = row + m_v[half, 0, pl.ds(rim + ROWS, 8, stride=ROWS), :]
                outer.append(row)
                lhs_v[half, 144 * smp : 144 * smp + 144, cols] = value[ROWS:168].astype(BF16)
                if tile < 3 or tile >= 7:
                    side = jnp.concatenate([value[:ROWS], value[168:]], axis=0)
                    at = 128 * (tile if tile < 3 else tile - 4)
                    side_v[half, 48 * smp : 48 * smp + 48, at : at + 128] = side.astype(BF16)
            rim_v[half, :, cols] = jnp.concatenate(outer, axis=0).astype(BF16)

    def weight(off, pair):
        return pw_v[1280 * off : 1280 * off + 1280, 256 * pair : 256 * pair + 256]

    for way, (off, half) in enumerate(((0, 1), (3, 0))):
        c_pw[off].wait()
        for pair in range(3):
            value = dot(rim_v[half], weight(off, pair))
            ns_s[way, :, 256 * pair : 256 * pair + 256] = value.astype(BF16)

    pl.semaphore_wait(barrier, NLON - 1 + 6 + 4)

    def remote(src, dst, ssem, rsem, dev):
        return pltpu.make_async_remote_copy(
            src_ref=src, dst_ref=dst, send_sem=ssem, recv_sem=rsem,
            device_id=dev, device_id_type=MESH,
        )

    halos = [
        remote(
            src, dst, halo_ss.at[sem], halo_rs.at[sem],
            (lax.rem(a + da, NLAT), lax.rem(b + db, NLON)),
        )
        for src, dst, sem, da, db in (
            [
                (ns_s.at[i], ns_r.at[3 * i + side], 3 * i + side, (1, NLAT - 1)[i], db)
                for i in range(2)
                for side, db in enumerate((0, 1, NLON - 1))
            ]
            + [
                (ew_s.at[i, smp], ew_r.at[i, smp], 6 + 2 * smp + i, 0, (1, NLON - 1)[i])
                for smp in range(2)
                for i in range(2)
            ]
        )
    ]
    for copy in halos[:6]:
        copy.start()

    c_pw[1].wait()
    c_pw[2].wait()
    none = jnp.zeros((4, 1, 256), F32)

    def outer_weight(off, pair):
        cols = slice(256 * pair, 256 * pair + 256)
        first = 1280 * off
        return jnp.concatenate(
            [pw_v[first : first + 384, cols], pw_v[first + 896 : first + 1280, cols]], axis=0
        )

    for pair in range(3):
        value = dot(side_v[0], outer_weight(1, pair)) + dot(side_v[1], outer_weight(2, pair))
        above = dot(side_v[1], outer_weight(0, pair)).reshape(4, ROWS, 256)
        below = dot(side_v[0], outer_weight(3, pair)).reshape(4, ROWS, 256)
        above = jnp.concatenate([none, above[:, :-1]], axis=1)
        below = jnp.concatenate([below[:, 1:], none], axis=1)
        value = (value + (above + below).reshape(96, 256)).astype(BF16)
        for smp in range(2):
            for way in range(2):
                first = ROWS * (2 * smp + 1 - way)
                ew_s[way, smp, :, 256 * pair : 256 * pair + 256] = value[first : first + ROWS]
    for copy in halos[6:]:
        copy.start()

    def rim_rows(way, cols):
        straight, west, east = [ns_r[3 * way + side, :, cols].astype(F32) for side in range(3)]
        none = jnp.zeros((4, 128), F32)
        value = jnp.concatenate([straight[1:7], straight[9:15]], axis=0)
        value = value + jnp.concatenate(
            [west[7:8], none, east[0:1], west[15:16], none, east[8:9]], axis=0
        )
        return jnp.where((a > 0, a < NLAT - 1)[way], value, 0.0)

    for pair in range(3):
        for off, half, out_v, lead in ((0, 1, q0_v, 1), (3, 0, q3_v, 7)):
            value = dot(lhs_v[half], weight(off, pair))
            for lane in range(2):
                lanes = slice(128 * lane, 128 * lane + 128)
                for m in range(12):
                    out_v[2 * pair + lane, 32 * m + lead : 32 * m + lead + ROWS, :] = value[
                        ROWS * m : ROWS * m + ROWS, lanes
                    ]
        value = dot(lhs_v[0], weight(1, pair)) + dot(lhs_v[1], weight(2, pair))
        for lane in range(2):
            tile = 2 * pair + lane
            shifted = (
                q0_v[tile].reshape(12, 32, 128)[:, :ROWS] + q3_v[tile].reshape(12, 32, 128)[:, 8:]
            )
            tot_v[tile] = value[:, 128 * lane : 128 * lane + 128] + shifted.reshape(288, 128)
    c_up = load(8, up_h, up_v)
    c_down = load(9, down_h, down_v)
    for copy in halos[:6]:
        copy.wait_recv()
    for tile in range(6):
        cols = slice(128 * tile, 128 * tile + 128)
        for way in range(2):
            at = pl.ds((0, ROWS - 1)[way], 12, stride=ROWS)
            tot_v[tile, at, :] += rim_rows(way, cols)
    for copy in small:
        copy.wait()

    def owner(part, smp, blk):
        return part * 16 + (blk // 2) * 4 + (blk % 2) * 2 + (smp + blk // 2) % 2

    for smp in range(2):
        rows = slice(144 * smp, 144 * smp + 144)
        for way, j in ((0, 0), (1, COLS - 1)):
            halos[6 + 2 * smp + way].wait_recv()
            first = ROWS * (COLS * smp + j)
            for tile in range(6):
                cols = slice(128 * tile, 128 * tile + 128)
                tot_v[tile, first : first + ROWS, :] += ew_r[way, smp, :, cols].astype(F32)
        tok = jnp.concatenate([tot_v[t, rows, :] for t in range(6)], axis=1)
        tok = tok.astype(BF16).astype(F32)
        normed = norm(tok, g1_ref[...].reshape(1, C)).astype(BF16).astype(F32)
        tn_v[rows, :] = tok + normed
        for tile in range(6):
            nf_v[tile, smp, :144] = normed[:, 128 * tile : 128 * tile + 128]
        for part in range(2):
            planes = [
                jnp.concatenate(
                    [nf_v[t, smp, pl.ds(part * ROW12 + i, 8, stride=ROWS), :] for t in range(6)],
                    axis=1,
                )
                for i in range(ROW12)
            ]
            for blk in range(NB):
                msg = jnp.concatenate(
                    [plane[:, BS * blk : BS * blk + BS] for plane in planes], axis=1
                )
                p1_s[owner(part, smp, blk)] = fold(msg).astype(BF16)
        odd = (smp + mine) % 2
        for dx in (1, 0):
            for dy in (2, 1, 3, 0):
                for dz in (2, 0):
                    dest = (
                        ((q + dx) % 2) * 16 + ((row_y + dy) % 4) * 4 + (row_z + dz + (odd + dy) % 2) % 4
                    )

                    def send(dest=dest):
                        remote(
                            p1_s.at[dest], p1_r.at[b], s1.at[dest], r1.at[b], (a, dest)
                        ).start()

                    if (dx, dy, dz) == (0, 0, 0):
                        pl.when(odd == 1)(send)
                    else:
                        send()
    p1_r[b] = p1_s[b]

    c_one.wait()
    c_two.wait()
    for src, dst in ((one_v, w1_v), (two_v, w2_v)):
        dst[...] = jnp.zeros_like(dst)
        dst[0:BS, 0:BS] = src[0].astype(BF16)
        dst[0:BS, 128 : 128 + BS] = src[1].astype(BF16)
        dst[128 : 128 + BS, 0:BS] = -src[1].astype(BF16)
        dst[128 : 128 + BS, 128 : 128 + BS] = src[0].astype(BF16)
    bias = jnp.zeros((1, 256), F32)
    for blk in range(NB):
        parts = []
        for ri in range(2):
            parts.append(bias_ref[ri : ri + 1, BS * blk : BS * blk + BS])
            parts.append(jnp.zeros((1, 32), F32))
        bias = bias + jnp.where(n == blk, jnp.concatenate(parts, axis=1), 0.0)

    def take1(d, _):
        src = lax.rem(b + d, NLON)

        @pl.when(d > 0)
        def _():
            remote(p1_s.at[src], p1_r.at[src], s1.at[src], r1.at[src], (a, src)).wait_recv()

        at = pl.ds(pl.multiple_of(8 * src, 8), 8)
        x_v[at, :] = unfold(p1_r[src].astype(F32))
        return 0

    lax.fori_loop(0, NLON, take1, 0)

    def mate_of(d):
        other = lax.rem(g + d, 8)
        return other, (other // 2, (other % 2) * 16 + p)

    x = x_v[...].astype(BF16)
    for kh in range(2):
        part = dot(fw_ref[64 * kh : 64 * kh + 64, :], x)
        p2_s[kh] = part.reshape(8, 8, MSG).astype(BF16)
        for d in range(1, 8):
            other, dev = mate_of(d)
            remote(
                p2_s.at[kh, other], p2_r.at[kh, g], s2.at[kh, other], r2.at[kh, g], dev
            ).start()

    def spread(kh, src, value):
        for i in range(ROW12):
            piece = value[:, BS * i : BS * i + BS]
            piece = jnp.concatenate([piece, jnp.zeros((8, 128 - BS), F32)], axis=1)
            z_v[pl.ds(768 * kh + ROW12 * src + i, 8, stride=H), :] = piece

    def gather(kh, dest):
        pieces = [
            v_v[pl.ds(768 * kh + ROW12 * dest + i, 8, stride=H), :][:, :BS] for i in range(ROW12)
        ]
        return jnp.concatenate(pieces, axis=1).astype(BF16)

    for kh in range(2):
        spread(kh, g, p2_s[kh, g].astype(F32))

        def take2(d, _):
            other, dev = mate_of(d)
            remote(
                p2_s.at[kh, other], p2_r.at[kh, other], s2.at[kh, other], r2.at[kh, other], dev
            ).wait_recv()
            spread(kh, other, p2_r[kh, other].astype(F32))
            return 0

        lax.fori_loop(1, 8, take2, 0)

        base = 768 * kh
        z = jnp.concatenate(
            [z_v[base + 192 * k : base + 192 * k + 192, :] for k in range(4)], axis=1
        )
        spec = dot(sq_v[1], z.astype(BF16))
        modes = jnp.concatenate(
            [
                jnp.concatenate(
                    [spec[:H, 128 * k : 128 * k + 128], spec[H:, 128 * k : 128 * k + 128]], axis=1
                )
                for k in range(4)
            ],
            axis=0,
        )
        mid = jnp.maximum(dot(modes.astype(BF16), w1_v[...]) + bias, 0.0)
        res = dot(mid.astype(BF16), w2_v[...])
        res = res - jnp.clip(res, -0.01, 0.01)
        back = jnp.concatenate(
            [
                jnp.concatenate(
                    [res[H * k : H * k + H, :128], res[H * k : H * k + H, 128:]], axis=0
                )
                for k in range(4)
            ],
            axis=1,
        )
        rows = dot(sq_v[2], back.astype(BF16))
        for k in range(4):
            v_v[base + 192 * k : base + 192 * k + 192, :] = rows[:, 128 * k : 128 * k + 128]

        def send3(d, _):
            other, dev = mate_of(d)
            p3_s[kh, other] = gather(kh, other)
            remote(
                p3_s.at[kh, other], p3_r.at[kh, g], s3.at[kh, other], r3.at[kh, g], dev
            ).start()
            return 0

        lax.fori_loop(1, 8, send3, 0)
        p3_r[kh, g] = gather(kh, g)

    def wait3(d, _):
        other, dev = mate_of(d)
        for kh in range(2):
            remote(
                p3_s.at[kh, other], p3_r.at[kh, other], s3.at[kh, other], r3.at[kh, other], dev
            ).wait_recv()
        return 0

    lax.fori_loop(1, 8, wait3, 0)

    spectra = p3_r[...].astype(F32).reshape(128, MSG).astype(BF16)
    for dx in (1, 0):
        other = (q + dx) % 2
        field = dot(bw_ref[pl.ds(pl.multiple_of(128 * other, 128), 128), :], spectra)
        p4_s[pl.ds(16 * other, 16)] = fold(field.reshape(16, 8, MSG)).astype(BF16)
        steps = [(dy, dz) for dy in range(4) for dz in range(4)]
        steps.sort(key=lambda t: -(min(t[0], 4 - t[0]) + min(t[1], 4 - t[1])))
        for dy, dz in steps:
            if (dx, dy, dz) != (0, 0, 0):
                dest = 16 * other + ((row_y + dy) % 4) * 4 + (row_z + dz) % 4
                remote(p4_s.at[dest], p4_r.at[b], s4.at[dest], r4.at[b], (a, dest)).start()
    p4_r[b] = p4_s[b]

    for copy in halos:
        copy.wait_send()

    def drain1(d, _):
        dest = lax.rem(b + d, NLON)
        remote(p1_s.at[dest], p1_r.at[b], s1.at[dest], r1.at[b], (a, dest)).wait_send()
        return 0

    lax.fori_loop(1, NLON, drain1, 0)

    def drain_lat(d, _):
        other, dev = mate_of(d)
        for kh in range(2):
            remote(
                p2_s.at[kh, other], p2_r.at[kh, g], s2.at[kh, other], r2.at[kh, g], dev
            ).wait_send()
            remote(
                p3_s.at[kh, other], p3_r.at[kh, g], s3.at[kh, other], r3.at[kh, g], dev
            ).wait_send()
        return 0

    lax.fori_loop(1, 8, drain_lat, 0)
    c_up.wait()
    c_down.wait()
    results = []
    for smp in range(2):
        def join(part, _):
            for blk in range(NB):
                src = owner(part, smp, blk)

                @pl.when(src != b)
                def _(src=src):
                    remote(
                        p4_s.at[src], p4_r.at[src], s4.at[src], r4.at[src], (a, src)
                    ).wait_recv()

            msgs = [unfold(p4_r[owner(part, smp, blk)].astype(F32)) for blk in range(NB)]
            for i in range(ROW12):
                plane = jnp.concatenate([m[:, BS * i : BS * i + BS] for m in msgs], axis=1)
                for tile in range(6):
                    nf_v[tile, smp, pl.ds(part * ROW12 + i, 8, stride=ROWS), :] = plane[
                        :, 128 * tile : 128 * tile + 128
                    ]
            return 0

        lax.fori_loop(0, 2, join, 0)
        rows = slice(144 * smp, 144 * smp + 144)
        field = jnp.concatenate([nf_v[tile, smp, :144] for tile in range(6)], axis=1)
        middle = (field + tn_v[rows, :]).astype(BF16).astype(F32)
        acc_v[rows, :] = middle
        nrm_v[rows, :] = norm(middle, g2_ref[...].reshape(1, C)).astype(BF16)

        def up(step):
            return dot(nrm_v[rows, :], up_v[:, pl.ds(pl.multiple_of(step * 512, 512), 512)])

        def down(hidden, step):
            hidden = 0.5 * hidden * (1.0 + lax.erf(hidden * (1.0 / math.sqrt(2.0))))
            part = pl.ds(pl.multiple_of(step * 512, 512), 512)
            return dot(hidden.astype(BF16), down_v[part, :])

        h0_v[...] = up(0)

        def mlp(it, _):
            step = 2 * it
            h1_v[...] = up(step + 1)
            acc_v[rows, :] += down(h0_v[...], step)
            h0_v[...] = up(jnp.minimum(step + 2, HID // 512 - 1))
            acc_v[rows, :] += down(h1_v[...], step + 1)
            return 0

        lax.fori_loop(0, HID // 1024, mlp, 0)
        res_v[smp] = acc_v[rows, :].reshape(COLS, ROWS, C).astype(BF16)
        results.append(load(16 + smp, res_v.at[smp], out_ref.at[smp]))

    def drain4(d, _):
        dest = lax.rem(b + d, NLON)
        remote(p4_s.at[dest], p4_r.at[b], s4.at[dest], r4.at[b], (a, dest)).wait_send()
        return 0

    lax.fori_loop(1, NLON, drain4, 0)
    for copy in results:
        copy.wait()


def local(
    grid, patch_weight, norm_gain_one, spectral_one, spectral_bias, spectral_two,
    norm_gain_two, fc_up, fc_down,
):
    fw, bw = lon_tables()
    fh, bh = lat_tables()
    const = lambda x: jnp.asarray(x, F32).astype(BF16)
    any_spec = pl.BlockSpec(memory_space=pl.ANY)
    dma = pltpu.SemaphoreType.DMA
    out = pl.pallas_call(
        kernel,
        out_shape=jax.ShapeDtypeStruct((2, COLS, ROWS, C), BF16),
        in_specs=[any_spec] * 13,
        out_specs=any_spec,
        scratch_shapes=[
            pltpu.VMEM((3, 192, 192), BF16),
            pltpu.VMEM((128, 256), BF16),
            pltpu.VMEM((256, 128), BF16),
            pltpu.VMEM((C,), F32),
            pltpu.VMEM((2, C), F32),
            pltpu.VMEM((C,), F32),
            pltpu.VMEM((2, NV, 48, 192), BF16),
            pltpu.VMEM((5120, C), BF16),
            pltpu.VMEM((2, BS, BS), F32),
            pltpu.VMEM((2, BS, BS), F32),
            pltpu.VMEM((C, HID), BF16),
            pltpu.VMEM((HID, C), BF16),
            pltpu.VMEM((4, 160, 768), BF16),
            pltpu.VMEM((8, 288, 160), F32),
            pltpu.VMEM((2, 6, 480, 128), F32),
            pltpu.VMEM((2, 288, 1280), BF16),
            pltpu.VMEM((2, 96, 768), BF16),
            pltpu.VMEM((2, 16, 1280), BF16),
            pltpu.VMEM((6, 384, 128), F32),
            pltpu.VMEM((6, 384, 128), F32),
            pltpu.VMEM((6, 288, 128), F32),
            pltpu.VMEM((288, C), F32),
            pltpu.VMEM((6, 2, 192, 128), F32),
            pltpu.VMEM((288, C), F32),
            pltpu.VMEM((288, C), BF16),
            pltpu.VMEM((2, 2, ROWS, C), BF16),
            pltpu.VMEM((2, 2, ROWS, C), BF16),
            pltpu.VMEM((2, 16, C), BF16),
            pltpu.VMEM((6, 16, C), BF16),
            pltpu.VMEM((NLON, 8, 896), BF16),
            pltpu.VMEM((NLON, 8, 896), BF16),
            pltpu.VMEM((2, 8, 8, MSG), BF16),
            pltpu.VMEM((2, 8, 8, MSG), BF16),
            pltpu.VMEM((2, 8, 8, MSG), BF16),
            pltpu.VMEM((2, 8, 8, MSG), BF16),
            pltpu.VMEM((NLON, 8, 896), BF16),
            pltpu.VMEM((NLON, 8, 896), BF16),
            pltpu.VMEM((8 * 192, 128), F32),
            pltpu.VMEM((8 * 192, 128), F32),
            pltpu.VMEM((256, 256), BF16),
            pltpu.VMEM((256, 256), BF16),
            pltpu.VMEM((144, 512), F32),
            pltpu.VMEM((144, 512), F32),
            pltpu.VMEM((2, COLS, ROWS, C), BF16),
            pltpu.VMEM((256, MSG), F32),
            dma((18,)),
            dma((10,)),
            dma((10,)),
            dma((NLON,)),
            dma((NLON,)),
            dma((2, 8)),
            dma((2, 8)),
            dma((2, 8)),
            dma((2, 8)),
            dma((NLON,)),
            dma((NLON,)),
        ],
        compiler_params=pltpu.CompilerParams(
            collective_id=0, has_side_effects=True, vmem_limit_bytes=56 * 1024 * 1024
        ),
    )(
        grid.transpose(0, 1, 3, 2), patch_weight, spectral_one, spectral_two, fc_up, fc_down,
        const(feature_table()),
        const(np.stack([pick_table(), fh, bh])), const(fw), const(bw),
        norm_gain_one, spectral_bias, norm_gain_two,
    )
    return out.transpose(0, 2, 1, 3)


def solution(mesh):
    in_specs = (P(None, None, "lat", "lon"), P(), P(), P(), P(), P(), P(), P(), P())
    out_specs = P(None, "lat", "lon", None)
    return jax.shard_map(local, mesh=mesh, in_specs=in_specs, out_specs=out_specs, check_vma=False)
```

```python
import math

import jax
import jax.numpy as jnp
import numpy as np
from jax import lax
from jax.experimental import pallas as pl
from jax.experimental.pallas import tpu as pltpu
from jax.sharding import PartitionSpec as P

MESH = pl.DeviceIdType.MESH
F32 = jnp.float32
BF16 = jnp.bfloat16

NLAT, NLON = 4, 32
NV, C, HID, NB, BS = 20, 768, 3072, 8, 96
H, W, KW = 96, 192, 64
ROWS, COLS = 24, 6
ROW12 = 12
MSG = ROW12 * BS


def pick_table():
    sel = np.zeros((192, 192), np.float32)
    for r8 in range(8):
        for row in range(ROWS):
            sel[r8 * ROWS + row, 8 * row + r8] = 1.0
    return sel


def feature_table():
    table = np.zeros((4, 160, 768), np.float32)
    for r in range(4):
        for v in range(NV):
            for c8 in range(8):
                table[r, v * 8 + c8, (64, 384)[c8 // 4] + v * 16 + 4 * r + c8 % 4] = 1.0
    return table


def lon_tables():
    k = np.arange(KW)
    w = np.arange(W)
    angle = 2.0 * math.pi * ((k[:, None] * w[None, :]) % W) / W
    scale = 1.0 / math.sqrt(W)
    both = np.stack([np.cos(angle), -np.sin(angle)]) * scale
    fwd = both.reshape(2, 8, 2, 4, W).transpose(2, 1, 3, 0, 4).reshape(128, NLON, COLS)
    fwd = np.pad(fwd, ((0, 0), (0, 0), (0, 2))).reshape(128, 256)
    weight = np.where(k == 0, 1.0, 2.0)
    back = both * weight[None, :, None]
    back = back.reshape(2, 8, 2, 4, W).transpose(4, 2, 1, 3, 0).reshape(NLON, COLS, 128)
    back = np.pad(back, ((0, 0), (0, 2), (0, 0))).reshape(256, 128)
    return fwd, back


def lat_tables():
    h = np.arange(H)
    angle = 2.0 * math.pi * ((h[:, None] * h[None, :]) % H) / H
    cos, sin = np.cos(angle) / math.sqrt(H), np.sin(angle) / math.sqrt(H)
    fwd = np.block([[cos, sin], [-sin, cos]])
    back = np.block([[cos, -sin], [sin, cos]])
    return fwd, back


def norm(values, gain):
    centre = jnp.mean(values, axis=-1, keepdims=True)
    off = values - centre
    spread = jnp.mean(jnp.square(off), axis=-1, keepdims=True)
    return off * lax.rsqrt(spread + 1e-05) * gain


def fold(msg):
    row = lax.broadcasted_iota(jnp.int32, msg.shape[:-1] + (128,), msg.ndim - 2)
    tiles = []
    for u in range(7):
        tile = msg[..., 128 * u : 128 * u + 128]
        if u < COLS:
            tile = jnp.where(row == 6, msg[..., u : u + 1, 896:1024], tile)
            tile = jnp.where(row == 7, msg[..., u : u + 1, 1024:], tile)
        tiles.append(tile)
    return jnp.concatenate(tiles, axis=-1)


def unfold(msg):
    row = lax.broadcasted_iota(jnp.int32, msg.shape[:-1] + (128,), msg.ndim - 2)
    last = [jnp.zeros(row.shape, F32)] * 2
    for u in range(COLS):
        for i in range(2):
            piece = msg[..., 6 + i : 7 + i, 128 * u : 128 * u + 128]
            last[i] = jnp.where(row == u, piece, last[i])
    return jnp.concatenate([msg] + last, axis=-1)


def dot(left, right):
    return jnp.dot(left, right, preferred_element_type=F32)


def kernel(
    grid_h, pw_h, one_h, two_h, up_h, down_h, tab_h, sq_h, fw_h, bw_h, g1_h, bias_h, g2_h,
    out_ref,
    sq_v, fw_ref, bw_ref, g1_ref, bias_ref, g2_ref,
    grid_v, pw_v, one_v, two_v, up_v, down_v, tab_v,
    t_v, m_v, lhs_v, side_v, rim_v, q0_v, q3_v, tot_v, acc_v, nf_v, tn_v, nrm_v,
    ew_s, ew_r, ns_s, ns_r,
    p1_s, p1_r, p2_s, p2_r, p3_s, p3_r, p4_s, p4_r,
    z_v, v_v, w1_v, w2_v, h0_v, h1_v, res_v, x_v,
    lsem, halo_ss, halo_rs, s1, r1, s2, r2, s3, r3, s4, r4,
):
    a = lax.axis_index("lat")
    b = lax.axis_index("lon")
    q = b // 16
    p = b % 16
    row_y = p // 4
    row_z = p % 4
    mine = (row_y + row_z) % 2
    n = 2 * row_y + row_z // 2
    g = 2 * a + q

    barrier = pltpu.get_barrier_semaphore()

    def greet_lon(d, _):
        pl.semaphore_signal(
            barrier, inc=1, device_id=(a, lax.rem(b + d, NLON)), device_id_type=MESH
        )
        return 0

    lax.fori_loop(1, NLON, greet_lon, 0)

    def greet_lat(d, _):
        mate = lax.rem(a + 1 + d // 2, NLAT)
        pl.semaphore_signal(
            barrier, inc=1, device_id=(mate, (d % 2) * 16 + p), device_id_type=MESH
        )
        return 0

    lax.fori_loop(0, 6, greet_lat, 0)
    for da in (1, NLAT - 1):
        for db in (1, NLON - 1):
            corner = (lax.rem(a + da, NLAT), lax.rem(b + db, NLON))
            pl.semaphore_signal(barrier, inc=1, device_id=corner, device_id_type=MESH)
    def load(index, src, dst):
        copy = pltpu.make_async_copy(src, dst, lsem.at[index])
        copy.start()
        return copy

    c_grid = load(0, grid_h, grid_v)
    c_sq = load(10, sq_h, sq_v)
    c_tab = load(1, tab_h, tab_v)
    c_pw = {}
    for i, off in enumerate((0, 3, 1, 2)):
        part = pl.ds(1280 * off, 1280)
        c_pw[off] = load(2 + i, pw_h.at[part], pw_v.at[part])
    c_one = load(6, one_h.at[:, n], one_v)
    c_two = load(7, two_h.at[:, n], two_v)
    small = [
        load(11 + i, src, dst)
        for i, (src, dst) in enumerate(
            ((g1_h, g1_ref), (bias_h, bias_ref), (g2_h, g2_ref), (fw_h, fw_ref), (bw_h, bw_ref))
        )
    ]

    nf_v[:, :, 144:] = jnp.zeros((6, 2, 48, 128), F32)
    for smp in range(2):
        for first in (240 * smp, 240 * smp + 192):
            m_v[:, :, first : first + 48] = jnp.zeros((2, 6, 48, 128), F32)
    for tile in range(6):
        q0_v[tile, pl.ds(0, 12, stride=32), :] = jnp.zeros((12, 128), F32)
        q3_v[tile, pl.ds(31, 12, stride=32), :] = jnp.zeros((12, 128), F32)
    c_grid.wait()
    c_sq.wait()
    for smp in range(2):
        for lp in range(3):
            block = grid_v[smp, :, 16 * lp : 16 * lp + 16, :]
            block = block.astype(F32).reshape(NV, 2, 8, 192)
            for half in range(2):
                x = block[:, half].reshape(NV * 8, 192).astype(BF16)
                turned = lax.dot_general(
                    sq_v[0], x, (((1,), (1,)), ((), ())), preferred_element_type=F32
                )
                first = (6 * smp + 2 * lp + half) * ROWS
                for r8 in range(8):
                    t_v[r8, first : first + ROWS, :] = turned[ROWS * r8 : ROWS * r8 + ROWS]

    c_tab.wait()
    for half in range(2):
        value = dot(t_v[4 * half].astype(BF16), tab_v[0])
        for r in range(1, 4):
            value = value + dot(t_v[4 * half + r].astype(BF16), tab_v[r])
        for tile in range(6):
            lanes = slice(128 * tile, 128 * tile + 128)
            for smp in range(2):
                m_v[half, tile, 240 * smp + 48 : 240 * smp + 192] = value[
                    144 * smp : 144 * smp + 144, lanes
                ]

    places = ((3, 0), (4, 0), (5, 0), (1, 1), (2, 1), (3, 1), (4, 1), (5, 1), (1, 2), (2, 2))
    for half in range(2):
        for tile, (lane, slot) in enumerate(places):
            cols = slice(128 * tile, 128 * tile + 128)
            outer = []
            for smp in range(2):
                first = (10 * smp + slot) * ROWS
                rim = first + (0, ROWS - 1)[half]
                value = m_v[half, lane, first : first + 192, :]
                row = m_v[half, lane, pl.ds(rim, 8, stride=ROWS), :]
                if tile in (2, 7):
                    value = value + m_v[half, 0, first + ROWS : first + ROWS + 192, :]
                    row = row + m_v[half, 0, pl.ds(rim + ROWS, 8, stride=ROWS), :]
                outer.append(row)
                lhs_v[half, 144 * smp : 144 * smp + 144, cols] = value[ROWS:168].astype(BF16)
                if tile < 3 or tile >= 7:
                    side = jnp.concatenate([value[:ROWS], value[168:]], axis=0)
                    at = 128 * (tile if tile < 3 else tile - 4)
                    side_v[half, 48 * smp : 48 * smp + 48, at : at + 128] = side.astype(BF16)
            rim_v[half, :, cols] = jnp.concatenate(outer, axis=0).astype(BF16)

    def weight(off, pair):
        return pw_v[1280 * off : 1280 * off + 1280, 256 * pair : 256 * pair + 256]

    for way, (off, half) in enumerate(((0, 1), (3, 0))):
        c_pw[off].wait()
        for pair in range(3):
            value = dot(rim_v[half], weight(off, pair))
            ns_s[way, :, 256 * pair : 256 * pair + 256] = value.astype(BF16)

    pl.semaphore_wait(barrier, NLON - 1 + 6 + 4)

    def remote(src, dst, ssem, rsem, dev):
        return pltpu.make_async_remote_copy(
            src_ref=src, dst_ref=dst, send_sem=ssem, recv_sem=rsem,
            device_id=dev, device_id_type=MESH,
        )

    halos = [
        remote(
            src, dst, halo_ss.at[sem], halo_rs.at[sem],
            (lax.rem(a + da, NLAT), lax.rem(b + db, NLON)),
        )
        for src, dst, sem, da, db in (
            [
                (ns_s.at[i], ns_r.at[3 * i + side], 3 * i + side, (1, NLAT - 1)[i], db)
                for i in range(2)
                for side, db in enumerate((0, 1, NLON - 1))
            ]
            + [
                (ew_s.at[i, smp], ew_r.at[i, smp], 6 + 2 * smp + i, 0, (1, NLON - 1)[i])
                for smp in range(2)
                for i in range(2)
            ]
        )
    ]
    for copy in halos[:6]:
        copy.start()

    c_pw[1].wait()
    c_pw[2].wait()
    none = jnp.zeros((4, 1, 256), F32)

    def outer_weight(off, pair):
        cols = slice(256 * pair, 256 * pair + 256)
        first = 1280 * off
        return jnp.concatenate(
            [pw_v[first : first + 384, cols], pw_v[first + 896 : first + 1280, cols]], axis=0
        )

    for pair in range(3):
        value = dot(side_v[0], outer_weight(1, pair)) + dot(side_v[1], outer_weight(2, pair))
        above = dot(side_v[1], outer_weight(0, pair)).reshape(4, ROWS, 256)
        below = dot(side_v[0], outer_weight(3, pair)).reshape(4, ROWS, 256)
        above = jnp.concatenate([none, above[:, :-1]], axis=1)
        below = jnp.concatenate([below[:, 1:], none], axis=1)
        value = (value + (above + below).reshape(96, 256)).astype(BF16)
        for smp in range(2):
            for way in range(2):
                first = ROWS * (2 * smp + 1 - way)
                ew_s[way, smp, :, 256 * pair : 256 * pair + 256] = value[first : first + ROWS]
    for copy in halos[6:]:
        copy.start()

    def rim_rows(way, smp, cols):
        straight, west, east = [
            ns_r[3 * way + side, :, cols].astype(F32)[8 * smp : 8 * smp + 8] for side in range(3)
        ]
        none = jnp.zeros((4, 128), F32)
        value = straight[1:7] + jnp.concatenate([west[7:8], none, east[0:1]], axis=0)
        return jnp.where((a > 0, a < NLAT - 1)[way], value, 0.0)

    c_up = load(8, up_h, up_v)
    c_down = load(9, down_h, down_v)
    for copy in small:
        copy.wait()

    def owner(part, smp, blk):
        return part * 16 + (blk // 2) * 4 + (blk % 2) * 2 + (smp + blk // 2) % 2

    for smp in range(2):
        rows = slice(144 * smp, 144 * smp + 144)
        for pair in range(3):
            for off, half, out_v, lead in ((0, 1, q0_v, 1), (3, 0, q3_v, 7)):
                value = dot(lhs_v[half, rows], weight(off, pair))
                for lane in range(2):
                    lanes = slice(128 * lane, 128 * lane + 128)
                    for m in range(COLS):
                        first = 32 * (COLS * smp + m) + lead
                        out_v[2 * pair + lane, first : first + ROWS, :] = value[
                            ROWS * m : ROWS * m + ROWS, lanes
                        ]
            value = dot(lhs_v[0, rows], weight(1, pair)) + dot(lhs_v[1, rows], weight(2, pair))
            for lane in range(2):
                tile = 2 * pair + lane
                groups = slice(192 * smp, 192 * smp + 192)
                shifted = (
                    q0_v[tile, groups].reshape(COLS, 32, 128)[:, :ROWS]
                    + q3_v[tile, groups].reshape(COLS, 32, 128)[:, 8:]
                )
                tot_v[tile, rows] = (
                    value[:, 128 * lane : 128 * lane + 128] + shifted.reshape(144, 128)
                )
        if smp == 0:
            for copy in halos[:6]:
                copy.wait_recv()
        for tile in range(6):
            cols = slice(128 * tile, 128 * tile + 128)
            for way in range(2):
                at = pl.ds(144 * smp + (0, ROWS - 1)[way], COLS, stride=ROWS)
                tot_v[tile, at, :] += rim_rows(way, smp, cols)
        for way, j in ((0, 0), (1, COLS - 1)):
            halos[6 + 2 * smp + way].wait_recv()
            first = ROWS * (COLS * smp + j)
            for tile in range(6):
                cols = slice(128 * tile, 128 * tile + 128)
                tot_v[tile, first : first + ROWS, :] += ew_r[way, smp, :, cols].astype(F32)
        tok = jnp.concatenate([tot_v[t, rows, :] for t in range(6)], axis=1)
        tok = tok.astype(BF16).astype(F32)
        normed = norm(tok, g1_ref[...].reshape(1, C)).astype(BF16).astype(F32)
        tn_v[rows, :] = tok + normed
        for tile in range(6):
            nf_v[tile, smp, :144] = normed[:, 128 * tile : 128 * tile + 128]
        for part in range(2):
            planes = [
                jnp.concatenate(
                    [nf_v[t, smp, pl.ds(part * ROW12 + i, 8, stride=ROWS), :] for t in range(6)],
                    axis=1,
                )
                for i in range(ROW12)
            ]
            for blk in range(NB):
                msg = jnp.concatenate(
                    [plane[:, BS * blk : BS * blk + BS] for plane in planes], axis=1
                )
                p1_s[owner(part, smp, blk)] = fold(msg).astype(BF16)
        odd = (smp + mine) % 2
        for dx in (1, 0):
            for dy in (2, 1, 3, 0):
                for dz in (2, 0):
                    dest = (
                        ((q + dx) % 2) * 16 + ((row_y + dy) % 4) * 4 + (row_z + dz + (odd + dy) % 2) % 4
                    )

                    def send(dest=dest):
                        remote(
                            p1_s.at[dest], p1_r.at[b], s1.at[dest], r1.at[b], (a, dest)
                        ).start()

                    if (dx, dy, dz) == (0, 0, 0):
                        pl.when(odd == 1)(send)
                    else:
                        send()
    p1_r[b] = p1_s[b]

    c_one.wait()
    c_two.wait()
    for src, dst in ((one_v, w1_v), (two_v, w2_v)):
        dst[...] = jnp.zeros_like(dst)
        dst[0:BS, 0:BS] = src[0].astype(BF16)
        dst[0:BS, 128 : 128 + BS] = src[1].astype(BF16)
        dst[128 : 128 + BS, 0:BS] = -src[1].astype(BF16)
        dst[128 : 128 + BS, 128 : 128 + BS] = src[0].astype(BF16)
    bias = jnp.zeros((1, 256), F32)
    for blk in range(NB):
        parts = []
        for ri in range(2):
            parts.append(bias_ref[ri : ri + 1, BS * blk : BS * blk + BS])
            parts.append(jnp.zeros((1, 32), F32))
        bias = bias + jnp.where(n == blk, jnp.concatenate(parts, axis=1), 0.0)

    def take1(d, _):
        src = lax.rem(b + d, NLON)

        @pl.when(d > 0)
        def _():
            remote(p1_s.at[src], p1_r.at[src], s1.at[src], r1.at[src], (a, src)).wait_recv()

        at = pl.ds(pl.multiple_of(8 * src, 8), 8)
        x_v[at, :] = unfold(p1_r[src].astype(F32))
        return 0

    lax.fori_loop(0, NLON, take1, 0)

    def mate_of(d):
        other = lax.rem(g + d, 8)
        return other, (other // 2, (other % 2) * 16 + p)

    mates = [(dh, dc, dl) for dh in range(2) for dc in range(2) for dl in range(2)][1:]
    mates.sort(key=lambda t: (not (t[0] and not t[2]), not t[2]))

    def mate_at(dh, dc, dl):
        lat = ((a // 2 + dh) % 2) * 2 + (a % 2 + dc) % 2
        half = (q + dl) % 2
        return 2 * lat + half, (lat, half * 16 + p)

    x = x_v[...].astype(BF16)
    for kh in range(2):
        part = dot(fw_ref[64 * kh : 64 * kh + 64, :], x)
        p2_s[kh] = part.reshape(8, 8, MSG).astype(BF16)
        for way in mates:
            other, dev = mate_at(*way)
            remote(
                p2_s.at[kh, other], p2_r.at[kh, g], s2.at[kh, other], r2.at[kh, g], dev
            ).start()

    def spread(kh, src, value):
        for i in range(ROW12):
            piece = value[:, BS * i : BS * i + BS]
            piece = jnp.concatenate([piece, jnp.zeros((8, 128 - BS), F32)], axis=1)
            z_v[pl.ds(768 * kh + ROW12 * src + i, 8, stride=H), :] = piece

    def gather(kh, dest):
        pieces = [
            v_v[pl.ds(768 * kh + ROW12 * dest + i, 8, stride=H), :][:, :BS] for i in range(ROW12)
        ]
        return jnp.concatenate(pieces, axis=1).astype(BF16)

    for kh in range(2):
        spread(kh, g, p2_s[kh, g].astype(F32))

        def take2(d, _):
            other, dev = mate_of(d)
            remote(
                p2_s.at[kh, other], p2_r.at[kh, other], s2.at[kh, other], r2.at[kh, other], dev
            ).wait_recv()
            spread(kh, other, p2_r[kh, other].astype(F32))
            return 0

        lax.fori_loop(1, 8, take2, 0)

        base = 768 * kh
        z = jnp.concatenate(
            [z_v[base + 192 * k : base + 192 * k + 192, :] for k in range(4)], axis=1
        )
        spec = dot(sq_v[1], z.astype(BF16))
        modes = jnp.concatenate(
            [
                jnp.concatenate(
                    [spec[:H, 128 * k : 128 * k + 128], spec[H:, 128 * k : 128 * k + 128]], axis=1
                )
                for k in range(4)
            ],
            axis=0,
        )
        mid = jnp.maximum(dot(modes.astype(BF16), w1_v[...]) + bias, 0.0)
        res = dot(mid.astype(BF16), w2_v[...])
        res = res - jnp.clip(res, -0.01, 0.01)
        back = jnp.concatenate(
            [
                jnp.concatenate(
                    [res[H * k : H * k + H, :128], res[H * k : H * k + H, 128:]], axis=0
                )
                for k in range(4)
            ],
            axis=1,
        )
        rows = dot(sq_v[2], back.astype(BF16))
        for k in range(4):
            v_v[base + 192 * k : base + 192 * k + 192, :] = rows[:, 128 * k : 128 * k + 128]

        for way in mates:
            other, dev = mate_at(*way)
            p3_s[kh, other] = gather(kh, other)
            remote(
                p3_s.at[kh, other], p3_r.at[kh, g], s3.at[kh, other], r3.at[kh, g], dev
            ).start()
        p3_r[kh, g] = gather(kh, g)

    def wait3(d, _):
        other, dev = mate_of(d)
        for kh in range(2):
            remote(
                p3_s.at[kh, other], p3_r.at[kh, other], s3.at[kh, other], r3.at[kh, other], dev
            ).wait_recv()
        return 0

    lax.fori_loop(1, 8, wait3, 0)

    spectra = p3_r[...].astype(F32).reshape(128, MSG).astype(BF16)
    for dx in (1, 0):
        other = (q + dx) % 2
        field = dot(bw_ref[pl.ds(pl.multiple_of(128 * other, 128), 128), :], spectra)
        p4_s[pl.ds(16 * other, 16)] = fold(field.reshape(16, 8, MSG)).astype(BF16)
        steps = [(dy, dz) for dy in range(4) for dz in range(4)]
        steps.sort(key=lambda t: -(min(t[0], 4 - t[0]) + min(t[1], 4 - t[1])))
        for dy, dz in steps:
            if (dx, dy, dz) != (0, 0, 0):
                dest = 16 * other + ((row_y + dy) % 4) * 4 + (row_z + dz) % 4
                remote(p4_s.at[dest], p4_r.at[b], s4.at[dest], r4.at[b], (a, dest)).start()
    p4_r[b] = p4_s[b]

    for copy in halos:
        copy.wait_send()

    def drain1(d, _):
        dest = lax.rem(b + d, NLON)
        remote(p1_s.at[dest], p1_r.at[b], s1.at[dest], r1.at[b], (a, dest)).wait_send()
        return 0

    lax.fori_loop(1, NLON, drain1, 0)

    def drain_lat(d, _):
        other, dev = mate_of(d)
        for kh in range(2):
            remote(
                p2_s.at[kh, other], p2_r.at[kh, g], s2.at[kh, other], r2.at[kh, g], dev
            ).wait_send()
            remote(
                p3_s.at[kh, other], p3_r.at[kh, g], s3.at[kh, other], r3.at[kh, g], dev
            ).wait_send()
        return 0

    lax.fori_loop(1, 8, drain_lat, 0)
    c_up.wait()
    c_down.wait()
    results = []
    for smp in range(2):
        def join(part, _):
            for blk in range(NB):
                src = owner(part, smp, blk)

                @pl.when(src != b)
                def _(src=src):
                    remote(
                        p4_s.at[src], p4_r.at[src], s4.at[src], r4.at[src], (a, src)
                    ).wait_recv()

            msgs = [unfold(p4_r[owner(part, smp, blk)].astype(F32)) for blk in range(NB)]
            for i in range(ROW12):
                plane = jnp.concatenate([m[:, BS * i : BS * i + BS] for m in msgs], axis=1)
                for tile in range(6):
                    nf_v[tile, smp, pl.ds(part * ROW12 + i, 8, stride=ROWS), :] = plane[
                        :, 128 * tile : 128 * tile + 128
                    ]
            return 0

        lax.fori_loop(0, 2, join, 0)
        rows = slice(144 * smp, 144 * smp + 144)
        field = jnp.concatenate([nf_v[tile, smp, :144] for tile in range(6)], axis=1)
        middle = (field + tn_v[rows, :]).astype(BF16).astype(F32)
        acc_v[rows, :] = middle
        nrm_v[rows, :] = norm(middle, g2_ref[...].reshape(1, C)).astype(BF16)

        def up(step):
            return dot(nrm_v[rows, :], up_v[:, pl.ds(pl.multiple_of(step * 512, 512), 512)])

        def down(hidden, step):
            hidden = 0.5 * hidden * (1.0 + lax.erf(hidden * (1.0 / math.sqrt(2.0))))
            part = pl.ds(pl.multiple_of(step * 512, 512), 512)
            return dot(hidden.astype(BF16), down_v[part, :])

        h0_v[...] = up(0)

        def mlp(it, _):
            step = 2 * it
            h1_v[...] = up(step + 1)
            acc_v[rows, :] += down(h0_v[...], step)
            h0_v[...] = up(jnp.minimum(step + 2, HID // 512 - 1))
            acc_v[rows, :] += down(h1_v[...], step + 1)
            return 0

        lax.fori_loop(0, HID // 1024, mlp, 0)
        res_v[smp] = acc_v[rows, :].reshape(COLS, ROWS, C).astype(BF16)
        results.append(load(16 + smp, res_v.at[smp], out_ref.at[smp]))

    def drain4(d, _):
        dest = lax.rem(b + d, NLON)
        remote(p4_s.at[dest], p4_r.at[b], s4.at[dest], r4.at[b], (a, dest)).wait_send()
        return 0

    lax.fori_loop(1, NLON, drain4, 0)
    for copy in results:
        copy.wait()


def local(
    grid, patch_weight, norm_gain_one, spectral_one, spectral_bias, spectral_two,
    norm_gain_two, fc_up, fc_down,
):
    fw, bw = lon_tables()
    fh, bh = lat_tables()
    const = lambda x: jnp.asarray(x, F32).astype(BF16)
    any_spec = pl.BlockSpec(memory_space=pl.ANY)
    dma = pltpu.SemaphoreType.DMA
    out = pl.pallas_call(
        kernel,
        out_shape=jax.ShapeDtypeStruct((2, COLS, ROWS, C), BF16),
        in_specs=[any_spec] * 13,
        out_specs=any_spec,
        scratch_shapes=[
            pltpu.VMEM((3, 192, 192), BF16),
            pltpu.VMEM((128, 256), BF16),
            pltpu.VMEM((256, 128), BF16),
            pltpu.VMEM((C,), F32),
            pltpu.VMEM((2, C), F32),
            pltpu.VMEM((C,), F32),
            pltpu.VMEM((2, NV, 48, 192), BF16),
            pltpu.VMEM((5120, C), BF16),
            pltpu.VMEM((2, BS, BS), F32),
            pltpu.VMEM((2, BS, BS), F32),
            pltpu.VMEM((C, HID), BF16),
            pltpu.VMEM((HID, C), BF16),
            pltpu.VMEM((4, 160, 768), BF16),
            pltpu.VMEM((8, 288, 160), F32),
            pltpu.VMEM((2, 6, 480, 128), F32),
            pltpu.VMEM((2, 288, 1280), BF16),
            pltpu.VMEM((2, 96, 768), BF16),
            pltpu.VMEM((2, 16, 1280), BF16),
            pltpu.VMEM((6, 384, 128), F32),
            pltpu.VMEM((6, 384, 128), F32),
            pltpu.VMEM((6, 288, 128), F32),
            pltpu.VMEM((288, C), F32),
            pltpu.VMEM((6, 2, 192, 128), F32),
            pltpu.VMEM((288, C), F32),
            pltpu.VMEM((288, C), BF16),
            pltpu.VMEM((2, 2, ROWS, C), BF16),
            pltpu.VMEM((2, 2, ROWS, C), BF16),
            pltpu.VMEM((2, 16, C), BF16),
            pltpu.VMEM((6, 16, C), BF16),
            pltpu.VMEM((NLON, 8, 896), BF16),
            pltpu.VMEM((NLON, 8, 896), BF16),
            pltpu.VMEM((2, 8, 8, MSG), BF16),
            pltpu.VMEM((2, 8, 8, MSG), BF16),
            pltpu.VMEM((2, 8, 8, MSG), BF16),
            pltpu.VMEM((2, 8, 8, MSG), BF16),
            pltpu.VMEM((NLON, 8, 896), BF16),
            pltpu.VMEM((NLON, 8, 896), BF16),
            pltpu.VMEM((8 * 192, 128), F32),
            pltpu.VMEM((8 * 192, 128), F32),
            pltpu.VMEM((256, 256), BF16),
            pltpu.VMEM((256, 256), BF16),
            pltpu.VMEM((144, 512), F32),
            pltpu.VMEM((144, 512), F32),
            pltpu.VMEM((2, COLS, ROWS, C), BF16),
            pltpu.VMEM((256, MSG), F32),
            dma((18,)),
            dma((10,)),
            dma((10,)),
            dma((NLON,)),
            dma((NLON,)),
            dma((2, 8)),
            dma((2, 8)),
            dma((2, 8)),
            dma((2, 8)),
            dma((NLON,)),
            dma((NLON,)),
        ],
        compiler_params=pltpu.CompilerParams(
            collective_id=0, has_side_effects=True, vmem_limit_bytes=56 * 1024 * 1024
        ),
    )(
        grid.transpose(0, 1, 3, 2), patch_weight, spectral_one, spectral_two, fc_up, fc_down,
        const(feature_table()),
        const(np.stack([pick_table(), fh, bh])), const(fw), const(bw),
        norm_gain_one, spectral_bias, norm_gain_two,
    )
    return out.transpose(0, 2, 1, 3)


def solution(mesh):
    in_specs = (P(None, None, "lat", "lon"), P(), P(), P(), P(), P(), P(), P(), P())
    out_specs = P(None, "lat", "lon", None)
    return jax.shard_map(local, mesh=mesh, in_specs=in_specs, out_specs=out_specs, check_vma=False)
```

```python
import math

import jax
import jax.numpy as jnp
import numpy as np
from jax import lax
from jax.experimental import pallas as pl
from jax.experimental.pallas import tpu as pltpu
from jax.sharding import PartitionSpec as P

MESH = pl.DeviceIdType.MESH
F32 = jnp.float32
BF16 = jnp.bfloat16

NLAT, NLON = 4, 32
NV, C, HID, NB, BS = 20, 768, 3072, 8, 96
H, W, KW = 96, 192, 64
ROWS, COLS = 24, 6
ROW12 = 12
MSG = ROW12 * BS


def pick_table():
    sel = np.zeros((192, 192), np.float32)
    for r8 in range(8):
        for row in range(ROWS):
            sel[r8 * ROWS + row, 8 * row + r8] = 1.0
    return sel


def feature_table():
    table = np.zeros((4, 160, 768), np.float32)
    for r in range(4):
        for v in range(NV):
            for c8 in range(8):
                table[r, v * 8 + c8, (64, 384)[c8 // 4] + v * 16 + 4 * r + c8 % 4] = 1.0
    return table


def lon_tables():
    k = np.arange(KW)
    w = np.arange(W)
    angle = 2.0 * math.pi * ((k[:, None] * w[None, :]) % W) / W
    scale = 1.0 / math.sqrt(W)
    both = np.stack([np.cos(angle), -np.sin(angle)]) * scale
    fwd = both.reshape(2, 8, 2, 4, W).transpose(2, 1, 3, 0, 4).reshape(128, NLON, COLS)
    fwd = np.pad(fwd, ((0, 0), (0, 0), (0, 2))).reshape(128, 256)
    weight = np.where(k == 0, 1.0, 2.0)
    back = both * weight[None, :, None]
    back = back.reshape(2, 8, 2, 4, W).transpose(4, 2, 1, 3, 0).reshape(NLON, COLS, 128)
    back = np.pad(back, ((0, 0), (0, 2), (0, 0))).reshape(256, 128)
    return fwd, back


def lat_tables():
    h = np.arange(H)
    angle = 2.0 * math.pi * ((h[:, None] * h[None, :]) % H) / H
    cos, sin = np.cos(angle) / math.sqrt(H), np.sin(angle) / math.sqrt(H)
    fwd = np.block([[cos, sin], [-sin, cos]])
    back = np.block([[cos, -sin], [sin, cos]])
    return fwd, back


def norm(values, gain):
    centre = jnp.mean(values, axis=-1, keepdims=True)
    off = values - centre
    spread = jnp.mean(jnp.square(off), axis=-1, keepdims=True)
    return off * lax.rsqrt(spread + 1e-05) * gain


def fold(msg):
    row = lax.broadcasted_iota(jnp.int32, msg.shape[:-1] + (128,), msg.ndim - 2)
    tiles = []
    for u in range(7):
        tile = msg[..., 128 * u : 128 * u + 128]
        if u < COLS:
            tile = jnp.where(row == 6, msg[..., u : u + 1, 896:1024], tile)
            tile = jnp.where(row == 7, msg[..., u : u + 1, 1024:], tile)
        tiles.append(tile)
    return jnp.concatenate(tiles, axis=-1)


def unfold(msg):
    row = lax.broadcasted_iota(jnp.int32, msg.shape[:-1] + (128,), msg.ndim - 2)
    last = [jnp.zeros(row.shape, F32)] * 2
    for u in range(COLS):
        for i in range(2):
            piece = msg[..., 6 + i : 7 + i, 128 * u : 128 * u + 128]
            last[i] = jnp.where(row == u, piece, last[i])
    return jnp.concatenate([msg] + last, axis=-1)


def dot(left, right):
    return jnp.dot(left, right, preferred_element_type=F32)


def kernel(
    grid_h, pw_h, one_h, two_h, up_h, down_h, tab_h, sq_h, fw_h, bw_h, g1_h, bias_h, g2_h,
    out_ref,
    sq_v, fw_ref, bw_ref, g1_ref, bias_ref, g2_ref,
    grid_v, pw_v, one_v, two_v, up_v, down_v, tab_v,
    t_v, m_v, lhs_v, side_v, rim_v, q0_v, q3_v, tot_v, acc_v, nf_v, tn_v, nrm_v,
    ew_s, ew_r, ns_s, ns_r,
    p1_s, p1_r, p2_s, p2_r, p3_s, p3_r, p4_s, p4_r,
    z_v, v_v, w1_v, w2_v, h0_v, h1_v, res_v, x_v,
    lsem, halo_ss, halo_rs, s1, r1, s2, r2, s3, r3, s4, r4,
):
    a = lax.axis_index("lat")
    b = lax.axis_index("lon")
    q = b // 16
    p = b % 16
    row_y = p // 4
    row_z = p % 4
    mine = (row_y + row_z) % 2
    n = 2 * row_y + row_z // 2
    g = 2 * a + q

    barrier = pltpu.get_barrier_semaphore()

    def greet_lon(d, _):
        pl.semaphore_signal(
            barrier, inc=1, device_id=(a, lax.rem(b + d, NLON)), device_id_type=MESH
        )
        return 0

    lax.fori_loop(1, NLON, greet_lon, 0)

    def greet_lat(d, _):
        mate = lax.rem(a + 1 + d // 2, NLAT)
        pl.semaphore_signal(
            barrier, inc=1, device_id=(mate, (d % 2) * 16 + p), device_id_type=MESH
        )
        return 0

    lax.fori_loop(0, 6, greet_lat, 0)
    for da in (1, NLAT - 1):
        for db in (1, NLON - 1):
            corner = (lax.rem(a + da, NLAT), lax.rem(b + db, NLON))
            pl.semaphore_signal(barrier, inc=1, device_id=corner, device_id_type=MESH)
    def load(index, src, dst):
        copy = pltpu.make_async_copy(src, dst, lsem.at[index])
        copy.start()
        return copy

    c_grid = load(0, grid_h, grid_v)
    c_sq = load(10, sq_h, sq_v)
    c_tab = load(1, tab_h, tab_v)
    c_pw = {}
    for i, off in enumerate((0, 3, 1, 2)):
        part = pl.ds(1280 * off, 1280)
        c_pw[off] = load(2 + i, pw_h.at[part], pw_v.at[part])
    c_one = load(6, one_h.at[:, n], one_v)
    c_two = load(7, two_h.at[:, n], two_v)
    small = [
        load(11 + i, src, dst)
        for i, (src, dst) in enumerate(
            ((g1_h, g1_ref), (bias_h, bias_ref), (g2_h, g2_ref), (fw_h, fw_ref), (bw_h, bw_ref))
        )
    ]

    nf_v[:, :, 144:] = jnp.zeros((6, 2, 48, 128), F32)
    for smp in range(2):
        for first in (240 * smp, 240 * smp + 192):
            m_v[:, :, first : first + 48] = jnp.zeros((2, 6, 48, 128), F32)
    for tile in range(6):
        q0_v[tile, pl.ds(0, 12, stride=32), :] = jnp.zeros((12, 128), F32)
        q3_v[tile, pl.ds(31, 12, stride=32), :] = jnp.zeros((12, 128), F32)
    c_grid.wait()
    c_sq.wait()
    for smp in range(2):
        for lp in range(3):
            block = grid_v[smp, :, 16 * lp : 16 * lp + 16, :]
            block = block.astype(F32).reshape(NV, 2, 8, 192)
            for half in range(2):
                x = block[:, half].reshape(NV * 8, 192).astype(BF16)
                turned = lax.dot_general(
                    sq_v[0], x, (((1,), (1,)), ((), ())), preferred_element_type=F32
                )
                first = (6 * smp + 2 * lp + half) * ROWS
                for r8 in range(8):
                    t_v[r8, first : first + ROWS, :] = turned[ROWS * r8 : ROWS * r8 + ROWS]

    c_tab.wait()
    for half in range(2):
        value = dot(t_v[4 * half].astype(BF16), tab_v[0])
        for r in range(1, 4):
            value = value + dot(t_v[4 * half + r].astype(BF16), tab_v[r])
        for tile in range(6):
            lanes = slice(128 * tile, 128 * tile + 128)
            for smp in range(2):
                m_v[half, tile, 240 * smp + 48 : 240 * smp + 192] = value[
                    144 * smp : 144 * smp + 144, lanes
                ]

    places = ((3, 0), (4, 0), (5, 0), (1, 1), (2, 1), (3, 1), (4, 1), (5, 1), (1, 2), (2, 2))
    for half in range(2):
        for tile, (lane, slot) in enumerate(places):
            cols = slice(128 * tile, 128 * tile + 128)
            outer = []
            for smp in range(2):
                first = (10 * smp + slot) * ROWS
                rim = first + (0, ROWS - 1)[half]
                value = m_v[half, lane, first : first + 192, :]
                row = m_v[half, lane, pl.ds(rim, 8, stride=ROWS), :]
                if tile in (2, 7):
                    value = value + m_v[half, 0, first + ROWS : first + ROWS + 192, :]
                    row = row + m_v[half, 0, pl.ds(rim + ROWS, 8, stride=ROWS), :]
                outer.append(row)
                lhs_v[half, 144 * smp : 144 * smp + 144, cols] = value[ROWS:168].astype(BF16)
                if tile < 3 or tile >= 7:
                    side = jnp.concatenate([value[:ROWS], value[168:]], axis=0)
                    at = 128 * (tile if tile < 3 else tile - 4)
                    side_v[half, 48 * smp : 48 * smp + 48, at : at + 128] = side.astype(BF16)
            rim_v[half, :, cols] = jnp.concatenate(outer, axis=0).astype(BF16)

    def weight(off, pair):
        return pw_v[1280 * off : 1280 * off + 1280, 256 * pair : 256 * pair + 256]

    for way, (off, half) in enumerate(((0, 1), (3, 0))):
        c_pw[off].wait()
        for pair in range(3):
            value = dot(rim_v[half], weight(off, pair))
            ns_s[way, :, 256 * pair : 256 * pair + 256] = value.astype(BF16)

    pl.semaphore_wait(barrier, NLON - 1 + 6 + 4)

    def remote(src, dst, ssem, rsem, dev):
        return pltpu.make_async_remote_copy(
            src_ref=src, dst_ref=dst, send_sem=ssem, recv_sem=rsem,
            device_id=dev, device_id_type=MESH,
        )

    halos = [
        remote(
            src, dst, halo_ss.at[sem], halo_rs.at[sem],
            (lax.rem(a + da, NLAT), lax.rem(b + db, NLON)),
        )
        for src, dst, sem, da, db in (
            [
                (ns_s.at[i], ns_r.at[3 * i + side], 3 * i + side, (1, NLAT - 1)[i], db)
                for i in range(2)
                for side, db in enumerate((0, 1, NLON - 1))
            ]
            + [
                (ew_s.at[i, smp], ew_r.at[i, smp], 6 + 2 * smp + i, 0, (1, NLON - 1)[i])
                for smp in range(2)
                for i in range(2)
            ]
        )
    ]
    for copy in halos[:6]:
        copy.start()

    c_pw[1].wait()
    c_pw[2].wait()
    none = jnp.zeros((4, 1, 256), F32)

    def outer_weight(off, pair):
        cols = slice(256 * pair, 256 * pair + 256)
        first = 1280 * off
        return jnp.concatenate(
            [pw_v[first : first + 384, cols], pw_v[first + 896 : first + 1280, cols]], axis=0
        )

    for pair in range(3):
        value = dot(side_v[0], outer_weight(1, pair)) + dot(side_v[1], outer_weight(2, pair))
        above = dot(side_v[1], outer_weight(0, pair)).reshape(4, ROWS, 256)
        below = dot(side_v[0], outer_weight(3, pair)).reshape(4, ROWS, 256)
        above = jnp.concatenate([none, above[:, :-1]], axis=1)
        below = jnp.concatenate([below[:, 1:], none], axis=1)
        value = (value + (above + below).reshape(96, 256)).astype(BF16)
        for smp in range(2):
            for way in range(2):
                first = ROWS * (2 * smp + 1 - way)
                ew_s[way, smp, :, 256 * pair : 256 * pair + 256] = value[first : first + ROWS]
    for copy in halos[6:]:
        copy.start()

    def rim_rows(way, smp, cols):
        straight, west, east = [
            ns_r[3 * way + side, :, cols].astype(F32)[8 * smp : 8 * smp + 8] for side in range(3)
        ]
        none = jnp.zeros((4, 128), F32)
        value = straight[1:7] + jnp.concatenate([west[7:8], none, east[0:1]], axis=0)
        return jnp.where((a > 0, a < NLAT - 1)[way], value, 0.0)

    c_up = load(8, up_h, up_v)
    c_down = load(9, down_h, down_v)
    for copy in small:
        copy.wait()

    def owner(part, smp, blk):
        return part * 16 + (blk // 2) * 4 + (blk % 2) * 2 + (smp + blk // 2) % 2

    for smp in range(2):
        rows = slice(144 * smp, 144 * smp + 144)
        for pair in range(3):
            for off, half, out_v, lead in ((0, 1, q0_v, 1), (3, 0, q3_v, 7)):
                value = dot(lhs_v[half, rows], weight(off, pair))
                for lane in range(2):
                    lanes = slice(128 * lane, 128 * lane + 128)
                    for m in range(COLS):
                        first = 32 * (COLS * smp + m) + lead
                        out_v[2 * pair + lane, first : first + ROWS, :] = value[
                            ROWS * m : ROWS * m + ROWS, lanes
                        ]
            value = dot(lhs_v[0, rows], weight(1, pair)) + dot(lhs_v[1, rows], weight(2, pair))
            for lane in range(2):
                tile = 2 * pair + lane
                groups = slice(192 * smp, 192 * smp + 192)
                shifted = (
                    q0_v[tile, groups].reshape(COLS, 32, 128)[:, :ROWS]
                    + q3_v[tile, groups].reshape(COLS, 32, 128)[:, 8:]
                )
                tot_v[tile, rows] = (
                    value[:, 128 * lane : 128 * lane + 128] + shifted.reshape(144, 128)
                )
        if smp == 0:
            for copy in halos[:6]:
                copy.wait_recv()
        for tile in range(6):
            cols = slice(128 * tile, 128 * tile + 128)
            for way in range(2):
                at = pl.ds(144 * smp + (0, ROWS - 1)[way], COLS, stride=ROWS)
                tot_v[tile, at, :] += rim_rows(way, smp, cols)
        for way, j in ((0, 0), (1, COLS - 1)):
            halos[6 + 2 * smp + way].wait_recv()
            first = ROWS * (COLS * smp + j)
            for tile in range(6):
                cols = slice(128 * tile, 128 * tile + 128)
                tot_v[tile, first : first + ROWS, :] += ew_r[way, smp, :, cols].astype(F32)
        tok = jnp.concatenate([tot_v[t, rows, :] for t in range(6)], axis=1)
        tok = tok.astype(BF16).astype(F32)
        normed = norm(tok, g1_ref[...].reshape(1, C)).astype(BF16).astype(F32)
        tn_v[rows, :] = tok + normed
        for tile in range(6):
            nf_v[tile, smp, :144] = normed[:, 128 * tile : 128 * tile + 128]
        for part in range(2):
            planes = [
                jnp.concatenate(
                    [nf_v[t, smp, pl.ds(part * ROW12 + i, 8, stride=ROWS), :] for t in range(6)],
                    axis=1,
                )
                for i in range(ROW12)
            ]
            for blk in range(NB):
                msg = jnp.concatenate(
                    [plane[:, BS * blk : BS * blk + BS] for plane in planes], axis=1
                )
                p1_s[owner(part, smp, blk)] = fold(msg).astype(BF16)
        odd = (smp + mine) % 2
        for dx in (1, 0):
            for dy in (2, 1, 3, 0):
                for dz in (2, 0):
                    dest = (
                        ((q + dx) % 2) * 16 + ((row_y + dy) % 4) * 4 + (row_z + dz + (odd + dy) % 2) % 4
                    )

                    def send(dest=dest):
                        remote(
                            p1_s.at[dest], p1_r.at[b], s1.at[dest], r1.at[b], (a, dest)
                        ).start()

                    if (dx, dy, dz) == (0, 0, 0):
                        pl.when(odd == 1)(send)
                    else:
                        send()
    p1_r[b] = p1_s[b]

    c_one.wait()
    c_two.wait()
    for src, dst in ((one_v, w1_v), (two_v, w2_v)):
        dst[...] = jnp.zeros_like(dst)
        dst[0:BS, 0:BS] = src[0].astype(BF16)
        dst[0:BS, 128 : 128 + BS] = src[1].astype(BF16)
        dst[128 : 128 + BS, 0:BS] = -src[1].astype(BF16)
        dst[128 : 128 + BS, 128 : 128 + BS] = src[0].astype(BF16)
    bias = jnp.zeros((1, 256), F32)
    for blk in range(NB):
        parts = []
        for ri in range(2):
            parts.append(bias_ref[ri : ri + 1, BS * blk : BS * blk + BS])
            parts.append(jnp.zeros((1, 32), F32))
        bias = bias + jnp.where(n == blk, jnp.concatenate(parts, axis=1), 0.0)

    def take1(d, _):
        src = lax.rem(b + d, NLON)

        @pl.when(d > 0)
        def _():
            remote(p1_s.at[src], p1_r.at[src], s1.at[src], r1.at[src], (a, src)).wait_recv()

        at = pl.ds(pl.multiple_of(8 * src, 8), 8)
        x_v[at, :] = unfold(p1_r[src].astype(F32))
        return 0

    lax.fori_loop(0, NLON, take1, 0)

    def mate_of(d):
        other = lax.rem(g + d, 8)
        return other, (other // 2, (other % 2) * 16 + p)

    mates = [(dh, dc, dl) for dh in range(2) for dc in range(2) for dl in range(2)][1:]
    mates.sort(key=lambda t: (not (t[0] and not t[2]), not t[2]))

    def mate_at(dh, dc, dl):
        lat = ((a // 2 + dh) % 2) * 2 + (a % 2 + dc) % 2
        half = (q + dl) % 2
        return 2 * lat + half, (lat, half * 16 + p)

    x = x_v[...].astype(BF16)
    for kh in range(2):
        part = dot(fw_ref[64 * kh : 64 * kh + 64, :], x)
        p2_s[kh] = part.reshape(8, 8, MSG).astype(BF16)
        for way in mates:
            other, dev = mate_at(*way)
            remote(
                p2_s.at[kh, other], p2_r.at[kh, g], s2.at[kh, other], r2.at[kh, g], dev
            ).start()

    def spread(kh, src, value):
        for i in range(ROW12):
            piece = value[:, BS * i : BS * i + BS]
            piece = jnp.concatenate([piece, jnp.zeros((8, 128 - BS), F32)], axis=1)
            z_v[pl.ds(768 * kh + ROW12 * src + i, 8, stride=H), :] = piece

    def gather(kh, dest):
        pieces = [
            v_v[pl.ds(768 * kh + ROW12 * dest + i, 8, stride=H), :][:, :BS] for i in range(ROW12)
        ]
        return jnp.concatenate(pieces, axis=1).astype(BF16)

    for kh in range(2):
        spread(kh, g, p2_s[kh, g].astype(F32))

        def take2(d, _):
            other, dev = mate_of(d)
            remote(
                p2_s.at[kh, other], p2_r.at[kh, other], s2.at[kh, other], r2.at[kh, other], dev
            ).wait_recv()
            spread(kh, other, p2_r[kh, other].astype(F32))
            return 0

        lax.fori_loop(1, 8, take2, 0)

        base = 768 * kh
        z = jnp.concatenate(
            [z_v[base + 192 * k : base + 192 * k + 192, :] for k in range(4)], axis=1
        )
        spec = dot(sq_v[1], z.astype(BF16))
        modes = jnp.concatenate(
            [
                jnp.concatenate(
                    [spec[:H, 128 * k : 128 * k + 128], spec[H:, 128 * k : 128 * k + 128]], axis=1
                )
                for k in range(4)
            ],
            axis=0,
        )
        mid = jnp.maximum(dot(modes.astype(BF16), w1_v[...]) + bias, 0.0)
        res = dot(mid.astype(BF16), w2_v[...])
        res = res - jnp.clip(res, -0.01, 0.01)
        back = jnp.concatenate(
            [
                jnp.concatenate(
                    [res[H * k : H * k + H, :128], res[H * k : H * k + H, 128:]], axis=0
                )
                for k in range(4)
            ],
            axis=1,
        )
        rows = dot(sq_v[2], back.astype(BF16))
        for k in range(4):
            v_v[base + 192 * k : base + 192 * k + 192, :] = rows[:, 128 * k : 128 * k + 128]

        for way in mates:
            other, dev = mate_at(*way)
            p3_s[kh, other] = gather(kh, other)
            remote(
                p3_s.at[kh, other], p3_r.at[kh, g], s3.at[kh, other], r3.at[kh, g], dev
            ).start()
        p3_r[kh, g] = gather(kh, g)

    def wait3(d, _):
        other, dev = mate_of(d)
        for kh in range(2):
            remote(
                p3_s.at[kh, other], p3_r.at[kh, other], s3.at[kh, other], r3.at[kh, other], dev
            ).wait_recv()
        return 0

    lax.fori_loop(1, 8, wait3, 0)

    spectra = p3_r[...].astype(F32).reshape(128, MSG).astype(BF16)
    for dx in (1, 0):
        other = (q + dx) % 2
        field = dot(bw_ref[pl.ds(pl.multiple_of(128 * other, 128), 128), :], spectra)
        p4_s[pl.ds(16 * other, 16)] = fold(field.reshape(16, 8, MSG)).astype(BF16)
        steps = [(dy, dz) for dy in range(4) for dz in range(4)]
        steps.sort(key=lambda t: -(min(t[0], 4 - t[0]) + min(t[1], 4 - t[1])))
        for dy, dz in steps:
            if (dx, dy, dz) != (0, 0, 0):
                dest = 16 * other + ((row_y + dy) % 4) * 4 + (row_z + dz) % 4
                remote(p4_s.at[dest], p4_r.at[b], s4.at[dest], r4.at[b], (a, dest)).start()
    p4_r[b] = p4_s[b]

    for copy in halos:
        copy.wait_send()

    def drain1(d, _):
        dest = lax.rem(b + d, NLON)
        remote(p1_s.at[dest], p1_r.at[b], s1.at[dest], r1.at[b], (a, dest)).wait_send()
        return 0

    lax.fori_loop(1, NLON, drain1, 0)

    def drain_lat(d, _):
        other, dev = mate_of(d)
        for kh in range(2):
            remote(
                p2_s.at[kh, other], p2_r.at[kh, g], s2.at[kh, other], r2.at[kh, g], dev
            ).wait_send()
            remote(
                p3_s.at[kh, other], p3_r.at[kh, g], s3.at[kh, other], r3.at[kh, g], dev
            ).wait_send()
        return 0

    lax.fori_loop(1, 8, drain_lat, 0)
    c_up.wait()
    c_down.wait()
    results = []
    for smp in range(2):
        def join(part, _):
            for blk in range(NB):
                src = owner(part, smp, blk)

                @pl.when(src != b)
                def _(src=src):
                    remote(
                        p4_s.at[src], p4_r.at[src], s4.at[src], r4.at[src], (a, src)
                    ).wait_recv()

            msgs = [unfold(p4_r[owner(part, smp, blk)].astype(F32)) for blk in range(NB)]
            for i in range(ROW12):
                plane = jnp.concatenate([m[:, BS * i : BS * i + BS] for m in msgs], axis=1)
                for tile in range(6):
                    nf_v[tile, smp, pl.ds(part * ROW12 + i, 8, stride=ROWS), :] = plane[
                        :, 128 * tile : 128 * tile + 128
                    ]
            return 0

        lax.fori_loop(0, 2, join, 0)
        rows = slice(144 * smp, 144 * smp + 144)
        field = jnp.concatenate([nf_v[tile, smp, :144] for tile in range(6)], axis=1)
        middle = (field + tn_v[rows, :]).astype(BF16).astype(F32)
        acc_v[rows, :] = middle
        nrm_v[rows, :] = norm(middle, g2_ref[...].reshape(1, C)).astype(BF16)

        def up(step):
            return dot(nrm_v[rows, :], up_v[:, pl.ds(pl.multiple_of(step * 512, 512), 512)])

        def down(hidden, step):
            hidden = 0.5 * hidden * (1.0 + lax.erf(hidden * (1.0 / math.sqrt(2.0))))
            part = pl.ds(pl.multiple_of(step * 512, 512), 512)
            return dot(hidden.astype(BF16), down_v[part, :])

        h0_v[...] = up(0)

        def mlp(it, _):
            step = 2 * it
            h1_v[...] = up(step + 1)
            acc_v[rows, :] += down(h0_v[...], step)
            h0_v[...] = up(jnp.minimum(step + 2, HID // 512 - 1))
            acc_v[rows, :] += down(h1_v[...], step + 1)
            return 0

        lax.fori_loop(0, HID // 1024, mlp, 0, unroll=True)
        res_v[smp] = acc_v[rows, :].reshape(COLS, ROWS, C).astype(BF16)
        results.append(load(16 + smp, res_v.at[smp], out_ref.at[smp]))

    def drain4(d, _):
        dest = lax.rem(b + d, NLON)
        remote(p4_s.at[dest], p4_r.at[b], s4.at[dest], r4.at[b], (a, dest)).wait_send()
        return 0

    lax.fori_loop(1, NLON, drain4, 0)
    for copy in results:
        copy.wait()


def local(
    grid, patch_weight, norm_gain_one, spectral_one, spectral_bias, spectral_two,
    norm_gain_two, fc_up, fc_down,
):
    fw, bw = lon_tables()
    fh, bh = lat_tables()
    const = lambda x: jnp.asarray(x, F32).astype(BF16)
    any_spec = pl.BlockSpec(memory_space=pl.ANY)
    dma = pltpu.SemaphoreType.DMA
    out = pl.pallas_call(
        kernel,
        out_shape=jax.ShapeDtypeStruct((2, COLS, ROWS, C), BF16),
        in_specs=[any_spec] * 13,
        out_specs=any_spec,
        scratch_shapes=[
            pltpu.VMEM((3, 192, 192), BF16),
            pltpu.VMEM((128, 256), BF16),
            pltpu.VMEM((256, 128), BF16),
            pltpu.VMEM((C,), F32),
            pltpu.VMEM((2, C), F32),
            pltpu.VMEM((C,), F32),
            pltpu.VMEM((2, NV, 48, 192), BF16),
            pltpu.VMEM((5120, C), BF16),
            pltpu.VMEM((2, BS, BS), F32),
            pltpu.VMEM((2, BS, BS), F32),
            pltpu.VMEM((C, HID), BF16),
            pltpu.VMEM((HID, C), BF16),
            pltpu.VMEM((4, 160, 768), BF16),
            pltpu.VMEM((8, 288, 160), F32),
            pltpu.VMEM((2, 6, 480, 128), F32),
            pltpu.VMEM((2, 288, 1280), BF16),
            pltpu.VMEM((2, 96, 768), BF16),
            pltpu.VMEM((2, 16, 1280), BF16),
            pltpu.VMEM((6, 384, 128), F32),
            pltpu.VMEM((6, 384, 128), F32),
            pltpu.VMEM((6, 288, 128), F32),
            pltpu.VMEM((288, C), F32),
            pltpu.VMEM((6, 2, 192, 128), F32),
            pltpu.VMEM((288, C), F32),
            pltpu.VMEM((288, C), BF16),
            pltpu.VMEM((2, 2, ROWS, C), BF16),
            pltpu.VMEM((2, 2, ROWS, C), BF16),
            pltpu.VMEM((2, 16, C), BF16),
            pltpu.VMEM((6, 16, C), BF16),
            pltpu.VMEM((NLON, 8, 896), BF16),
            pltpu.VMEM((NLON, 8, 896), BF16),
            pltpu.VMEM((2, 8, 8, MSG), BF16),
            pltpu.VMEM((2, 8, 8, MSG), BF16),
            pltpu.VMEM((2, 8, 8, MSG), BF16),
            pltpu.VMEM((2, 8, 8, MSG), BF16),
            pltpu.VMEM((NLON, 8, 896), BF16),
            pltpu.VMEM((NLON, 8, 896), BF16),
            pltpu.VMEM((8 * 192, 128), F32),
            pltpu.VMEM((8 * 192, 128), F32),
            pltpu.VMEM((256, 256), BF16),
            pltpu.VMEM((256, 256), BF16),
            pltpu.VMEM((144, 512), F32),
            pltpu.VMEM((144, 512), F32),
            pltpu.VMEM((2, COLS, ROWS, C), BF16),
            pltpu.VMEM((256, MSG), F32),
            dma((18,)),
            dma((10,)),
            dma((10,)),
            dma((NLON,)),
            dma((NLON,)),
            dma((2, 8)),
            dma((2, 8)),
            dma((2, 8)),
            dma((2, 8)),
            dma((NLON,)),
            dma((NLON,)),
        ],
        compiler_params=pltpu.CompilerParams(
            collective_id=0, has_side_effects=True, vmem_limit_bytes=56 * 1024 * 1024
        ),
    )(
        grid.transpose(0, 1, 3, 2), patch_weight, spectral_one, spectral_two, fc_up, fc_down,
        const(feature_table()),
        const(np.stack([pick_table(), fh, bh])), const(fw), const(bw),
        norm_gain_one, spectral_bias, norm_gain_two,
    )
    return out.transpose(0, 2, 1, 3)


def solution(mesh):
    in_specs = (P(None, None, "lat", "lon"), P(), P(), P(), P(), P(), P(), P(), P())
    out_specs = P(None, "lat", "lon", None)
    return jax.shard_map(local, mesh=mesh, in_specs=in_specs, out_specs=out_specs, check_vma=False)
```
